256 devices in a mesh: passage: 32 (over z, x), cell: 4 (over y), tm: 2 (over core).
Axes of the slice: x: 4, y: 4, z: 8, core: 2. Of those that a mesh axis runs over, the one named last changes fastest.
Arguments:
- adjoint_start: float32 [8, 5, 8, 1024, 256], P('tm', None, 'cell', 'passage'), may hold values from -6 to 6
- adjoint_source: float32 [8, 5, 8, 1024, 256], P('tm', None, 'cell', 'passage'), may hold values from -6 to 6
- jacobian: bfloat16 [2, 5, 5, 8, 1024, 256], P(None, None, None, 'cell', 'passage'), may hold values from -2.5 to 2.5
- pseudo_time: float32 [8, 1024, 256], P('cell', 'passage'), may hold values from 3 to 12
- dissipation: float32 [8, 1024, 256], P('cell', 'passage'), may hold values from 0.2 to 1
- surface_cells: int32 [4, 1024], P('cell'), may hold values from 0 to 1023, as said below
- surface_weights: float32 [8, 5, 4096], P('tm', None, 'cell'), may hold values from -1 to 1
Outputs:
- adjoint_final: float32 [8, 5, 8, 1024, 256], P('tm', None, 'cell', 'passage')
- diameter_modes: float32 [2, 16, 4096], P(None, None, 'cell')
The draws below stay inside these ranges and needn't reach their ends.
Inputs may be any that keep to these rules, and one draw needn't show every extreme that they name: `surface_cells`: each row holds every value from 0 to 1023 exactly once, in a drawn order.
All inputs are finite; a program needn't handle non-finite values.
Results may differ from the reference program's by a relative error of at most 0.0025.
Values may be sent and summed in bfloat16 or wider, within the bound.
No kernel may reach another device: no remote copies, remote signals or barrier semaphores. Data moves between devices by JAX's collectives and lax.ppermute only.
A program may use at most 128 MiB of HBM per device.

```python
import math
import jax
import jax.numpy as jnp
from jax import lax

NV = 5
NT = 8
PASSAGES = 16
CJ = 64
PITCH = 1024
CI = 2
CK = 256
SWEEPS = 2
NI = 8
SURF_DEV = 1024
SURF = 4096
N_CELL = 4


def draw_surface_cells(key, part):
    row_keys = jax.random.split(key, SURF // SURF_DEV)

    def one_block(row_key):
        return jax.random.permutation(row_key, SURF_DEV).astype(jnp.int32)
    return jax.vmap(one_block)(row_keys)


def level_of(stream_key, shape, shards, smallest, largest):
    level, own = 1.0, jax.random.fold_in(stream_key, 6)
    for axis_at, shards_of in shards:
        steps = jnp.exp(jax.random.uniform(jax.random.fold_in(own, axis_at), (shards_of,), jnp.float32, smallest / len(shards), largest / len(shards)))
        level = level * jnp.repeat(steps, shape[axis_at] // shards_of).reshape([-1 if axis == axis_at else 1 for axis in range(len(shape))])
    return level


def bell_draw(rng, extent, width, most, shards=(), kind=jnp.bfloat16):
    loudness = level_of(rng, extent, shards, -0.22, 0.18) if shards else 1.0
    entries = jax.random.normal(rng, extent, jnp.float32) * width * loudness
    return jnp.minimum(jnp.maximum(entries, -most), most).astype(kind)


def setup_inputs(seed: int = 0) -> dict:
    key_of = jax.random.split(jax.random.key(seed), 8)
    adjoint_start = bell_draw(key_of[0], (NT, NV, NI, PITCH, CK), 1.0, 6.0, ((0, 2), (2, 4), (3, 32)), jnp.float32)
    adjoint_source = bell_draw(key_of[1], (NT, NV, NI, PITCH, CK), 1.0, 6.0, ((0, 2), (2, 4), (3, 32)), jnp.float32)
    jacobian = bell_draw(key_of[2], (2, NV, NV, NI, PITCH, CK), NV ** -0.5, 2.5, ((3, 4), (4, 32)))
    pseudo_time = jnp.clip(jnp.exp(math.log(12.0) - 1.3862944 * jax.random.uniform(key_of[3], (NI, PITCH, CK), jnp.float32) ** level_of(key_of[3], (NI, PITCH, CK), ((0, 4), (1, 32)), -0.2, 0.2)), 3.0, 12.0)
    dissipation = jnp.clip(jnp.exp(math.log(1.0) - 1.609438 * jax.random.uniform(key_of[4], (NI, PITCH, CK), jnp.float32) ** level_of(key_of[4], (NI, PITCH, CK), ((0, 4), (1, 32)), -0.2, 0.2)), 0.2, 1.0)
    surface_cells = draw_surface_cells(jax.random.fold_in(key_of[7], 71), 0)
    surface_weights = bell_draw(key_of[6], (NT, NV, SURF), (NT * NV) ** -0.5, 1.0, ((0, 2), (2, 4)), jnp.float32)
    return dict(adjoint_start=adjoint_start, adjoint_source=adjoint_source, jacobian=jacobian, pseudo_time=pseudo_time, dissipation=dissipation, surface_cells=surface_cells, surface_weights=surface_weights)


OMEGA = 1.0


def spectral_matrix(total):
    index = jnp.arange(total, dtype=jnp.int32)
    offset = index[:, None] - index[None, :]
    parity = (1 - 2 * (offset % 2)).astype(jnp.float32)
    phase_arg = jnp.pi * offset.astype(jnp.float32) / total
    sine_safe = jnp.where(offset == 0, jnp.float32(1.0), jnp.sin(phase_arg))
    values = 0.5 * parity * jnp.cos(phase_arg) / sine_safe
    return jnp.where(offset == 0, jnp.float32(0.0), values)


def blade_table(passages):
    index = jnp.arange(passages, dtype=jnp.int32)
    product_mod = (index[:, None] * index[None, :]) % passages
    phase_arg = 2.0 * jnp.pi * product_mod.astype(jnp.float32) / passages
    factor = 1.0 / (passages ** 0.5)
    return jnp.stack([jnp.cos(phase_arg), -jnp.sin(phase_arg)]) * factor


def adjoint_operator(field, plus_i, minus_i, plus_j, minus_j, jacobian, sigma, damping):
    total_out = sigma * field + damping * (4.0 * field - plus_i - minus_i - plus_j - minus_j)
    variables = field.shape[1]
    flux_rows = []
    for target_var in range(variables):
        acc_flux = jnp.zeros_like(field[:, 0])
        for source_var in range(variables):
            acc_flux = acc_flux + jacobian[0, source_var, target_var].astype(jnp.float32) * (field[:, source_var] - plus_i[:, source_var])
            acc_flux = acc_flux + jacobian[1, source_var, target_var].astype(jnp.float32) * (field[:, source_var] - plus_j[:, source_var])
        flux_rows.append(acc_flux)
    return total_out + jnp.stack(flux_rows, axis=1)


def neighbours(field):
    zero_slab = jnp.zeros_like(field[:, :, :1])
    plus_i = jnp.concatenate([field[:, :, 1:], zero_slab], axis=2)
    minus_i = jnp.concatenate([zero_slab, field[:, :, :-1]], axis=2)
    plus_j = jnp.roll(field, -1, axis=3)
    minus_j = jnp.roll(field, 1, axis=3)
    return plus_i, minus_i, plus_j, minus_j


def reference(adjoint_start, adjoint_source, jacobian, pseudo_time, dissipation, surface_cells, surface_weights):
    start_rounded = adjoint_start.astype(jnp.bfloat16)
    dmatrix = spectral_matrix(NT)
    spectral_term = OMEGA * jnp.einsum('ab,avipk->bvipk', dmatrix, start_rounded.astype(jnp.float32), precision=lax.Precision.HIGHEST)
    scaling = 1.0 / (pseudo_time + 4.0 * dissipation)
    field = adjoint_start
    for sweep_index in range(SWEEPS):
        plus_i, minus_i, plus_j, minus_j = neighbours(field)
        applied = adjoint_operator(field, plus_i, minus_i, plus_j, minus_j, jacobian, pseudo_time, dissipation)
        field = field + (adjoint_source - applied - spectral_term) * scaling
    side_rows = (jnp.arange(PASSAGES, dtype=jnp.int32)[:, None] * CJ + jnp.arange(2, dtype=jnp.int32)[None, :] * (CJ - 1)).reshape(2 * PASSAGES)
    rows = jnp.take(field, side_rows, axis=3)
    rows = rows.reshape(NT, NV, N_CELL, CI, PASSAGES, 2, CK)
    rows = rows.transpose(0, 1, 4, 2, 5, 3, 6).reshape(NT, NV, PASSAGES, N_CELL * SURF_DEV)
    block_base = (jnp.arange(N_CELL, dtype=jnp.int32) * SURF_DEV)[:, None]
    global_index = (surface_cells + block_base).reshape(SURF).astype(jnp.int32)
    picked = jnp.take(rows, global_index, axis=3)
    sensitivity = jnp.einsum('tvs,tvps->ps', surface_weights, picked, precision=lax.Precision.HIGHEST)
    table = blade_table(PASSAGES)
    diameter_modes = jnp.einsum('cmp,ps->cms', table, sensitivity, precision=lax.Precision.HIGHEST)
    return field, diameter_modes
```

```python
import functools
import math

import jax
import jax.numpy as jnp
from jax import lax
from jax.experimental import pallas as pl
from jax.experimental.pallas import tpu as pltpu
from jax.sharding import PartitionSpec as P

PASSAGES = 16
SWEEPS = 2
NT = 8
F32 = jnp.float32
BF16 = jnp.bfloat16
VMEM = pl.BlockSpec(memory_space=pltpu.VMEM)
SMEM = pl.BlockSpec(memory_space=pltpu.SMEM)


def derivative(offset):
    offset = offset % NT
    if offset in (0, NT // 2):
        return 0.0
    angle = math.pi * offset / NT
    return 0.5 * (-1) ** offset * math.cos(angle) / math.sin(angle)


def call(kernel, outs, args, specs, mib, flops, name):
    nbytes = sum(a.size * a.dtype.itemsize for a in args) + sum(
        math.prod(o.shape) * o.dtype.itemsize for o in outs
    )
    return pl.pallas_call(
        kernel,
        out_shape=outs,
        in_specs=specs,
        out_specs=[VMEM] * len(outs),
        compiler_params=pltpu.CompilerParams(vmem_limit_bytes=mib << 20),
        cost_estimate=pl.CostEstimate(
            flops=flops, bytes_accessed=nbytes, transcendentals=0
        ),
        name=name,
    )(*args)


def by_parity(ids_ref, run):
    @pl.when(ids_ref[0] == 0)
    def _():
        run(1, 0)

    @pl.when(ids_ref[0] != 0)
    def _():
        run(0, 1)


def pack_layers(f_ref, a_ref, b_ref, low_ref, high_ref, layer_a, layer_b):
    nt, nv, ni, nj, nk = f_ref.shape
    for t in range(nt):
        for v in range(nv):
            a_ref[t, v] = f_ref[t, v, layer_a].astype(BF16)
            b_ref[t, v] = f_ref[t, v, layer_b].astype(BF16)
            for i in range(ni):
                row = (t * nv + v) * ni + i
                low_ref[row : row + 1, :] = f_ref[t, v, i, 0:1, :]
                high_ref[row : row + 1, :] = f_ref[t, v, i, nj - 1 : nj, :]


def prepare_kernel(ids_ref, f_ref, a_ref, b_ref, low_ref, high_ref):
    by_parity(
        ids_ref,
        lambda la, lb: pack_layers(f_ref, a_ref, b_ref, low_ref, high_ref, la, lb),
    )


def rhs_kernel(ids_ref, f_ref, src_ref, pa_ref, pb_ref, out_ref):
    nt, nv, ni, nj, nk = f_ref.shape

    def run(layer_a, layer_b):
        for layer, other in ((layer_a, pa_ref), (layer_b, pb_ref)):

            def one(v, carry):
                for j in range(0, nj, 16):
                    rows = slice(j, j + 16)
                    own = [
                        f_ref[t, v, layer, rows, :].astype(BF16).astype(F32)
                        for t in range(nt)
                    ]
                    far = [other[t, v, rows, :].astype(F32) for t in range(nt)]
                    times = own + far
                    for b in range(nt):
                        total = src_ref[b, v, layer, rows, :]
                        for n in range(1, NT // 2):
                            diff = times[(b + n) % NT] - times[(b - n) % NT]
                            total = total - derivative(n) * diff
                        out_ref[b, v, layer, rows, :] = total
                return carry

            lax.fori_loop(0, nv, one, 0)

    by_parity(ids_ref, run)


def shifted(f_ref, t, u, i, j, lanes, low_ref, high_ref, row, rows_id):
    nj = f_ref.shape[3]
    here = f_ref[t, u, i, j : j + 8, lanes]
    if j + 8 < nj:
        after = f_ref[t, u, i, j + 8 : j + 16, lanes]
        plus = jnp.where(rows_id == 7, pltpu.roll(after, 7, 0), pltpu.roll(here, 7, 0))
    else:
        edge = jnp.broadcast_to(high_ref[row : row + 1, lanes], here.shape)
        plus = jnp.where(rows_id == 7, edge, pltpu.roll(here, 7, 0))
    if j > 0:
        before = f_ref[t, u, i, j - 8 : j, lanes]
        minus = jnp.where(
            rows_id == 0, pltpu.roll(before, 1, 0), pltpu.roll(here, 1, 0)
        )
    else:
        edge = jnp.broadcast_to(low_ref[row : row + 1, lanes], here.shape)
        minus = jnp.where(rows_id == 0, edge, pltpu.roll(here, 1, 0))
    return here, plus, minus


def sweep_tile(refs, out_ref, halo_of, i, j, lanes):
    f_ref, rhs_ref, jac_ref, sig_ref, dmp_ref, low_ref, high_ref = refs
    nt, nv, ni = f_ref.shape[:3]
    pair = slice(j // 16 * 16, j // 16 * 16 + 16)
    half = slice(j % 16, j % 16 + 8)
    halo = halo_of[i]
    sigma = sig_ref[i, j : j + 8, lanes]
    damping = dmp_ref[i, j : j + 8, lanes]
    scaling = 1.0 / (sigma + 4.0 * damping)
    rows_id = lax.broadcasted_iota(jnp.int32, sigma.shape, 0)
    acc = [[None] * nv for _ in range(nt)]
    for u in range(nv):
        jac = [
            [jac_ref[d, u, v, i, pair, lanes].astype(F32)[half] for v in range(nv)]
            for d in range(2)
        ]
        for t in range(nt):
            row = (t * nv + u) * ni + i
            here, plus_j, minus_j = shifted(
                f_ref, t, u, i, j, lanes, low_ref, high_ref, row, rows_id
            )
            outer = halo[t, u, pair, lanes].astype(F32)[half]
            inner = f_ref[t, u, 1 - i, j : j + 8, lanes]
            plus_i, minus_i = (outer, inner) if i else (inner, outer)
            diff_i, diff_j = here - plus_i, here - plus_j
            both = diff_i + diff_j + ((here - minus_i) + (here - minus_j))
            own = sigma * here + damping * both
            for v in range(nv):
                term = jac[0][v] * diff_i + jac[1][v] * diff_j
                if v == u:
                    term = term + own
                acc[t][v] = term if acc[t][v] is None else acc[t][v] + term
    for t in range(nt):
        for v in range(nv):
            spot = (t, v, i, slice(j, j + 8), lanes)
            out_ref[spot] = f_ref[spot] + (rhs_ref[spot] - acc[t][v]) * scaling


def sweep_all(refs, out_ref, halo_of):
    nt, nv, ni, nj, nk = out_ref.shape

    def one(k, carry):
        lanes = pl.ds(pl.multiple_of(k * 128, 128), 128)
        for i in range(ni):
            for j in range(0, nj, 8):
                sweep_tile(refs, out_ref, halo_of, i, j, lanes)
        return carry

    lax.fori_loop(0, nk // 128, one, 0)


def first_kernel(ids_ref, *refs):
    ins, ha_ref, hb_ref = refs[:7], refs[7], refs[8]
    out_ref, a_ref, b_ref, low_ref, high_ref = refs[9:]

    def run(layer_a, layer_b):
        sweep_all(ins, out_ref, {layer_a: ha_ref, layer_b: hb_ref})
        pack_layers(out_ref, a_ref, b_ref, low_ref, high_ref, layer_a, layer_b)

    by_parity(ids_ref, run)


def second_kernel(ids_ref, *refs):
    ins, ha_ref, hb_ref, w_ref = refs[:7], refs[7], refs[8], refs[9]
    out_ref, sens_ref = refs[10:]
    nt, nv, ni, nj, nk = out_ref.shape

    def run(layer_a, layer_b):
        sweep_all(ins, out_ref, {layer_a: ha_ref, layer_b: hb_ref})

    by_parity(ids_ref, run)
    side = ids_ref[1]
    start = pl.multiple_of(side * (nj - 8), 8)
    mask = lax.broadcasted_iota(jnp.int32, (8, nk), 0) == side * 7
    for i in range(ni):
        total = jnp.zeros((8, nk), F32)
        for t in range(nt):
            for v in range(nv):
                weight = w_ref[t * nv + v : t * nv + v + 1, i * nk : (i + 1) * nk]
                total = total + out_ref[t, v, i, pl.ds(start, 8), :] * weight
        value = jnp.sum(jnp.where(mask, total, 0.0), axis=0, keepdims=True)
        for c in range(nk // 128):
            sens_ref[:, i * (nk // 128) + c, :] = jnp.broadcast_to(
                value[:, c * 128 : (c + 1) * 128], (sens_ref.shape[0], 128)
            )


def split3(x):
    one = x.astype(BF16)
    rest = x - one.astype(F32)
    two = rest.astype(BF16)
    three = (rest - two.astype(F32)).astype(BF16)
    return one, two, three


def one_hot(cells_ref, first, rows):
    cells = cells_ref.shape[1]
    index = lax.broadcasted_iota(jnp.int32, (rows, cells), 0) + first
    return jnp.where(cells_ref[0:1, :] == index, 1.0, 0.0).astype(BF16)


def weights_kernel(ids_ref, cells_ref, w_ref, out_ref):
    half = out_ref.shape[1]
    chosen = one_hot(cells_ref, ids_ref[1] * half, half)
    out_ref[...] = sum(
        lax.dot_general(
            part, chosen, (((1,), (1,)), ((), ())), preferred_element_type=F32
        )
        for part in split3(w_ref[...])
    )


def modes_kernel(cells_ref, table_ref, sens_ref, out_ref):
    devices = sens_ref.shape[0] // 2
    pieces = sens_ref.shape[1]
    half = pieces * 128
    total = []
    for side in range(2):
        modes = jnp.concatenate(
            [
                jnp.dot(
                    table_ref[side],
                    sens_ref[:, c, :],
                    precision=lax.Precision.HIGHEST,
                    preferred_element_type=F32,
                )
                for c in range(pieces)
            ],
            axis=1,
        )
        chosen = one_hot(cells_ref, side * half, half)
        for part in split3(modes):
            total.append(jnp.dot(part, chosen, preferred_element_type=F32))
    out_ref[...] = functools.reduce(lambda x, y: x + y, total)


def mode_table(devices):
    per = devices // PASSAGES
    m = jnp.arange(PASSAGES, dtype=jnp.int32)[:, None]
    d = jnp.arange(devices, dtype=jnp.int32)[None, :]
    angle = 2.0 * jnp.pi * (m * (d // per) % PASSAGES).astype(F32) / PASSAGES
    base = jnp.concatenate([jnp.cos(angle), -jnp.sin(angle)]) / PASSAGES**0.5
    sides = [jnp.where(d % per == s, base, 0.0) for s in range(per)]
    return jnp.repeat(jnp.stack(sides), 2, axis=2)


def body(start, source, jac, sigma, damping, cells, weights):
    nt, nv, ni, nj, nk = start.shape
    ring = lax.axis_size("passage")
    cell = lax.axis_index("cell")
    ids = jnp.stack([cell % 2, lax.axis_index("passage") % 2]).astype(jnp.int32)
    n_cell = lax.axis_size("cell")
    even = [(c, c ^ 1) for c in range(n_cell)]
    odd = [(c, c + 1) for c in range(1, n_cell - 1, 2)]
    odd += [(b, a) for a, b in odd]
    up = [(d, (d + 1) % ring) for d in range(ring)]
    down = [(d, (d - 1) % ring) for d in range(ring)]
    swap = [(0, 1), (1, 0)]

    field_like = jax.ShapeDtypeStruct(start.shape, F32)
    layer_like = jax.ShapeDtypeStruct((nt, nv, nj, nk), BF16)
    rows_like = jax.ShapeDtypeStruct((nt * nv * ni, nk), F32)
    sends = [layer_like, layer_like, rows_like, rows_like]

    def exchange(a, b, low, high):
        with jax.named_scope("halos"):
            return (
                lax.ppermute(high, "passage", up),
                lax.ppermute(low, "passage", down),
                lax.ppermute(a, "cell", even),
                lax.ppermute(b, "cell", odd),
            )

    a, b, low, high = call(
        prepare_kernel, sends, (ids, start), [SMEM, VMEM], 8, 10**6, "prepare"
    )
    before, after, ha, hb = exchange(a, b, low, high)
    pa = lax.ppermute(a, "tm", swap)
    pb = lax.ppermute(b, "tm", swap)
    ordered = call(
        weights_kernel,
        [jax.ShapeDtypeStruct((nt * nv, ni * nk), F32)],
        (ids, cells, weights.reshape(nt * nv, -1)),
        [SMEM, VMEM, VMEM],
        16,
        10**6,
        "weights",
    )[0]
    rhs = call(
        rhs_kernel,
        [field_like],
        (ids, start, source, pa, pb),
        [SMEM] + [VMEM] * 4,
        16,
        10**7,
        "rhs",
    )[0]
    field, a, b, low, high = call(
        first_kernel,
        [field_like] + sends,
        (ids, start, rhs, jac, sigma, damping, before, after, ha, hb),
        [SMEM] + [VMEM] * 9,
        24,
        2 * 10**7,
        "first_sweep",
    )
    before, after, ha, hb = exchange(a, b, low, high)
    group = ("passage", "tm")
    members = 2 * ring
    field, sens = call(
        second_kernel,
        [field_like, jax.ShapeDtypeStruct((members, ni * nk // 128, 128), F32)],
        (ids, field, rhs, jac, sigma, damping, before, after, ha, hb, ordered),
        [SMEM] + [VMEM] * 10,
        24,
        2 * 10**7,
        "second_sweep",
    )
    with jax.named_scope("share_sensitivities"):
        gathered = lax.all_to_all(sens, group, 0, 0, tiled=True)
    modes = call(
        modes_kernel,
        [jax.ShapeDtypeStruct((2 * PASSAGES, cells.shape[1]), F32)],
        (cells, mode_table(ring), gathered),
        [VMEM] * 3,
        16,
        10**7,
        "modes",
    )[0]
    return field, modes.reshape(2, PASSAGES, -1)


def solution(mesh):
    in_specs = (
        P("tm", None, "cell", "passage", None),
        P("tm", None, "cell", "passage", None),
        P(None, None, None, "cell", "passage", None),
        P("cell", "passage", None),
        P("cell", "passage", None),
        P("cell", None),
        P("tm", None, "cell"),
    )
    out_specs = (P("tm", None, "cell", "passage", None), P(None, None, "cell"))
    return jax.shard_map(
        body, mesh=mesh, in_specs=in_specs, out_specs=out_specs, check_vma=False
    )
```

```python
import functools
import math

import jax
import jax.numpy as jnp
import numpy as np
from jax import lax
from jax.experimental import pallas as pl
from jax.experimental.pallas import tpu as pltpu
from jax.sharding import PartitionSpec as P

PASSAGES = 16
SWEEPS = 2
NT = 8
F32 = jnp.float32
BF16 = jnp.bfloat16
VMEM = pl.BlockSpec(memory_space=pltpu.VMEM)
SMEM = pl.BlockSpec(memory_space=pltpu.SMEM)


def derivative(offset):
    offset = offset % NT
    if offset in (0, NT // 2):
        return 0.0
    angle = math.pi * offset / NT
    return 0.5 * (-1) ** offset * math.cos(angle) / math.sin(angle)


def call(kernel, outs, args, specs, mib, flops, name):
    nbytes = sum(a.size * a.dtype.itemsize for a in args) + sum(
        math.prod(o.shape) * o.dtype.itemsize for o in outs
    )
    return pl.pallas_call(
        kernel,
        out_shape=outs,
        in_specs=specs,
        out_specs=[VMEM] * len(outs),
        compiler_params=pltpu.CompilerParams(vmem_limit_bytes=mib << 20),
        cost_estimate=pl.CostEstimate(
            flops=flops, bytes_accessed=nbytes, transcendentals=0
        ),
        name=name,
    )(*args)


def by_parity(ids_ref, run):
    @pl.when(ids_ref[0] == 0)
    def _():
        run(1, 0)

    @pl.when(ids_ref[0] != 0)
    def _():
        run(0, 1)


def edge_row(ids_ref, f_ref, t, v, i, outer):
    nj = f_ref.shape[3]
    low, high = f_ref[t, v, i, 0:1, :], f_ref[t, v, i, nj - 1 : nj, :]
    first = ids_ref[1] == (0 if outer else 1)
    return jnp.where(first, low, high)


def pack_layers(f_ref, a_ref, b_ref, layer_a, layer_b):
    nt, nv = f_ref.shape[:2]
    for t in range(nt):
        for v in range(nv):
            a_ref[t, v] = f_ref[t, v, layer_a].astype(BF16)
            b_ref[t, v] = f_ref[t, v, layer_b].astype(BF16)


def pack_rows(ids_ref, f_ref, outer_ref, inner_ref, ra_ref=None, rb_ref=None, layer_a=0):
    nt, nv, ni = f_ref.shape[:3]
    for t in range(nt):
        for v in range(nv):
            at = t * nv + v
            for i in range(ni):
                row = at * ni + i
                outer = edge_row(ids_ref, f_ref, t, v, i, True)
                outer_ref[row : row + 1, :] = outer
                inner_ref[row : row + 1, :] = edge_row(ids_ref, f_ref, t, v, i, False)
                if ra_ref is not None:
                    to = ra_ref if i == layer_a else rb_ref
                    to[at : at + 1, :] = outer


def prepare_kernel(ids_ref, f_ref, a_ref, b_ref, outer_ref, inner_ref):
    pack_rows(ids_ref, f_ref, outer_ref, inner_ref)
    by_parity(ids_ref, functools.partial(pack_layers, f_ref, a_ref, b_ref))


def rhs_kernel(ids_ref, f_ref, src_ref, pa_ref, pb_ref, out_ref):
    nt, nv, ni, nj, nk = f_ref.shape

    def run(layer_a, layer_b):
        for layer, other in ((layer_a, pa_ref), (layer_b, pb_ref)):

            def one(v, carry):
                for j in range(0, nj, 16):
                    rows = slice(j, j + 16)
                    own = [
                        f_ref[t, v, layer, rows, :].astype(BF16).astype(F32)
                        for t in range(nt)
                    ]
                    far = [other[t, v, rows, :].astype(F32) for t in range(nt)]
                    times = own + far
                    for b in range(nt):
                        total = src_ref[b, v, layer, rows, :]
                        for n in range(1, NT // 2):
                            diff = times[(b + n) % NT] - times[(b - n) % NT]
                            total = total - derivative(n) * diff
                        out_ref[b, v, layer, rows, :] = total
                return carry

            lax.fori_loop(0, nv, one, 0)

    by_parity(ids_ref, run)


def shifted(f_ref, t, u, i, j, lanes, edges, rows_id):
    nj = f_ref.shape[3]
    here = f_ref[t, u, i, j : j + 8, lanes]
    if j + 8 < nj:
        after = pltpu.roll(f_ref[t, u, i, j + 8 : j + 16, lanes], 7, 0)
    else:
        after = edges(t, u, i, True)
    if j > 0:
        before = pltpu.roll(f_ref[t, u, i, j - 8 : j, lanes], 1, 0)
    else:
        before = edges(t, u, i, False)
    plus = jnp.where(rows_id == 7, after, pltpu.roll(here, 7, 0))
    minus = jnp.where(rows_id == 0, before, pltpu.roll(here, 1, 0))
    return here, plus, minus


def sweep_tile(refs, halo, edges, i, j, lanes):
    f_ref, rhs_ref, jac_ref, sig_ref, dmp_ref = refs
    nt, nv, ni = f_ref.shape[:3]
    pair = slice(j // 16 * 16, j // 16 * 16 + 16)
    half = slice(j % 16, j % 16 + 8)
    sigma = sig_ref[i, j : j + 8, lanes]
    damping = dmp_ref[i, j : j + 8, lanes]
    scaling = 1.0 / (sigma + 4.0 * damping)
    rows_id = lax.broadcasted_iota(jnp.int32, sigma.shape, 0)
    acc = [[None] * nv for _ in range(nt)]
    for u in range(nv):
        jac = [
            [jac_ref[d, u, v, i, pair, lanes].astype(F32)[half] for v in range(nv)]
            for d in range(2)
        ]
        for t in range(nt):
            here, plus_j, minus_j = shifted(f_ref, t, u, i, j, lanes, edges, rows_id)
            outer = halo(t, u)
            inner = f_ref[t, u, 1 - i, j : j + 8, lanes]
            plus_i, minus_i = (outer, inner) if i else (inner, outer)
            diff_i, diff_j = here - plus_i, here - plus_j
            both = diff_i + diff_j + ((here - minus_i) + (here - minus_j))
            own = sigma * here + damping * both
            for v in range(nv):
                term = jac[0][v] * diff_i + jac[1][v] * diff_j
                if v == u:
                    term = term + own
                acc[t][v] = term if acc[t][v] is None else acc[t][v] + term
    return [
        [
            f_ref[t, v, i, j : j + 8, lanes]
            + (rhs_ref[t, v, i, j : j + 8, lanes] - acc[t][v]) * scaling
            for v in range(nv)
        ]
        for t in range(nt)
    ]


def lanes_at(k):
    return pl.ds(pl.multiple_of(k * 128, 128), 128)


def sweep_all(ids_ref, refs, outer_ref, inner_ref, out_ref, layers):
    nt, nv, ni, nj, nk = out_ref.shape
    upper = ids_ref[1] == 1

    def one(k, carry):
        lanes = lanes_at(k)

        def edges(t, u, i, high):
            row = (t * nv + u) * ni + i
            outer = outer_ref[row : row + 1, lanes]
            inner = inner_ref[row : row + 1, lanes]
            edge = jnp.where(upper, outer, inner) if high else jnp.where(upper, inner, outer)
            return jnp.broadcast_to(edge, (8, 128))

        for i in range(ni):
            for j in range(0, nj, 8):
                pair = slice(j // 16 * 16, j // 16 * 16 + 16)
                half = slice(j % 16, j % 16 + 8)
                new = sweep_tile(
                    refs,
                    lambda t, u: layers[i][t, u, pair, lanes].astype(F32)[half],
                    edges,
                    i,
                    j,
                    lanes,
                )
                for t in range(nt):
                    for v in range(nv):
                        out_ref[t, v, i, j : j + 8, lanes] = new[t][v]
        return carry

    lax.fori_loop(0, nk // 128, one, 0)


def first_kernel(ids_ref, *refs):
    ins, outer_ref, inner_ref, ha_ref, hb_ref = refs[:5], *refs[5:9]
    out_ref, no_ref, ni_ref, ra_ref, rb_ref = refs[9:]

    def run(layer_a, layer_b):
        layers = {layer_a: ha_ref, layer_b: hb_ref}
        sweep_all(ids_ref, ins, outer_ref, inner_ref, out_ref, layers)
        pack_rows(ids_ref, out_ref, no_ref, ni_ref, ra_ref, rb_ref, layer_a)

    by_parity(ids_ref, run)


def surface_kernel(ids_ref, *refs):
    ins, outer_ref, ra_ref, rb_ref, w_ref = refs[:5], *refs[5:9]
    sens_ref, a_ref, b_ref = refs[9:]
    f_ref = ins[0]
    nt, nv, ni, nj, nk = f_ref.shape

    def row_of(side, layers):
        j = side * (nj - 8)
        mask = lax.broadcasted_iota(jnp.int32, (8, 128), 0) == side * 7

        def one(k, carry):
            lanes = lanes_at(k)

            def edges(t, u, i, high):
                row = (t * nv + u) * ni + i
                return jnp.broadcast_to(outer_ref[row : row + 1, lanes], (8, 128))

            def halo(i, t, u):
                at = t * nv + u
                return jnp.broadcast_to(layers[i][at : at + 1, lanes], (8, 128))

            for i in range(ni):
                new = sweep_tile(ins, functools.partial(halo, i), edges, i, j, lanes)
                total = jnp.zeros((8, 128), F32)
                for t in range(nt):
                    for v in range(nv):
                        at = t * nv + v
                        start = pl.multiple_of(i * nk + k * 128, 128)
                        weight = w_ref[at : at + 1, pl.ds(start, 128)]
                        total = total + new[t][v] * weight
                value = jnp.sum(jnp.where(mask, total, 0.0), axis=0, keepdims=True)
                sens_ref[:, pl.ds(i * (nk // 128) + k, 1), :] = jnp.broadcast_to(
                    value[None], (sens_ref.shape[0], 1, 128)
                )
            return carry

        lax.fori_loop(0, nk // 128, one, 0)

    def run(layer_a, layer_b):
        layers = {layer_a: ra_ref, layer_b: rb_ref}
        for side in range(2):
            pl.when(ids_ref[1] == side)(functools.partial(row_of, side, layers))
        pack_layers(f_ref, a_ref, b_ref, layer_a, layer_b)

    by_parity(ids_ref, run)


def second_kernel(ids_ref, *refs):
    ins, outer_ref, inner_ref, ha_ref, hb_ref = refs[:5], *refs[5:9]
    out_ref, done_ref = refs[9:]
    done_ref[...] = jnp.zeros(done_ref.shape, F32)

    def run(layer_a, layer_b):
        layers = {layer_a: ha_ref, layer_b: hb_ref}
        sweep_all(ids_ref, ins, outer_ref, inner_ref, out_ref, layers)

    by_parity(ids_ref, run)


def split3(x):
    one = x.astype(BF16)
    rest = x - one.astype(F32)
    two = rest.astype(BF16)
    three = (rest - two.astype(F32)).astype(BF16)
    return one, two, three


def one_hot(cells_ref, first, rows):
    cells = cells_ref.shape[1]
    index = lax.broadcasted_iota(jnp.int32, (rows, cells), 0) + first
    return jnp.where(cells_ref[0:1, :] == index, 1.0, 0.0).astype(BF16)


def order_kernel(ids_ref, cells_ref, w_ref, out_ref, chosen_ref):
    half = out_ref.shape[1]
    nv, nt, _ = w_ref.shape
    chosen_ref[...] = one_hot(cells_ref, 0, chosen_ref.shape[0])
    own = chosen_ref[pl.ds(pl.multiple_of(ids_ref[1] * half, 512), half), :]
    for v in range(nv):
        parts = [
            lax.dot_general(
                part, own, (((1,), (1,)), ((), ())), preferred_element_type=F32
            )
            for part in split3(w_ref[v])
        ]
        total = parts[0] + (parts[1] + parts[2])
        for t in range(nt):
            out_ref[t * nv + v : t * nv + v + 1, :] = total[t : t + 1]


def modes_kernel(table_ref, chosen_ref, sens_ref, done_ref, out_ref):
    pieces = sens_ref.shape[1]
    half = pieces * 128
    rows = out_ref.shape[0]
    seen = jnp.concatenate([sens_ref[:, c, :] for c in range(pieces)], axis=1)
    both = jnp.dot(
        table_ref[...],
        seen,
        precision=lax.Precision.HIGHEST,
        preferred_element_type=F32,
    )
    total = None
    for side in range(2):
        modes = both[side * rows : (side + 1) * rows]
        parts = jnp.concatenate(split3(modes), axis=0)
        chosen = chosen_ref[side * half : (side + 1) * half, :]
        found = jnp.dot(parts, chosen, preferred_element_type=F32)
        found = found[:rows] + (found[rows : 2 * rows] + found[2 * rows :])
        total = found if total is None else total + found
    out_ref[...] = total


def mode_table(devices):
    per = devices // PASSAGES
    m = np.arange(PASSAGES)[:, None]
    d = np.arange(devices)[None, :]
    angle = 2.0 * np.pi * (m * (d // per) % PASSAGES) / PASSAGES
    base = np.concatenate([np.cos(angle), -np.sin(angle)]) / PASSAGES**0.5
    sides = [np.where(d % per == s, base, 0.0) for s in range(per)]
    return np.repeat(np.concatenate(sides), 2, axis=1).astype(np.float32)


def body(start, source, jac, sigma, damping, cells, weights):
    nt, nv, ni, nj, nk = start.shape
    ring = lax.axis_size("passage")
    n_cell = lax.axis_size("cell")
    ids = jnp.stack([lax.axis_index("cell") & 1, lax.axis_index("passage") & 1])
    even = [(c, c ^ 1) for c in range(n_cell)]
    odd = [(c, c + 1) for c in range(1, n_cell - 1, 2)]
    odd += [(b, a) for a, b in odd]
    within = [(d, d ^ 1) for d in range(ring)]
    across = [(d, (d + 1) % ring) for d in range(1, ring, 2)]
    across += [(b, a) for a, b in across]
    swap = [(0, 1), (1, 0)]

    field_like = jax.ShapeDtypeStruct(start.shape, F32)
    layer_like = jax.ShapeDtypeStruct((nt, nv, nj, nk), BF16)
    rows_like = jax.ShapeDtypeStruct((nt * nv * ni, nk), F32)
    row_like = jax.ShapeDtypeStruct((nt * nv, nk), F32)

    a, b, outer, inner = call(
        prepare_kernel,
        [layer_like, layer_like, rows_like, rows_like],
        (ids, start),
        [SMEM, VMEM],
        4,
        10**6,
        "prepare",
    )
    with jax.named_scope("halos"):
        outer = lax.ppermute(outer, "passage", across)
        inner = lax.ppermute(inner, "passage", within)
        ha = lax.ppermute(a, "cell", even)
        hb = lax.ppermute(b, "cell", odd)
        pa = lax.ppermute(a, "tm", swap)
        pb = lax.ppermute(b, "tm", swap)
    rhs = call(
        rhs_kernel,
        [field_like],
        (ids, start, source, pa, pb),
        [SMEM] + [VMEM] * 4,
        4,
        10**7,
        "rhs",
    )[0]
    ordered, chosen = call(
        order_kernel,
        [
            jax.ShapeDtypeStruct((nt * nv, ni * nk), F32),
            jax.ShapeDtypeStruct((cells.shape[1], cells.shape[1]), BF16),
        ],
        (ids, cells, weights.transpose(1, 0, 2)),
        [SMEM, VMEM, VMEM],
        8,
        10**6,
        "order",
    )
    fixed = (jac, sigma, damping)
    field, outer, inner, ra, rb = call(
        first_kernel,
        [field_like, rows_like, rows_like, row_like, row_like],
        (ids, start, rhs, *fixed, outer, inner, ha, hb),
        [SMEM] + [VMEM] * 9,
        8,
        2 * 10**7,
        "first_sweep",
    )
    with jax.named_scope("surface_halos"):
        outer = lax.ppermute(outer, "passage", across)
        ra = lax.ppermute(ra, "cell", even)
        rb = lax.ppermute(rb, "cell", odd)
        inner = lax.ppermute(inner, "passage", within)
    sens, a, b = call(
        surface_kernel,
        [
            jax.ShapeDtypeStruct((2 * ring, ni * nk // 128, 128), F32),
            layer_like,
            layer_like,
        ],
        (ids, field, rhs, *fixed, outer, ra, rb, ordered),
        [SMEM] + [VMEM] * 9,
        8,
        5 * 10**6,
        "surface",
    )
    with jax.named_scope("halos"):
        ha = lax.ppermute(a, "cell", even)
        hb = lax.ppermute(b, "cell", odd)
    with jax.named_scope("share_sensitivities"):
        gathered = lax.all_to_all(sens, ("passage", "tm"), 0, 0, tiled=True)
    field, done = call(
        second_kernel,
        [field_like, jax.ShapeDtypeStruct((8, 128), F32)],
        (ids, field, rhs, *fixed, outer, inner, ha, hb),
        [SMEM] + [VMEM] * 9,
        8,
        2 * 10**7,
        "second_sweep",
    )
    modes = call(
        modes_kernel,
        [jax.ShapeDtypeStruct((2 * PASSAGES, cells.shape[1]), F32)],
        (mode_table(ring), chosen, gathered, done),
        [VMEM] * 4,
        8,
        10**7,
        "modes",
    )[0]
    return field, modes.reshape(2, PASSAGES, -1)


def solution(mesh):
    in_specs = (
        P("tm", None, "cell", "passage", None),
        P("tm", None, "cell", "passage", None),
        P(None, None, None, "cell", "passage", None),
        P("cell", "passage", None),
        P("cell", "passage", None),
        P("cell", None),
        P("tm", None, "cell"),
    )
    out_specs = (P("tm", None, "cell", "passage", None), P(None, None, "cell"))
    return jax.shard_map(
        body, mesh=mesh, in_specs=in_specs, out_specs=out_specs, check_vma=False
    )
```

```python
import functools
import math

import jax
import jax.numpy as jnp
from jax import lax
from jax.experimental import pallas as pl
from jax.experimental.pallas import tpu as pltpu
from jax.sharding import PartitionSpec as P

PASSAGES = 16
SWEEPS = 2
NT = 8
F32 = jnp.float32
BF16 = jnp.bfloat16
VMEM = pl.BlockSpec(memory_space=pltpu.VMEM)
SMEM = pl.BlockSpec(memory_space=pltpu.SMEM)


def derivative(offset):
    offset = offset % NT
    if offset in (0, NT // 2):
        return 0.0
    angle = math.pi * offset / NT
    return 0.5 * (-1) ** offset * math.cos(angle) / math.sin(angle)


def call(kernel, outs, args, specs, mib, flops, name):
    nbytes = sum(a.size * a.dtype.itemsize for a in args) + sum(
        math.prod(o.shape) * o.dtype.itemsize for o in outs
    )
    return pl.pallas_call(
        kernel,
        out_shape=outs,
        in_specs=specs,
        out_specs=[VMEM] * len(outs),
        compiler_params=pltpu.CompilerParams(vmem_limit_bytes=mib << 20),
        cost_estimate=pl.CostEstimate(
            flops=flops, bytes_accessed=nbytes, transcendentals=0
        ),
        name=name,
    )(*args)


def by_parity(ids_ref, run):
    @pl.when(ids_ref[0] == 0)
    def _():
        run(1, 0)

    @pl.when(ids_ref[0] != 0)
    def _():
        run(0, 1)


def edge_row(ids_ref, f_ref, t, v, i, outer):
    nj = f_ref.shape[3]
    low, high = f_ref[t, v, i, 0:1, :], f_ref[t, v, i, nj - 1 : nj, :]
    first = ids_ref[1] == (0 if outer else 1)
    return jnp.where(first, low, high)


def pack_layers(f_ref, a_ref, b_ref, layer_a, layer_b):
    nt, nv = f_ref.shape[:2]
    for t in range(nt):
        for v in range(nv):
            a_ref[t, v] = f_ref[t, v, layer_a].astype(BF16)
            b_ref[t, v] = f_ref[t, v, layer_b].astype(BF16)


def pack_rows(ids_ref, f_ref, outer_ref, inner_ref, ra_ref=None, rb_ref=None, layer_a=0):
    nt, nv, ni = f_ref.shape[:3]
    for t in range(nt):
        for v in range(nv):
            at = t * nv + v
            for i in range(ni):
                row = at * ni + i
                outer = edge_row(ids_ref, f_ref, t, v, i, True)
                outer_ref[row : row + 1, :] = outer
                inner_ref[row : row + 1, :] = edge_row(ids_ref, f_ref, t, v, i, False)
                if ra_ref is not None:
                    to = ra_ref if i == layer_a else rb_ref
                    to[at : at + 1, :] = outer


def prepare_kernel(ids_ref, f_ref, a_ref, b_ref, outer_ref, inner_ref):
    pack_rows(ids_ref, f_ref, outer_ref, inner_ref)
    by_parity(ids_ref, functools.partial(pack_layers, f_ref, a_ref, b_ref))


def rhs_kernel(ids_ref, f_ref, src_ref, pa_ref, pb_ref, out_ref):
    nt, nv, ni, nj, nk = f_ref.shape

    def run(layer_a, layer_b):
        for layer, other in ((layer_a, pa_ref), (layer_b, pb_ref)):

            def one(v, carry):
                for j in range(0, nj, 16):
                    rows = slice(j, j + 16)
                    own = [
                        f_ref[t, v, layer, rows, :].astype(BF16).astype(F32)
                        for t in range(nt)
                    ]
                    far = [other[t, v, rows, :].astype(F32) for t in range(nt)]
                    times = own + far
                    for b in range(nt):
                        total = src_ref[b, v, layer, rows, :]
                        for n in range(1, NT // 2):
                            diff = times[(b + n) % NT] - times[(b - n) % NT]
                            total = total - derivative(n) * diff
                        out_ref[b, v, layer, rows, :] = total
                return carry

            lax.fori_loop(0, nv, one, 0)

    by_parity(ids_ref, run)


def shifted(f_ref, t, u, i, j, lanes, edges, rows_id):
    nj = f_ref.shape[3]
    here = f_ref[t, u, i, j : j + 8, lanes]
    if j + 8 < nj:
        after = pltpu.roll(f_ref[t, u, i, j + 8 : j + 16, lanes], 7, 0)
    else:
        after = edges(t, u, i, True)
    if j > 0:
        before = pltpu.roll(f_ref[t, u, i, j - 8 : j, lanes], 1, 0)
    else:
        before = edges(t, u, i, False)
    plus = jnp.where(rows_id == 7, after, pltpu.roll(here, 7, 0))
    minus = jnp.where(rows_id == 0, before, pltpu.roll(here, 1, 0))
    return here, plus, minus


def sweep_tile(refs, halo, edges, i, j, lanes):
    f_ref, rhs_ref, jac_ref, sig_ref, dmp_ref = refs
    nt, nv, ni = f_ref.shape[:3]
    pair = slice(j // 16 * 16, j // 16 * 16 + 16)
    half = slice(j % 16, j % 16 + 8)
    sigma = sig_ref[i, j : j + 8, lanes]
    damping = dmp_ref[i, j : j + 8, lanes]
    scaling = 1.0 / (sigma + 4.0 * damping)
    rows_id = lax.broadcasted_iota(jnp.int32, sigma.shape, 0)
    acc = [[None] * nv for _ in range(nt)]
    for u in range(nv):
        jac = [
            [jac_ref[d, u, v, i, pair, lanes].astype(F32)[half] for v in range(nv)]
            for d in range(2)
        ]
        for t in range(nt):
            here, plus_j, minus_j = shifted(f_ref, t, u, i, j, lanes, edges, rows_id)
            outer = halo(t, u)
            inner = f_ref[t, u, 1 - i, j : j + 8, lanes]
            plus_i, minus_i = (outer, inner) if i else (inner, outer)
            diff_i, diff_j = here - plus_i, here - plus_j
            both = diff_i + diff_j + ((here - minus_i) + (here - minus_j))
            own = sigma * here + damping * both
            for v in range(nv):
                term = jac[0][v] * diff_i + jac[1][v] * diff_j
                if v == u:
                    term = term + own
                acc[t][v] = term if acc[t][v] is None else acc[t][v] + term
    return [
        [
            f_ref[t, v, i, j : j + 8, lanes]
            + (rhs_ref[t, v, i, j : j + 8, lanes] - acc[t][v]) * scaling
            for v in range(nv)
        ]
        for t in range(nt)
    ]


def lanes_at(k):
    return pl.ds(pl.multiple_of(k * 128, 128), 128)


def sweep_all(ids_ref, refs, outer_ref, inner_ref, out_ref, layers):
    nt, nv, ni, nj, nk = out_ref.shape
    upper = ids_ref[1] == 1

    def one(k, carry):
        lanes = lanes_at(k)

        def edges(t, u, i, high):
            row = (t * nv + u) * ni + i
            outer = outer_ref[row : row + 1, lanes]
            inner = inner_ref[row : row + 1, lanes]
            edge = jnp.where(upper, outer, inner) if high else jnp.where(upper, inner, outer)
            return jnp.broadcast_to(edge, (8, 128))

        for i in range(ni):
            for j in range(0, nj, 8):
                pair = slice(j // 16 * 16, j // 16 * 16 + 16)
                half = slice(j % 16, j % 16 + 8)
                new = sweep_tile(
                    refs,
                    lambda t, u: layers[i][t, u, pair, lanes].astype(F32)[half],
                    edges,
                    i,
                    j,
                    lanes,
                )
                for t in range(nt):
                    for v in range(nv):
                        out_ref[t, v, i, j : j + 8, lanes] = new[t][v]
        return carry

    lax.fori_loop(0, nk // 128, one, 0)


def first_kernel(ids_ref, *refs):
    ins, outer_ref, inner_ref, ha_ref, hb_ref = refs[:5], *refs[5:9]
    out_ref, no_ref, ni_ref, ra_ref, rb_ref = refs[10:]

    def run(layer_a, layer_b):
        layers = {layer_a: ha_ref, layer_b: hb_ref}
        sweep_all(ids_ref, ins, outer_ref, inner_ref, out_ref, layers)
        pack_rows(ids_ref, out_ref, no_ref, ni_ref, ra_ref, rb_ref, layer_a)

    by_parity(ids_ref, run)


def surface_kernel(ids_ref, *refs):
    ins, outer_ref, ra_ref, rb_ref, w_ref = refs[:5], *refs[5:9]
    sens_ref, done_ref = refs[10:]
    done_ref[...] = jnp.zeros(done_ref.shape, F32)
    f_ref = ins[0]
    nt, nv, ni, nj, nk = f_ref.shape

    def row_of(side, layers):
        j = side * (nj - 8)
        mask = lax.broadcasted_iota(jnp.int32, (8, 128), 0) == side * 7

        def one(k, carry):
            lanes = lanes_at(k)

            def edges(t, u, i, high):
                row = (t * nv + u) * ni + i
                return jnp.broadcast_to(outer_ref[row : row + 1, lanes], (8, 128))

            def halo(i, t, u):
                at = t * nv + u
                return jnp.broadcast_to(layers[i][at : at + 1, lanes], (8, 128))

            for i in range(ni):
                new = sweep_tile(ins, functools.partial(halo, i), edges, i, j, lanes)
                total = jnp.zeros((8, 128), F32)
                for t in range(nt):
                    for v in range(nv):
                        at = t * nv + v
                        start = pl.multiple_of(i * nk + k * 128, 128)
                        weight = w_ref[at : at + 1, pl.ds(start, 128)]
                        total = total + new[t][v] * weight
                value = jnp.sum(jnp.where(mask, total, 0.0), axis=0, keepdims=True)
                sens_ref[:, pl.ds(i * (nk // 128) + k, 1), :] = jnp.broadcast_to(
                    value[None], (sens_ref.shape[0], 1, 128)
                )
            return carry

        lax.fori_loop(0, nk // 128, one, 0)

    def run(layer_a, layer_b):
        layers = {layer_a: ra_ref, layer_b: rb_ref}
        for side in range(2):
            pl.when(ids_ref[1] == side)(functools.partial(row_of, side, layers))

    by_parity(ids_ref, run)


def pack_kernel(ids_ref, f_ref, done_ref, a_ref, b_ref):
    by_parity(ids_ref, functools.partial(pack_layers, f_ref, a_ref, b_ref))


def second_kernel(ids_ref, *refs):
    ins, outer_ref, inner_ref, ha_ref, hb_ref = refs[:5], *refs[5:9]
    out_ref, done_ref = refs[9:]
    done_ref[...] = jnp.zeros(done_ref.shape, F32)

    def run(layer_a, layer_b):
        layers = {layer_a: ha_ref, layer_b: hb_ref}
        sweep_all(ids_ref, ins, outer_ref, inner_ref, out_ref, layers)

    by_parity(ids_ref, run)


def split3(x):
    one = x.astype(BF16)
    rest = x - one.astype(F32)
    two = rest.astype(BF16)
    three = (rest - two.astype(F32)).astype(BF16)
    return one, two, three


def one_hot(cells_ref, first, rows):
    cells = cells_ref.shape[1]
    index = lax.broadcasted_iota(jnp.int32, (rows, cells), 0) + first
    return jnp.where(cells_ref[0:1, :] == index, 1.0, 0.0).astype(BF16)


def order_kernel(ids_ref, cells_ref, w_ref, out_ref):
    rows, half = out_ref.shape
    nv, nt, _ = w_ref.shape
    own = one_hot(cells_ref, ids_ref[1] * half, half)
    parts = [part for v in range(nv) for part in split3(w_ref[v])]
    found = lax.dot_general(
        jnp.concatenate(parts, axis=0),
        own,
        (((1,), (1,)), ((), ())),
        preferred_element_type=F32,
    )
    for t in range(nt):
        for v in range(nv):
            one, two, three = (found[(v * 3 + p) * nt + t][None] for p in range(3))
            out_ref[t * nv + v : t * nv + v + 1, :] = one + (two + three)


def mode_table(side, modes, senders):
    row = lax.broadcasted_iota(jnp.int32, (2 * modes, senders), 0)
    sender = lax.broadcasted_iota(jnp.int32, (2 * modes, senders), 1)
    turns = ((row % modes) * (sender // 4)) % PASSAGES
    angle = turns.astype(F32) * (2.0 * math.pi / PASSAGES)
    value = jnp.where(row < modes, jnp.cos(angle), -jnp.sin(angle)) / PASSAGES**0.5
    return jnp.where((sender // 2) % 2 == side, value, 0.0)


def modes_kernel(cells_ref, sens_ref, done_ref, out_ref):
    senders, pieces = sens_ref.shape[:2]
    half = pieces * 128
    rows = out_ref.shape[0]
    table = jnp.concatenate(
        [mode_table(side, rows // 2, senders) for side in range(2)], axis=0
    )
    seen = jnp.concatenate([sens_ref[:, c, :] for c in range(pieces)], axis=1)
    both = jnp.dot(
        table,
        seen,
        precision=lax.Precision.HIGHEST,
        preferred_element_type=F32,
    )
    total = None
    for side in range(2):
        modes = both[side * rows : (side + 1) * rows]
        parts = jnp.concatenate(split3(modes), axis=0)
        chosen = one_hot(cells_ref, side * half, half)
        found = jnp.dot(parts, chosen, preferred_element_type=F32)
        found = found[:rows] + (found[rows : 2 * rows] + found[2 * rows :])
        total = found if total is None else total + found
    out_ref[...] = total


def body(start, source, jac, sigma, damping, cells, weights):
    nt, nv, ni, nj, nk = start.shape
    ring = lax.axis_size("passage")
    n_cell = lax.axis_size("cell")
    ids = jnp.stack([lax.axis_index("cell") & 1, lax.axis_index("passage") & 1])
    even = [(c, c ^ 1) for c in range(n_cell)]
    odd = [(c, c + 1) for c in range(1, n_cell - 1, 2)]
    odd += [(b, a) for a, b in odd]
    within = [(d, d ^ 1) for d in range(ring)]
    across = [(d, (d + 1) % ring) for d in range(1, ring, 2)]
    across += [(b, a) for a, b in across]
    swap = [(0, 1), (1, 0)]

    field_like = jax.ShapeDtypeStruct(start.shape, F32)
    layer_like = jax.ShapeDtypeStruct((nt, nv, nj, nk), BF16)
    rows_like = jax.ShapeDtypeStruct((nt * nv * ni, nk), F32)
    row_like = jax.ShapeDtypeStruct((nt * nv, nk), F32)

    a, b, outer, inner = call(
        prepare_kernel,
        [layer_like, layer_like, rows_like, rows_like],
        (ids, start),
        [SMEM, VMEM],
        4,
        10**6,
        "prepare",
    )
    with jax.named_scope("halos"):
        outer = lax.ppermute(outer, "passage", across)
        inner = lax.ppermute(inner, "passage", within)
        ha = lax.ppermute(a, "cell", even)
        hb = lax.ppermute(b, "cell", odd)
        pa = lax.ppermute(a, "tm", swap)
        pb = lax.ppermute(b, "tm", swap)
    rhs = call(
        rhs_kernel,
        [field_like],
        (ids, start, source, pa, pb),
        [SMEM] + [VMEM] * 4,
        4,
        10**7,
        "rhs",
    )[0]
    ordered = call(
        order_kernel,
        [jax.ShapeDtypeStruct((nt * nv, ni * nk), F32)],
        (ids, cells, weights.transpose(1, 0, 2)),
        [SMEM, VMEM, VMEM],
        8,
        10**6,
        "order",
    )[0]
    fixed = (jac, sigma, damping)
    field, outer, inner, ra, rb = call(
        first_kernel,
        [field_like, rows_like, rows_like, row_like, row_like],
        (ids, start, rhs, *fixed, outer, inner, ha, hb, ordered),
        [SMEM] + [VMEM] * 10,
        8,
        2 * 10**7,
        "first_sweep",
    )
    with jax.named_scope("surface_halos"):
        outer = lax.ppermute(outer, "passage", across)
        ra = lax.ppermute(ra, "cell", even)
        rb = lax.ppermute(rb, "cell", odd)
        inner = lax.ppermute(inner, "passage", within)
    token_like = jax.ShapeDtypeStruct((8, 128), F32)
    sens, done = call(
        surface_kernel,
        [jax.ShapeDtypeStruct((2 * ring, ni * nk // 128, 128), F32), token_like],
        (ids, field, rhs, *fixed, outer, ra, rb, ordered, inner),
        [SMEM] + [VMEM] * 10,
        8,
        5 * 10**6,
        "surface",
    )
    a, b = call(
        pack_kernel,
        [layer_like, layer_like],
        (ids, field, done),
        [SMEM, VMEM, VMEM],
        4,
        10**6,
        "pack",
    )
    with jax.named_scope("halos"):
        ha = lax.ppermute(a, "cell", even)
        hb = lax.ppermute(b, "cell", odd)
    with jax.named_scope("share_sensitivities"):
        gathered = lax.all_to_all(sens, ("passage", "tm"), 0, 0, tiled=True)
    field, done = call(
        second_kernel,
        [field_like, token_like],
        (ids, field, rhs, *fixed, outer, inner, ha, hb),
        [SMEM] + [VMEM] * 9,
        8,
        2 * 10**7,
        "second_sweep",
    )
    modes = call(
        modes_kernel,
        [jax.ShapeDtypeStruct((2 * PASSAGES, cells.shape[1]), F32)],
        (cells, gathered, done),
        [VMEM] * 3,
        8,
        10**7,
        "modes",
    )[0]
    return field, modes.reshape(2, PASSAGES, -1)


def solution(mesh):
    in_specs = (
        P("tm", None, "cell", "passage", None),
        P("tm", None, "cell", "passage", None),
        P(None, None, None, "cell", "passage", None),
        P("cell", "passage", None),
        P("cell", "passage", None),
        P("cell", None),
        P("tm", None, "cell"),
    )
    out_specs = (P("tm", None, "cell", "passage", None), P(None, None, "cell"))
    return jax.shard_map(
        body, mesh=mesh, in_specs=in_specs, out_specs=out_specs, check_vma=False
    )
```

```python
import functools
import math

import jax
import jax.numpy as jnp
from jax import lax
from jax.experimental import pallas as pl
from jax.experimental.pallas import tpu as pltpu
from jax.sharding import PartitionSpec as P

PASSAGES = 16
NT = 8
F32 = jnp.float32
BF16 = jnp.bfloat16
VMEM = pl.BlockSpec(memory_space=pltpu.VMEM)
SMEM = pl.BlockSpec(memory_space=pltpu.SMEM)


def derivative(offset):
    offset = offset % NT
    if offset in (0, NT // 2):
        return 0.0
    angle = math.pi * offset / NT
    return 0.5 * (-1) ** offset * math.cos(angle) / math.sin(angle)


def call(kernel, outs, args, specs, mib, flops, name):
    nbytes = sum(a.size * a.dtype.itemsize for a in args) + sum(
        math.prod(o.shape) * o.dtype.itemsize for o in outs
    )
    return pl.pallas_call(
        kernel,
        out_shape=outs,
        in_specs=specs,
        out_specs=[VMEM] * len(outs),
        compiler_params=pltpu.CompilerParams(vmem_limit_bytes=mib << 20),
        cost_estimate=pl.CostEstimate(
            flops=flops, bytes_accessed=nbytes, transcendentals=0
        ),
        name=name,
    )(*args)


def by_parity(ids_ref, run):
    @pl.when(ids_ref[0] == 0)
    def _():
        run(1, 0)

    @pl.when(ids_ref[0] != 0)
    def _():
        run(0, 1)


def edge_row(ids_ref, f_ref, t, v, i, outer):
    nj = f_ref.shape[3]
    low, high = f_ref[t, v, i, 0:1, :], f_ref[t, v, i, nj - 1 : nj, :]
    first = ids_ref[1] == (0 if outer else 1)
    return jnp.where(first, low, high)


def pack_layers(f_ref, a_ref, b_ref, layer_a, layer_b):
    nt, nv = f_ref.shape[:2]
    for t in range(nt):
        for v in range(nv):
            a_ref[t, v] = f_ref[t, v, layer_a].astype(BF16)
            b_ref[t, v] = f_ref[t, v, layer_b].astype(BF16)


def pack_rows(ids_ref, f_ref, outer_ref, inner_ref):
    nt, nv, ni = f_ref.shape[:3]
    for t in range(nt):
        for v in range(nv):
            for i in range(ni):
                row = (t * nv + v) * ni + i
                here = slice(row, row + 1)
                outer_ref[here, :] = edge_row(ids_ref, f_ref, t, v, i, True)
                inner_ref[here, :] = edge_row(ids_ref, f_ref, t, v, i, False)


def prepare_kernel(ids_ref, f_ref, a_ref, b_ref, outer_ref, inner_ref):
    pack_rows(ids_ref, f_ref, outer_ref, inner_ref)
    by_parity(ids_ref, functools.partial(pack_layers, f_ref, a_ref, b_ref))


def rhs_kernel(ids_ref, f_ref, src_ref, pa_ref, pb_ref, out_ref):
    nt, nv, ni, nj, nk = f_ref.shape

    def run(layer_a, layer_b):
        for layer, other in ((layer_a, pa_ref), (layer_b, pb_ref)):

            def one(v, carry):
                for j in range(0, nj, 16):
                    rows = slice(j, j + 16)
                    own = [
                        f_ref[t, v, layer, rows, :].astype(BF16).astype(F32)
                        for t in range(nt)
                    ]
                    far = [other[t, v, rows, :].astype(F32) for t in range(nt)]
                    times = own + far
                    for b in range(nt):
                        total = src_ref[b, v, layer, rows, :]
                        for n in range(1, NT // 2):
                            diff = times[(b + n) % NT] - times[(b - n) % NT]
                            total = total - derivative(n) * diff
                        out_ref[b, v, layer, rows, :] = total
                return carry

            lax.fori_loop(0, nv, one, 0)

    by_parity(ids_ref, run)


def shifted(f_ref, t, u, i, j, lanes, edges, rows_id):
    nj = f_ref.shape[3]
    here = f_ref[t, u, i, j : j + 8, lanes]
    if j + 8 < nj:
        after = pltpu.roll(f_ref[t, u, i, j + 8 : j + 16, lanes], 7, 0)
    else:
        after = edges(t, u, i, True)
    if j > 0:
        before = pltpu.roll(f_ref[t, u, i, j - 8 : j, lanes], 1, 0)
    else:
        before = edges(t, u, i, False)
    plus = jnp.where(rows_id == 7, after, pltpu.roll(here, 7, 0))
    minus = jnp.where(rows_id == 0, before, pltpu.roll(here, 1, 0))
    return here, plus, minus


def local_tile(refs, edges, i, j, lanes):
    f_ref, rhs_ref, jac_ref, sig_ref, dmp_ref = refs
    nt, nv, ni = f_ref.shape[:3]
    pair = slice(j // 16 * 16, j // 16 * 16 + 16)
    half = slice(j % 16, j % 16 + 8)
    sigma = sig_ref[i, j : j + 8, lanes]
    damping = dmp_ref[i, j : j + 8, lanes]
    scaling = 1.0 / (sigma + 4.0 * damping)
    rows_id = lax.broadcasted_iota(jnp.int32, sigma.shape, 0)
    acc = [[None] * nv for _ in range(nt)]
    for u in range(nv):
        jac = [
            [jac_ref[d, u, v, i, pair, lanes].astype(F32)[half] for v in range(nv)]
            for d in range(2)
        ]
        for t in range(nt):
            here, plus_j, minus_j = shifted(f_ref, t, u, i, j, lanes, edges, rows_id)
            inner = f_ref[t, u, 1 - i, j : j + 8, lanes]
            diff_i = here if i else here - inner
            diff_j = here - plus_j
            both = (here + (here - inner)) + (diff_j + (here - minus_j))
            own = sigma * here + damping * both
            for v in range(nv):
                term = jac[0][v] * diff_i + jac[1][v] * diff_j
                if v == u:
                    term = term + own
                acc[t][v] = term if acc[t][v] is None else acc[t][v] + term
    return [
        [
            f_ref[t, v, i, j : j + 8, lanes]
            + (rhs_ref[t, v, i, j : j + 8, lanes] - acc[t][v]) * scaling
            for v in range(nv)
        ]
        for t in range(nt)
    ]


def finish_tile(refs, layer_ref, i, j, lanes):
    part_ref, jac_ref, sig_ref, dmp_ref = refs
    nt, nv = part_ref.shape[:2]
    pair = slice(j // 16 * 16, j // 16 * 16 + 16)
    half = slice(j % 16, j % 16 + 8)
    sigma = sig_ref[i, j : j + 8, lanes]
    damping = dmp_ref[i, j : j + 8, lanes]
    scaling = 1.0 / (sigma + 4.0 * damping)
    damping = damping * scaling
    acc = [[None] * nv for _ in range(nt)]
    for u in range(nv):
        jac = (
            [
                jac_ref[0, u, v, i, pair, lanes].astype(F32)[half] * scaling
                for v in range(nv)
            ]
            if i
            else None
        )
        for t in range(nt):
            layer = layer_ref[t, u, pair, lanes].astype(F32)[half]
            for v in range(nv) if i else (u,):
                term = jac[v] * layer if i else damping * layer
                if i and v == u:
                    term = term + damping * layer
                acc[t][v] = term if acc[t][v] is None else acc[t][v] + term
    return [
        [part_ref[t, v, i, j : j + 8, lanes] + acc[t][v] for v in range(nv)]
        for t in range(nt)
    ]


def lanes_at(k):
    return pl.ds(pl.multiple_of(k * 128, 128), 128)


def local_kernel(ids_ref, *refs):
    ins, outer_ref, inner_ref, out_ref = refs[:5], *refs[5:8]
    nt, nv, ni, nj, nk = out_ref.shape
    upper = ids_ref[1] == 1

    def one(k, carry):
        lanes = lanes_at(k)

        def edges(t, u, i, high):
            row = (t * nv + u) * ni + i
            outer = outer_ref[row : row + 1, lanes]
            inner = inner_ref[row : row + 1, lanes]
            edge = jnp.where(upper == high, outer, inner)
            return jnp.broadcast_to(edge, (8, 128))

        for i in range(ni):
            for j in range(0, nj, 8):
                new = local_tile(ins, edges, i, j, lanes)
                for t in range(nt):
                    for v in range(nv):
                        out_ref[t, v, i, j : j + 8, lanes] = new[t][v]
        return carry

    lax.fori_loop(0, nk // 128, one, 0)


def finish_all(ins, out_ref, layers):
    nt, nv, ni, nj, nk = out_ref.shape

    def one(k, carry):
        lanes = lanes_at(k)
        for i in range(ni):
            for j in range(0, nj, 8):
                new = finish_tile(ins, layers[i], i, j, lanes)
                for t in range(nt):
                    for v in range(nv):
                        out_ref[t, v, i, j : j + 8, lanes] = new[t][v]
        return carry

    lax.fori_loop(0, nk // 128, one, 0)


def first_kernel(ids_ref, *refs):
    ins, ha_ref, hb_ref = refs[:4], refs[4], refs[5]
    out_ref, a_ref, b_ref, no_ref, ni_ref = refs[6:]

    def run(layer_a, layer_b):
        finish_all(ins, out_ref, {layer_a: ha_ref, layer_b: hb_ref})
        pack_layers(out_ref, a_ref, b_ref, layer_a, layer_b)

    by_parity(ids_ref, run)
    pack_rows(ids_ref, out_ref, no_ref, ni_ref)


def surface_kernel(ids_ref, *refs):
    ins, ha_ref, hb_ref, w_ref, sens_ref = refs[:4], *refs[4:8]
    nt, nv, ni, nj, nk = ins[0].shape

    def row_of(side, layers):
        j = side * (nj - 8)
        mask = lax.broadcasted_iota(jnp.int32, (8, 128), 0) == side * 7

        def one(k, carry):
            lanes = lanes_at(k)
            for i in range(ni):
                new = finish_tile(ins, layers[i], i, j, lanes)
                total = jnp.zeros((8, 128), F32)
                for t in range(nt):
                    for v in range(nv):
                        at = t * nv + v
                        start = pl.multiple_of(i * nk + k * 128, 128)
                        weight = w_ref[at : at + 1, pl.ds(start, 128)]
                        total = total + new[t][v] * weight
                value = jnp.sum(jnp.where(mask, total, 0.0), axis=0, keepdims=True)
                sens_ref[:, pl.ds(i * (nk // 128) + k, 1), :] = jnp.broadcast_to(
                    value[None], (sens_ref.shape[0], 1, 128)
                )
            return carry

        lax.fori_loop(0, nk // 128, one, 0)

    def run(layer_a, layer_b):
        layers = {layer_a: ha_ref, layer_b: hb_ref}
        for side in range(2):
            pl.when(ids_ref[1] == side)(functools.partial(row_of, side, layers))

    by_parity(ids_ref, run)


def second_kernel(ids_ref, *refs):
    ins, ha_ref, hb_ref, out_ref, done_ref = refs[:4], *refs[4:8]
    done_ref[...] = jnp.zeros(done_ref.shape, F32)

    def run(layer_a, layer_b):
        finish_all(ins, out_ref, {layer_a: ha_ref, layer_b: hb_ref})

    by_parity(ids_ref, run)


def split3(x):
    one = x.astype(BF16)
    rest = x - one.astype(F32)
    two = rest.astype(BF16)
    three = (rest - two.astype(F32)).astype(BF16)
    return one, two, three


def one_hot(cells_ref, first, rows):
    cells = cells_ref.shape[1]
    index = lax.broadcasted_iota(jnp.int32, (rows, cells), 0) + first
    return jnp.where(cells_ref[0:1, :] == index, 1.0, 0.0).astype(BF16)


def order_kernel(ids_ref, cells_ref, w_ref, out_ref):
    rows, half = out_ref.shape
    nv, nt, _ = w_ref.shape
    own = one_hot(cells_ref, ids_ref[1] * half, half)
    parts = [part for v in range(nv) for part in split3(w_ref[v])]
    found = lax.dot_general(
        jnp.concatenate(parts, axis=0),
        own,
        (((1,), (1,)), ((), ())),
        preferred_element_type=F32,
    )
    for t in range(nt):
        for v in range(nv):
            one, two, three = (found[(v * 3 + p) * nt + t][None] for p in range(3))
            out_ref[t * nv + v : t * nv + v + 1, :] = one + (two + three)


def mode_table(side, modes, senders):
    row = lax.broadcasted_iota(jnp.int32, (2 * modes, senders), 0)
    sender = lax.broadcasted_iota(jnp.int32, (2 * modes, senders), 1)
    turns = ((row % modes) * (sender // 4)) % PASSAGES
    angle = turns.astype(F32) * (2.0 * math.pi / PASSAGES)
    value = jnp.where(row < modes, jnp.cos(angle), -jnp.sin(angle)) / PASSAGES**0.5
    return jnp.where((sender // 2) % 2 == side, value, 0.0)


def modes_kernel(cells_ref, sens_ref, done_ref, out_ref):
    senders, pieces = sens_ref.shape[:2]
    half = pieces * 128
    rows = out_ref.shape[0]
    table = jnp.concatenate(
        [mode_table(side, rows // 2, senders) for side in range(2)], axis=0
    )
    seen = jnp.concatenate([sens_ref[:, c, :] for c in range(pieces)], axis=1)
    both = jnp.dot(
        table,
        seen,
        precision=lax.Precision.HIGHEST,
        preferred_element_type=F32,
    )
    total = None
    for side in range(2):
        modes = both[side * rows : (side + 1) * rows]
        parts = jnp.concatenate(split3(modes), axis=0)
        chosen = one_hot(cells_ref, side * half, half)
        found = jnp.dot(parts, chosen, preferred_element_type=F32)
        found = found[:rows] + (found[rows : 2 * rows] + found[2 * rows :])
        total = found if total is None else total + found
    out_ref[...] = total


def body(start, source, jac, sigma, damping, cells, weights):
    nt, nv, ni, nj, nk = start.shape
    ring = lax.axis_size("passage")
    n_cell = lax.axis_size("cell")
    ids = jnp.stack([lax.axis_index("cell") & 1, lax.axis_index("passage") & 1])
    even = [(c, c ^ 1) for c in range(n_cell)]
    odd = [(c, c + 1) for c in range(1, n_cell - 1, 2)]
    odd += [(b, a) for a, b in odd]
    within = [(d, d ^ 1) for d in range(ring)]
    across = [(d, (d + 1) % ring) for d in range(1, ring, 2)]
    across += [(b, a) for a, b in across]
    swap = [(0, 1), (1, 0)]

    field_like = jax.ShapeDtypeStruct(start.shape, F32)
    layer_like = jax.ShapeDtypeStruct((nt, nv, nj, nk), BF16)
    rows_like = jax.ShapeDtypeStruct((nt * nv * ni, nk), F32)

    sends = [layer_like, layer_like, rows_like, rows_like]

    def exchange(a, b, outer, inner):
        with jax.named_scope("halos"):
            return (
                lax.ppermute(outer, "passage", across),
                lax.ppermute(inner, "passage", within),
                lax.ppermute(a, "cell", even),
                lax.ppermute(b, "cell", odd),
            )

    packed = call(
        prepare_kernel, sends, (ids, start), [SMEM, VMEM], 4, 10**6, "prepare"
    )
    with jax.named_scope("other_times"):
        pa = lax.ppermute(packed[0], "tm", swap)
        pb = lax.ppermute(packed[1], "tm", swap)
    outer, inner, ha, hb = exchange(*packed)
    rhs = call(
        rhs_kernel,
        [field_like],
        (ids, start, source, pa, pb),
        [SMEM] + [VMEM] * 4,
        4,
        10**7,
        "rhs",
    )[0]
    ordered = call(
        order_kernel,
        [jax.ShapeDtypeStruct((nt * nv, ni * nk), F32)],
        (ids, cells, weights.transpose(1, 0, 2)),
        [SMEM, VMEM, VMEM],
        8,
        10**6,
        "order",
    )[0]
    fixed = (jac, sigma, damping)

    def local(field, outer, inner, name):
        args = (ids, field, rhs, *fixed, outer, inner)
        specs = [SMEM] + [VMEM] * 7
        return call(local_kernel, [field_like], args, specs, 4, 2 * 10**7, name)[0]

    part = local(start, outer, inner, "first_local")
    field, *packed = call(
        first_kernel,
        [field_like] + sends,
        (ids, part, *fixed, ha, hb),
        [SMEM] + [VMEM] * 6,
        4,
        10**7,
        "first_finish",
    )
    outer, inner, ha, hb = exchange(*packed)
    part = local(field, outer, inner, "second_local")
    sens = call(
        surface_kernel,
        [jax.ShapeDtypeStruct((2 * ring, ni * nk // 128, 128), F32)],
        (ids, part, *fixed, ha, hb, ordered),
        [SMEM] + [VMEM] * 7,
        4,
        5 * 10**6,
        "surface",
    )[0]
    token_like = jax.ShapeDtypeStruct((8, 128), F32)
    with jax.named_scope("share_sensitivities"):
        gathered = lax.all_to_all(sens, ("passage", "tm"), 0, 0, tiled=True)
    field, done = call(
        second_kernel,
        [field_like, token_like],
        (ids, part, *fixed, ha, hb),
        [SMEM] + [VMEM] * 6,
        4,
        10**7,
        "second_finish",
    )
    modes = call(
        modes_kernel,
        [jax.ShapeDtypeStruct((2 * PASSAGES, cells.shape[1]), F32)],
        (cells, gathered, done),
        [VMEM] * 3,
        8,
        10**7,
        "modes",
    )[0]
    return field, modes.reshape(2, PASSAGES, -1)


def solution(mesh):
    in_specs = (
        P("tm", None, "cell", "passage", None),
        P("tm", None, "cell", "passage", None),
        P(None, None, None, "cell", "passage", None),
        P("cell", "passage", None),
        P("cell", "passage", None),
        P("cell", None),
        P("tm", None, "cell"),
    )
    out_specs = (P("tm", None, "cell", "passage", None), P(None, None, "cell"))
    return jax.shard_map(
        body, mesh=mesh, in_specs=in_specs, out_specs=out_specs, check_vma=False
    )
```

```python
import functools
import math

import jax
import jax.numpy as jnp
from jax import lax
from jax.experimental import pallas as pl
from jax.experimental.pallas import tpu as pltpu
from jax.sharding import PartitionSpec as P

PASSAGES = 16
NT = 8
F32 = jnp.float32
BF16 = jnp.bfloat16
VMEM = pl.BlockSpec(memory_space=pltpu.VMEM)
SMEM = pl.BlockSpec(memory_space=pltpu.SMEM)


def derivative(offset):
    offset = offset % NT
    if offset in (0, NT // 2):
        return 0.0
    angle = math.pi * offset / NT
    return 0.5 * (-1) ** offset * math.cos(angle) / math.sin(angle)


def call(kernel, outs, args, specs, mib, flops, name):
    nbytes = sum(a.size * a.dtype.itemsize for a in args) + sum(
        math.prod(o.shape) * o.dtype.itemsize for o in outs
    )
    return pl.pallas_call(
        kernel,
        out_shape=outs,
        in_specs=specs,
        out_specs=[VMEM] * len(outs),
        compiler_params=pltpu.CompilerParams(vmem_limit_bytes=mib << 20),
        cost_estimate=pl.CostEstimate(
            flops=flops, bytes_accessed=nbytes, transcendentals=0
        ),
        name=name,
    )(*args)


def by_parity(ids_ref, run):
    @pl.when(ids_ref[0] == 0)
    def _():
        run(1, 0)

    @pl.when(ids_ref[0] != 0)
    def _():
        run(0, 1)


def edge_row(ids_ref, f_ref, t, v, i, outer):
    nj = f_ref.shape[3]
    low, high = f_ref[t, v, i, 0:1, :], f_ref[t, v, i, nj - 1 : nj, :]
    first = ids_ref[1] == (0 if outer else 1)
    return jnp.where(first, low, high)


def pack_layers(f_ref, a_ref, b_ref, layer_a, layer_b):
    nt, nv = f_ref.shape[:2]
    for t in range(nt):
        for v in range(nv):
            a_ref[t, v] = f_ref[t, v, layer_a].astype(BF16)
            b_ref[t, v] = f_ref[t, v, layer_b].astype(BF16)


def pack_rows(ids_ref, f_ref, outer_ref, inner_ref):
    nt, nv, ni = f_ref.shape[:3]
    for t in range(nt):
        for v in range(nv):
            for i in range(ni):
                row = (t * nv + v) * ni + i
                here = slice(row, row + 1)
                outer_ref[here, :] = edge_row(ids_ref, f_ref, t, v, i, True)
                inner_ref[here, :] = edge_row(ids_ref, f_ref, t, v, i, False)


def prepare_kernel(ids_ref, f_ref, a_ref, b_ref, outer_ref, inner_ref):
    pack_rows(ids_ref, f_ref, outer_ref, inner_ref)
    by_parity(ids_ref, functools.partial(pack_layers, f_ref, a_ref, b_ref))


def rhs_kernel(ids_ref, f_ref, src_ref, pa_ref, pb_ref, out_ref):
    nt, nv, ni, nj, nk = f_ref.shape

    def run(layer_a, layer_b):
        for layer, other in ((layer_a, pa_ref), (layer_b, pb_ref)):

            def one(v, carry):
                for j in range(0, nj, 16):
                    rows = slice(j, j + 16)
                    own = [
                        f_ref[t, v, layer, rows, :].astype(BF16).astype(F32)
                        for t in range(nt)
                    ]
                    far = [other[t, v, rows, :].astype(F32) for t in range(nt)]
                    times = own + far
                    for b in range(nt):
                        total = src_ref[b, v, layer, rows, :]
                        for n in range(1, NT // 2):
                            diff = times[(b + n) % NT] - times[(b - n) % NT]
                            total = total - derivative(n) * diff
                        out_ref[b, v, layer, rows, :] = total
                return carry

            lax.fori_loop(0, nv, one, 0)

    by_parity(ids_ref, run)


def shifted(f_ref, t, u, i, j, lanes, rows_id):
    nj = f_ref.shape[3]
    here = f_ref[t, u, i, j : j + 8, lanes]
    after = before = jnp.zeros_like(here)
    if j + 8 < nj:
        after = pltpu.roll(f_ref[t, u, i, j + 8 : j + 16, lanes], 7, 0)
    if j > 0:
        before = pltpu.roll(f_ref[t, u, i, j - 8 : j, lanes], 1, 0)
    plus = jnp.where(rows_id == 7, after, pltpu.roll(here, 7, 0))
    minus = jnp.where(rows_id == 0, before, pltpu.roll(here, 1, 0))
    return here, plus, minus


def local_tile(refs, i, j, lanes):
    f_ref, rhs_ref, jac_ref, sig_ref, dmp_ref = refs
    nt, nv, ni = f_ref.shape[:3]
    pair = slice(j // 16 * 16, j // 16 * 16 + 16)
    half = slice(j % 16, j % 16 + 8)
    sigma = sig_ref[i, j : j + 8, lanes]
    damping = dmp_ref[i, j : j + 8, lanes]
    scaling = 1.0 / (sigma + 4.0 * damping)
    rows_id = lax.broadcasted_iota(jnp.int32, sigma.shape, 0)
    acc = [[None] * nv for _ in range(nt)]
    for u in range(nv):
        jac = [
            [jac_ref[d, u, v, i, pair, lanes].astype(F32)[half] for v in range(nv)]
            for d in range(2)
        ]
        for t in range(nt):
            here, plus_j, minus_j = shifted(f_ref, t, u, i, j, lanes, rows_id)
            inner = f_ref[t, u, 1 - i, j : j + 8, lanes]
            diff_i = here if i else here - inner
            diff_j = here - plus_j
            both = (here + (here - inner)) + (diff_j + (here - minus_j))
            own = sigma * here + damping * both
            for v in range(nv):
                term = jac[0][v] * diff_i + jac[1][v] * diff_j
                if v == u:
                    term = term + own
                acc[t][v] = term if acc[t][v] is None else acc[t][v] + term
    return [
        [
            f_ref[t, v, i, j : j + 8, lanes]
            + (rhs_ref[t, v, i, j : j + 8, lanes] - acc[t][v]) * scaling
            for v in range(nv)
        ]
        for t in range(nt)
    ]


def finish_tile(upper, refs, layer_ref, i, j, lanes):
    part_ref, jac_i_ref, jac_j_ref, sig_ref, dmp_ref, outer_ref, inner_ref = refs
    nt, nv, ni, nj, nk = part_ref.shape
    pair = slice(j // 16 * 16, j // 16 * 16 + 16)
    half = slice(j % 16, j % 16 + 8)
    sigma = sig_ref[i, j : j + 8, lanes]
    damping = dmp_ref[i, j : j + 8, lanes]
    scaling = 1.0 / (sigma + 4.0 * damping)
    damping = damping * scaling
    first, last = j == 0, j == nj - 8
    rows_id = lax.broadcasted_iota(jnp.int32, sigma.shape, 0)
    acc = [[0.0] * nv for _ in range(nt)]

    def edge(t, u, high):
        row = (t * nv + u) * ni + i
        outer = outer_ref[row : row + 1, lanes]
        inner = inner_ref[row : row + 1, lanes]
        value = jnp.where(upper == high, outer, inner)
        mask = rows_id == (7 if high else 0)
        return jnp.where(mask, jnp.broadcast_to(value, sigma.shape), 0.0)

    for u in range(nv):
        jac_i = jac_j = None
        if i > 0:
            jac_i = [
                jac_i_ref[u, v, pair, lanes].astype(F32)[half] * scaling
                for v in range(nv)
            ]
        if last:
            jac_j = [
                jac_j_ref[u, v, i, :, lanes].astype(F32)[8:] * scaling
                for v in range(nv)
            ]
        for t in range(nt):
            layer = layer_ref[t, u, pair, lanes].astype(F32)[half]
            near = layer
            if first:
                near = near + edge(t, u, False)
            if last:
                high = edge(t, u, True)
                near = near + high
            acc[t][u] = acc[t][u] + damping * near
            for v in range(nv):
                if jac_i is not None:
                    acc[t][v] = acc[t][v] + jac_i[v] * layer
                if jac_j is not None:
                    acc[t][v] = acc[t][v] + jac_j[v] * high
    return [
        [part_ref[t, v, i, j : j + 8, lanes] + acc[t][v] for v in range(nv)]
        for t in range(nt)
    ]


def lanes_at(k):
    return pl.ds(pl.multiple_of(k * 128, 128), 128)


def local_kernel(*refs):
    ins, out_ref = refs[:5], refs[5]
    nt, nv, ni, nj, nk = out_ref.shape

    def one(k, carry):
        lanes = lanes_at(k)
        for i in range(ni):
            for j in range(0, nj, 8):
                new = local_tile(ins, i, j, lanes)
                for t in range(nt):
                    for v in range(nv):
                        out_ref[t, v, i, j : j + 8, lanes] = new[t][v]
        return carry

    lax.fori_loop(0, nk // 128, one, 0)


def finish_all(ids_ref, ins, out_ref, layers):
    nt, nv, ni, nj, nk = out_ref.shape
    upper = ids_ref[1] == 1

    def one(k, carry):
        lanes = lanes_at(k)
        for i in range(ni):
            for j in range(0, nj, 8):
                new = finish_tile(upper, ins, layers[i], i, j, lanes)
                for t in range(nt):
                    for v in range(nv):
                        out_ref[t, v, i, j : j + 8, lanes] = new[t][v]
        return carry

    lax.fori_loop(0, nk // 128, one, 0)


def first_kernel(ids_ref, *refs):
    ins, ha_ref, hb_ref = refs[:7], refs[7], refs[8]
    out_ref, a_ref, b_ref, no_ref, ni_ref = refs[9:]

    def run(layer_a, layer_b):
        finish_all(ids_ref, ins, out_ref, {layer_a: ha_ref, layer_b: hb_ref})
        pack_layers(out_ref, a_ref, b_ref, layer_a, layer_b)

    by_parity(ids_ref, run)
    pack_rows(ids_ref, out_ref, no_ref, ni_ref)


def surface_kernel(ids_ref, *refs):
    ins, ha_ref, hb_ref, w_ref, sens_ref = refs[:7], *refs[7:11]
    nt, nv, ni, nj, nk = ins[0].shape

    def row_of(side, layers):
        j = side * (nj - 8)
        mask = lax.broadcasted_iota(jnp.int32, (8, 128), 0) == side * 7
        values = []
        for i in range(ni):
            for k in range(0, nk, 128):
                new = finish_tile(side == 1, ins, layers[i], i, j, slice(k, k + 128))
                total = jnp.zeros((8, 128), F32)
                for t in range(nt):
                    for v in range(nv):
                        at = t * nv + v
                        weight = w_ref[at : at + 1, i * nk + k : i * nk + k + 128]
                        total = total + new[t][v] * weight
                values.append(
                    jnp.sum(jnp.where(mask, total, 0.0), axis=0, keepdims=True)
                )
        value = jnp.concatenate(values, axis=0)
        for member in range(sens_ref.shape[0]):
            sens_ref[member] = value

    def run(layer_a, layer_b):
        layers = {layer_a: ha_ref, layer_b: hb_ref}
        for side in range(2):
            pl.when(ids_ref[1] == side)(functools.partial(row_of, side, layers))

    by_parity(ids_ref, run)


def second_kernel(ids_ref, *refs):
    ins, ha_ref, hb_ref, out_ref, done_ref = refs[:7], *refs[7:11]
    done_ref[...] = jnp.zeros(done_ref.shape, F32)

    def run(layer_a, layer_b):
        finish_all(ids_ref, ins, out_ref, {layer_a: ha_ref, layer_b: hb_ref})

    by_parity(ids_ref, run)


def split3(x):
    one = x.astype(BF16)
    rest = x - one.astype(F32)
    two = rest.astype(BF16)
    three = (rest - two.astype(F32)).astype(BF16)
    return one, two, three


def one_hot(cells_ref, first, rows):
    cells = cells_ref.shape[1]
    index = lax.broadcasted_iota(jnp.int32, (rows, cells), 0) + first
    return jnp.where(cells_ref[0:1, :] == index, 1.0, 0.0).astype(BF16)


def order_kernel(ids_ref, cells_ref, w_ref, out_ref):
    rows, half = out_ref.shape
    nv, nt, _ = w_ref.shape
    own = one_hot(cells_ref, ids_ref[1] * half, half)
    parts = [part for v in range(nv) for part in split3(w_ref[v])]
    found = lax.dot_general(
        jnp.concatenate(parts, axis=0),
        own,
        (((1,), (1,)), ((), ())),
        preferred_element_type=F32,
    )
    for t in range(nt):
        for v in range(nv):
            one, two, three = (found[(v * 3 + p) * nt + t][None] for p in range(3))
            out_ref[t * nv + v : t * nv + v + 1, :] = one + (two + three)


def mode_table(side, modes, senders):
    row = lax.broadcasted_iota(jnp.int32, (2 * modes, senders), 0)
    sender = lax.broadcasted_iota(jnp.int32, (2 * modes, senders), 1)
    turns = ((row % modes) * (sender // 4)) % PASSAGES
    angle = turns.astype(F32) * (2.0 * math.pi / PASSAGES)
    value = jnp.where(row < modes, jnp.cos(angle), -jnp.sin(angle)) / PASSAGES**0.5
    return jnp.where((sender // 2) % 2 == side, value, 0.0)


def tables_kernel(cells_ref, done_ref, chosen_ref, table_ref):
    chosen_ref[...] = one_hot(cells_ref, 0, chosen_ref.shape[0])
    rows, senders = table_ref.shape
    for side in range(2):
        here = slice(side * rows // 2, (side + 1) * rows // 2)
        table_ref[here, :] = mode_table(side, rows // 4, senders)


def modes_kernel(chosen_ref, table_ref, sens_ref, out_ref):
    senders, pieces = sens_ref.shape[:2]
    half = pieces * 128
    rows = out_ref.shape[0]
    seen = jnp.concatenate([sens_ref[:, c, :] for c in range(pieces)], axis=1)
    both = jnp.dot(
        table_ref[...],
        seen,
        precision=lax.Precision.HIGHEST,
        preferred_element_type=F32,
    )
    modes = jnp.concatenate([both[:rows], both[rows:]], axis=1)
    found = jnp.dot(
        jnp.concatenate(split3(modes), axis=0),
        chosen_ref[...],
        preferred_element_type=F32,
    )
    out_ref[...] = found[:rows] + (found[rows : 2 * rows] + found[2 * rows :])


def body(start, source, jac, sigma, damping, cells, weights):
    nt, nv, ni, nj, nk = start.shape
    ring = lax.axis_size("passage")
    n_cell = lax.axis_size("cell")
    ids = jnp.stack([lax.axis_index("cell") & 1, lax.axis_index("passage") & 1])
    even = [(c, c ^ 1) for c in range(n_cell)]
    odd = [(c, c + 1) for c in range(1, n_cell - 1, 2)]
    odd += [(b, a) for a, b in odd]
    within = [(d, d ^ 1) for d in range(ring)]
    across = [(d, (d + 1) % ring) for d in range(1, ring, 2)]
    across += [(b, a) for a, b in across]
    swap = [(0, 1), (1, 0)]

    field_like = jax.ShapeDtypeStruct(start.shape, F32)
    layer_like = jax.ShapeDtypeStruct((nt, nv, nj, nk), BF16)
    rows_like = jax.ShapeDtypeStruct((nt * nv * ni, nk), F32)

    sends = [layer_like, layer_like, rows_like, rows_like]

    def exchange(a, b, outer, inner):
        with jax.named_scope("halos"):
            return (
                lax.ppermute(outer, "passage", across),
                lax.ppermute(inner, "passage", within),
                lax.ppermute(a, "cell", even),
                lax.ppermute(b, "cell", odd),
            )

    packed = call(
        prepare_kernel, sends, (ids, start), [SMEM, VMEM], 4, 10**6, "prepare"
    )
    with jax.named_scope("other_times"):
        pa = lax.ppermute(packed[0], "tm", swap)
        pb = lax.ppermute(packed[1], "tm", swap)
    halos = exchange(*packed)
    rhs = call(
        rhs_kernel,
        [field_like],
        (ids, start, source, pa, pb),
        [SMEM] + [VMEM] * 4,
        4,
        10**7,
        "rhs",
    )[0]
    ordered = call(
        order_kernel,
        [jax.ShapeDtypeStruct((nt * nv, ni * nk), F32)],
        (ids, cells, weights.transpose(1, 0, 2)),
        [SMEM, VMEM, VMEM],
        8,
        10**6,
        "order",
    )[0]
    def local(field, name):
        args = (field, rhs, jac, sigma, damping)
        return call(local_kernel, [field_like], args, [VMEM] * 5, 4, 2 * 10**7, name)[0]

    jac_i = jac[0, :, :, ni - 1]
    jac_j = jac[1, :, :, :, nj - 16 :]

    def finish(kernel, outs, part, halos, more, name):
        outer, inner, ha, hb = halos
        args = (ids, part, jac_i, jac_j, sigma, damping, outer, inner, ha, hb, *more)
        specs = [SMEM] + [VMEM] * (len(args) - 1)
        return call(kernel, outs, args, specs, 4, 10**7, name)

    field, *packed = finish(
        first_kernel,
        [field_like] + sends,
        local(start, "first_local"),
        halos,
        (),
        "first_finish",
    )
    halos = exchange(*packed)
    part = local(field, "second_local")
    share_like = jax.ShapeDtypeStruct((2 * ring, ni * nk // 128, 128), F32)
    sens = finish(surface_kernel, [share_like], part, halos, (ordered,), "surface")[0]
    with jax.named_scope("share_sensitivities"):
        gathered = lax.all_to_all(sens, ("passage", "tm"), 0, 0, tiled=True)
    token_like = jax.ShapeDtypeStruct((8, 128), F32)
    field, done = finish(
        second_kernel, [field_like, token_like], part, halos, (), "second_finish"
    )
    chosen, table = call(
        tables_kernel,
        [
            jax.ShapeDtypeStruct((cells.shape[1], cells.shape[1]), BF16),
            jax.ShapeDtypeStruct((4 * PASSAGES, 2 * ring), F32),
        ],
        (cells, done),
        [VMEM] * 2,
        8,
        10**6,
        "tables",
    )
    modes = call(
        modes_kernel,
        [jax.ShapeDtypeStruct((2 * PASSAGES, cells.shape[1]), F32)],
        (chosen, table, gathered),
        [VMEM] * 3,
        8,
        10**7,
        "modes",
    )[0]
    return field, modes.reshape(2, PASSAGES, -1)


def solution(mesh):
    in_specs = (
        P("tm", None, "cell", "passage", None),
        P("tm", None, "cell", "passage", None),
        P(None, None, None, "cell", "passage", None),
        P("cell", "passage", None),
        P("cell", "passage", None),
        P("cell", None),
        P("tm", None, "cell"),
    )
    out_specs = (P("tm", None, "cell", "passage", None), P(None, None, "cell"))
    return jax.shard_map(
        body, mesh=mesh, in_specs=in_specs, out_specs=out_specs, check_vma=False
    )
```

```python
import functools
import math

import jax
import jax.numpy as jnp
from jax import lax
from jax.experimental import pallas as pl
from jax.experimental.pallas import tpu as pltpu
from jax.sharding import PartitionSpec as P

PASSAGES = 16
NT = 8
F32 = jnp.float32
BF16 = jnp.bfloat16
VMEM = pl.BlockSpec(memory_space=pltpu.VMEM)
SMEM = pl.BlockSpec(memory_space=pltpu.SMEM)


def derivative(offset):
    offset = offset % NT
    if offset in (0, NT // 2):
        return 0.0
    angle = math.pi * offset / NT
    return 0.5 * (-1) ** offset * math.cos(angle) / math.sin(angle)


def call(kernel, outs, args, specs, mib, flops, name):
    nbytes = sum(a.size * a.dtype.itemsize for a in args) + sum(
        math.prod(o.shape) * o.dtype.itemsize for o in outs
    )
    return pl.pallas_call(
        kernel,
        out_shape=outs,
        in_specs=specs,
        out_specs=[VMEM] * len(outs),
        compiler_params=pltpu.CompilerParams(vmem_limit_bytes=mib << 20),
        cost_estimate=pl.CostEstimate(
            flops=flops, bytes_accessed=nbytes, transcendentals=0
        ),
        name=name,
    )(*args)


def by_parity(ids_ref, run):
    @pl.when(ids_ref[0] == 0)
    def _():
        run(1, 0)

    @pl.when(ids_ref[0] != 0)
    def _():
        run(0, 1)


def edge_row(ids_ref, f_ref, t, v, i, outer):
    nj = f_ref.shape[3]
    low, high = f_ref[t, v, i, 0:1, :], f_ref[t, v, i, nj - 1 : nj, :]
    first = ids_ref[1] == (0 if outer else 1)
    return jnp.where(first, low, high)


def pack_layers(f_ref, a_ref, b_ref, layer_a, layer_b):
    nt, nv = f_ref.shape[:2]
    for t in range(nt):
        for v in range(nv):
            a_ref[t, v] = f_ref[t, v, layer_a].astype(BF16)
            b_ref[t, v] = f_ref[t, v, layer_b].astype(BF16)


def pack_rows(ids_ref, f_ref, outer_ref, inner_ref):
    nt, nv, ni = f_ref.shape[:3]
    for t in range(nt):
        for v in range(nv):
            for i in range(ni):
                row = (t * nv + v) * ni + i
                here = slice(row, row + 1)
                outer_ref[here, :] = edge_row(ids_ref, f_ref, t, v, i, True)
                inner_ref[here, :] = edge_row(ids_ref, f_ref, t, v, i, False)


def prepare_kernel(ids_ref, f_ref, a_ref, b_ref, outer_ref, inner_ref):
    pack_rows(ids_ref, f_ref, outer_ref, inner_ref)
    by_parity(ids_ref, functools.partial(pack_layers, f_ref, a_ref, b_ref))


def rhs_kernel(ids_ref, f_ref, src_ref, pa_ref, pb_ref, out_ref):
    nt, nv, ni, nj, nk = f_ref.shape

    def run(layer_a, layer_b):
        for layer, other in ((layer_a, pb_ref), (layer_b, pa_ref)):

            def one(v, carry):
                for j in range(0, nj, 16):
                    rows = slice(j, j + 16)
                    own = [
                        f_ref[t, v, layer, rows, :].astype(BF16).astype(F32)
                        for t in range(nt)
                    ]
                    far = [other[t, v, rows, :].astype(F32) for t in range(nt)]
                    times = own + far
                    for b in range(nt):
                        total = src_ref[b, v, layer, rows, :]
                        for n in range(1, NT // 2):
                            diff = times[(b + n) % NT] - times[(b - n) % NT]
                            total = total - derivative(n) * diff
                        out_ref[b, v, layer, rows, :] = total
                return carry

            lax.fori_loop(0, nv, one, 0)

    by_parity(ids_ref, run)


def shifted(f_ref, t, u, i, j, lanes, rows_id):
    nj = f_ref.shape[3]
    here = f_ref[t, u, i, j : j + 8, lanes]
    after = before = jnp.zeros_like(here)
    if j + 8 < nj:
        after = pltpu.roll(f_ref[t, u, i, j + 8 : j + 16, lanes], 7, 0)
    if j > 0:
        before = pltpu.roll(f_ref[t, u, i, j - 8 : j, lanes], 1, 0)
    plus = jnp.where(rows_id == 7, after, pltpu.roll(here, 7, 0))
    minus = jnp.where(rows_id == 0, before, pltpu.roll(here, 1, 0))
    return here, plus, minus


def local_tile(refs, i, j, lanes):
    f_ref, rhs_ref, jac_ref, sig_ref, dmp_ref = refs
    nt, nv, ni = f_ref.shape[:3]
    pair = slice(j // 16 * 16, j // 16 * 16 + 16)
    half = slice(j % 16, j % 16 + 8)
    sigma = sig_ref[i, j : j + 8, lanes]
    damping = dmp_ref[i, j : j + 8, lanes]
    scaling = 1.0 / (sigma + 4.0 * damping)
    rows_id = lax.broadcasted_iota(jnp.int32, sigma.shape, 0)
    acc = [[None] * nv for _ in range(nt)]
    for u in range(nv):
        jac = [
            [jac_ref[d, u, v, i, pair, lanes].astype(F32)[half] for v in range(nv)]
            for d in range(2)
        ]
        for t in range(nt):
            here, plus_j, minus_j = shifted(f_ref, t, u, i, j, lanes, rows_id)
            inner = f_ref[t, u, 1 - i, j : j + 8, lanes]
            diff_i = here if i else here - inner
            diff_j = here - plus_j
            both = (here + (here - inner)) + (diff_j + (here - minus_j))
            own = sigma * here + damping * both
            for v in range(nv):
                term = jac[0][v] * diff_i + jac[1][v] * diff_j
                if v == u:
                    term = term + own
                acc[t][v] = term if acc[t][v] is None else acc[t][v] + term
    return [
        [
            f_ref[t, v, i, j : j + 8, lanes]
            + (rhs_ref[t, v, i, j : j + 8, lanes] - acc[t][v]) * scaling
            for v in range(nv)
        ]
        for t in range(nt)
    ]


def finish_tile(upper, refs, layer_ref, i, j, lanes):
    part_ref, jac_i_ref, jac_j_ref, sig_ref, dmp_ref, outer_ref, inner_ref = refs
    nt, nv, ni, nj, nk = part_ref.shape
    pair = slice(j // 16 * 16, j // 16 * 16 + 16)
    half = slice(j % 16, j % 16 + 8)
    sigma = sig_ref[i, j : j + 8, lanes]
    damping = dmp_ref[i, j : j + 8, lanes]
    scaling = 1.0 / (sigma + 4.0 * damping)
    damping = damping * scaling
    first, last = j == 0, j == nj - 8
    rows_id = lax.broadcasted_iota(jnp.int32, sigma.shape, 0)
    acc = [[0.0] * nv for _ in range(nt)]

    def edge(t, u, high):
        row = (t * nv + u) * ni + i
        outer = outer_ref[row : row + 1, lanes]
        inner = inner_ref[row : row + 1, lanes]
        value = jnp.where(upper == high, outer, inner)
        mask = rows_id == (7 if high else 0)
        return jnp.where(mask, jnp.broadcast_to(value, sigma.shape), 0.0)

    for u in range(nv):
        jac_i = jac_j = None
        if i > 0:
            jac_i = [
                jac_i_ref[u, v, pair, lanes].astype(F32)[half] * scaling
                for v in range(nv)
            ]
        if last:
            jac_j = [
                jac_j_ref[u, v, i, :, lanes].astype(F32)[8:] * scaling
                for v in range(nv)
            ]
        for t in range(nt):
            layer = layer_ref[t, u, pair, lanes].astype(F32)[half]
            near = layer
            if first:
                near = near + edge(t, u, False)
            if last:
                high = edge(t, u, True)
                near = near + high
            acc[t][u] = acc[t][u] + damping * near
            for v in range(nv):
                if jac_i is not None:
                    acc[t][v] = acc[t][v] + jac_i[v] * layer
                if jac_j is not None:
                    acc[t][v] = acc[t][v] + jac_j[v] * high
    return [
        [part_ref[t, v, i, j : j + 8, lanes] + acc[t][v] for v in range(nv)]
        for t in range(nt)
    ]


def lanes_at(k):
    return pl.ds(pl.multiple_of(k * 128, 128), 128)


def local_kernel(*refs):
    ins, out_ref = refs[:5], refs[5]
    nt, nv, ni, nj, nk = out_ref.shape

    def one(k, carry):
        lanes = lanes_at(k)
        for i in range(ni):
            for j in range(0, nj, 8):
                new = local_tile(ins, i, j, lanes)
                for t in range(nt):
                    for v in range(nv):
                        out_ref[t, v, i, j : j + 8, lanes] = new[t][v]
        return carry

    lax.fori_loop(0, nk // 128, one, 0)


def finish_all(ids_ref, ins, out_ref, layers):
    nt, nv, ni, nj, nk = out_ref.shape
    upper = ids_ref[1] == 1

    def one(k, carry):
        lanes = lanes_at(k)
        for i in range(ni):
            for j in range(0, nj, 8):
                new = finish_tile(upper, ins, layers[i], i, j, lanes)
                for t in range(nt):
                    for v in range(nv):
                        out_ref[t, v, i, j : j + 8, lanes] = new[t][v]
        return carry

    lax.fori_loop(0, nk // 128, one, 0)


def first_kernel(ids_ref, *refs):
    ins, ha_ref, hb_ref = refs[:7], refs[7], refs[8]
    out_ref, a_ref, b_ref, no_ref, ni_ref = refs[9:]

    def run(layer_a, layer_b):
        finish_all(ids_ref, ins, out_ref, {layer_a: ha_ref, layer_b: hb_ref})
        pack_layers(out_ref, a_ref, b_ref, layer_a, layer_b)

    by_parity(ids_ref, run)
    pack_rows(ids_ref, out_ref, no_ref, ni_ref)


def surface_kernel(ids_ref, *refs):
    ins, ha_ref, hb_ref, w_ref, sens_ref = refs[:7], *refs[7:11]
    nt, nv, ni, nj, nk = ins[0].shape

    def row_of(side, layers):
        j = side * (nj - 8)
        mask = lax.broadcasted_iota(jnp.int32, (8, 128), 0) == side * 7
        values = []
        for i in range(ni):
            for k in range(0, nk, 128):
                new = finish_tile(side == 1, ins, layers[i], i, j, slice(k, k + 128))
                total = jnp.zeros((8, 128), F32)
                for t in range(nt):
                    for v in range(nv):
                        at = t * nv + v
                        weight = w_ref[at : at + 1, i * nk + k : i * nk + k + 128]
                        total = total + new[t][v] * weight
                values.append(
                    jnp.sum(jnp.where(mask, total, 0.0), axis=0, keepdims=True)
                )
        value = jnp.concatenate(values, axis=0)
        for member in range(sens_ref.shape[0]):
            sens_ref[member] = value

    def run(layer_a, layer_b):
        layers = {layer_a: ha_ref, layer_b: hb_ref}
        for side in range(2):
            pl.when(ids_ref[1] == side)(functools.partial(row_of, side, layers))

    by_parity(ids_ref, run)


def second_kernel(ids_ref, *refs):
    ins, ha_ref, hb_ref, out_ref, done_ref = refs[:7], *refs[7:11]
    done_ref[...] = jnp.zeros(done_ref.shape, F32)

    def run(layer_a, layer_b):
        finish_all(ids_ref, ins, out_ref, {layer_a: ha_ref, layer_b: hb_ref})

    by_parity(ids_ref, run)


def split3(x):
    one = x.astype(BF16)
    rest = x - one.astype(F32)
    two = rest.astype(BF16)
    three = (rest - two.astype(F32)).astype(BF16)
    return one, two, three


def one_hot(cells_ref, first, rows):
    cells = cells_ref.shape[1]
    index = lax.broadcasted_iota(jnp.int32, (rows, cells), 0) + first
    return jnp.where(cells_ref[0:1, :] == index, 1.0, 0.0).astype(BF16)


def order_kernel(ids_ref, cells_ref, w_ref, out_ref):
    rows, half = out_ref.shape
    nv, nt, _ = w_ref.shape
    own = one_hot(cells_ref, ids_ref[1] * half, half)
    parts = [part for v in range(nv) for part in split3(w_ref[v])]
    found = lax.dot_general(
        jnp.concatenate(parts, axis=0),
        own,
        (((1,), (1,)), ((), ())),
        preferred_element_type=F32,
    )
    for t in range(nt):
        for v in range(nv):
            one, two, three = (found[(v * 3 + p) * nt + t][None] for p in range(3))
            out_ref[t * nv + v : t * nv + v + 1, :] = one + (two + three)


def mode_table(side, modes, senders):
    row = lax.broadcasted_iota(jnp.int32, (2 * modes, senders), 0)
    sender = lax.broadcasted_iota(jnp.int32, (2 * modes, senders), 1)
    turns = ((row % modes) * (sender // 4)) % PASSAGES
    angle = turns.astype(F32) * (2.0 * math.pi / PASSAGES)
    value = jnp.where(row < modes, jnp.cos(angle), -jnp.sin(angle)) / PASSAGES**0.5
    return jnp.where((sender // 2) % 2 == side, value, 0.0)


def tables_kernel(cells_ref, done_ref, chosen_ref, table_ref):
    chosen_ref[...] = one_hot(cells_ref, 0, chosen_ref.shape[0])
    rows, senders = table_ref.shape
    for side in range(2):
        here = slice(side * rows // 2, (side + 1) * rows // 2)
        table_ref[here, :] = mode_table(side, rows // 4, senders)


def modes_kernel(chosen_ref, table_ref, sens_ref, out_ref):
    senders, pieces = sens_ref.shape[:2]
    half = pieces * 128
    rows = out_ref.shape[0]
    seen = jnp.concatenate([sens_ref[:, c, :] for c in range(pieces)], axis=1)
    both = jnp.dot(
        table_ref[...],
        seen,
        precision=lax.Precision.HIGHEST,
        preferred_element_type=F32,
    )
    modes = jnp.concatenate([both[:rows], both[rows:]], axis=1)
    found = jnp.dot(
        jnp.concatenate(split3(modes), axis=0),
        chosen_ref[...],
        preferred_element_type=F32,
    )
    out_ref[...] = found[:rows] + (found[rows : 2 * rows] + found[2 * rows :])


def body(start, source, jac, sigma, damping, cells, weights):
    nt, nv, ni, nj, nk = start.shape
    ring = lax.axis_size("passage")
    n_cell = lax.axis_size("cell")
    parity = (lax.axis_index("cell") ^ lax.axis_index("tm")) & 1
    ids = jnp.stack([parity, lax.axis_index("passage") & 1])
    even = [(c, c ^ 1) for c in range(n_cell)]
    odd = [(c, c + 1) for c in range(1, n_cell - 1, 2)]
    odd += [(b, a) for a, b in odd]
    turns = [
        [(2 * c + core, 2 * d + core) for core in range(2) for c, d in pairs[core]]
        for pairs in ((even, odd), (odd, even))
    ]
    within = [(d, d ^ 1) for d in range(ring)]
    across = [(d, (d + 1) % ring) for d in range(1, ring, 2)]
    across += [(b, a) for a, b in across]
    swap = [(0, 1), (1, 0)]

    field_like = jax.ShapeDtypeStruct(start.shape, F32)
    layer_like = jax.ShapeDtypeStruct((nt, nv, nj, nk), BF16)
    rows_like = jax.ShapeDtypeStruct((nt * nv * ni, nk), F32)

    sends = [layer_like, layer_like, rows_like, rows_like]

    def exchange(a, b, outer, inner):
        with jax.named_scope("halos"):
            return (
                lax.ppermute(outer, "passage", across),
                lax.ppermute(inner, "passage", within),
                lax.ppermute(a, ("cell", "tm"), turns[0]),
                lax.ppermute(b, ("cell", "tm"), turns[1]),
            )

    packed = call(
        prepare_kernel, sends, (ids, start), [SMEM, VMEM], 4, 10**6, "prepare"
    )
    with jax.named_scope("other_times"):
        pa = lax.ppermute(packed[0], "tm", swap)
        pb = lax.ppermute(packed[1], "tm", swap)
    halos = exchange(*packed)
    rhs = call(
        rhs_kernel,
        [field_like],
        (ids, start, source, pa, pb),
        [SMEM] + [VMEM] * 4,
        4,
        10**7,
        "rhs",
    )[0]
    ordered = call(
        order_kernel,
        [jax.ShapeDtypeStruct((nt * nv, ni * nk), F32)],
        (ids, cells, weights.transpose(1, 0, 2)),
        [SMEM, VMEM, VMEM],
        8,
        10**6,
        "order",
    )[0]
    def local(field, name):
        args = (field, rhs, jac, sigma, damping)
        return call(local_kernel, [field_like], args, [VMEM] * 5, 4, 2 * 10**7, name)[0]

    jac_i = jac[0, :, :, ni - 1]
    jac_j = jac[1, :, :, :, nj - 16 :]

    def finish(kernel, outs, part, halos, more, name):
        outer, inner, ha, hb = halos
        args = (ids, part, jac_i, jac_j, sigma, damping, outer, inner, ha, hb, *more)
        specs = [SMEM] + [VMEM] * (len(args) - 1)
        return call(kernel, outs, args, specs, 4, 10**7, name)

    field, *packed = finish(
        first_kernel,
        [field_like] + sends,
        local(start, "first_local"),
        halos,
        (),
        "first_finish",
    )
    halos = exchange(*packed)
    part = local(field, "second_local")
    share_like = jax.ShapeDtypeStruct((2 * ring, ni * nk // 128, 128), F32)
    sens = finish(surface_kernel, [share_like], part, halos, (ordered,), "surface")[0]
    with jax.named_scope("share_sensitivities"):
        gathered = lax.all_to_all(sens, ("passage", "tm"), 0, 0, tiled=True)
    token_like = jax.ShapeDtypeStruct((8, 128), F32)
    field, done = finish(
        second_kernel, [field_like, token_like], part, halos, (), "second_finish"
    )
    chosen, table = call(
        tables_kernel,
        [
            jax.ShapeDtypeStruct((cells.shape[1], cells.shape[1]), BF16),
            jax.ShapeDtypeStruct((4 * PASSAGES, 2 * ring), F32),
        ],
        (cells, done),
        [VMEM] * 2,
        8,
        10**6,
        "tables",
    )
    modes = call(
        modes_kernel,
        [jax.ShapeDtypeStruct((2 * PASSAGES, cells.shape[1]), F32)],
        (chosen, table, gathered),
        [VMEM] * 3,
        8,
        10**7,
        "modes",
    )[0]
    return field, modes.reshape(2, PASSAGES, -1)


def solution(mesh):
    in_specs = (
        P("tm", None, "cell", "passage", None),
        P("tm", None, "cell", "passage", None),
        P(None, None, None, "cell", "passage", None),
        P("cell", "passage", None),
        P("cell", "passage", None),
        P("cell", None),
        P("tm", None, "cell"),
    )
    out_specs = (P("tm", None, "cell", "passage", None), P(None, None, "cell"))
    return jax.shard_map(
        body, mesh=mesh, in_specs=in_specs, out_specs=out_specs, check_vma=False
    )
```

```python
import functools
import math

import jax
import jax.numpy as jnp
from jax import lax
from jax.experimental import pallas as pl
from jax.experimental.pallas import tpu as pltpu
from jax.sharding import PartitionSpec as P

PASSAGES = 16
NT = 8
F32 = jnp.float32
BF16 = jnp.bfloat16
VMEM = pl.BlockSpec(memory_space=pltpu.VMEM)
SMEM = pl.BlockSpec(memory_space=pltpu.SMEM)


def derivative(offset):
    offset = offset % NT
    if offset in (0, NT // 2):
        return 0.0
    angle = math.pi * offset / NT
    return 0.5 * (-1) ** offset * math.cos(angle) / math.sin(angle)


def call(kernel, outs, args, specs, mib, flops, name):
    nbytes = sum(a.size * a.dtype.itemsize for a in args) + sum(
        math.prod(o.shape) * o.dtype.itemsize for o in outs
    )
    return pl.pallas_call(
        kernel,
        out_shape=outs,
        in_specs=specs,
        out_specs=[VMEM] * len(outs),
        compiler_params=pltpu.CompilerParams(vmem_limit_bytes=mib << 20),
        cost_estimate=pl.CostEstimate(
            flops=flops, bytes_accessed=nbytes, transcendentals=0
        ),
        name=name,
    )(*args)


def by_parity(ids_ref, run):
    @pl.when(ids_ref[0] == 0)
    def _():
        run(1, 0)

    @pl.when(ids_ref[0] != 0)
    def _():
        run(0, 1)


def edge_row(ids_ref, f_ref, t, v, i, outer):
    nj = f_ref.shape[3]
    low, high = f_ref[t, v, i, 0:1, :], f_ref[t, v, i, nj - 1 : nj, :]
    first = ids_ref[1] == (0 if outer else 1)
    return jnp.where(first, low, high)


def pack_layers(f_ref, a_ref, b_ref, layer_a, layer_b):
    nt, nv = f_ref.shape[:2]
    for t in range(nt):
        for v in range(nv):
            a_ref[t, v] = f_ref[t, v, layer_a].astype(BF16)
            b_ref[t, v] = f_ref[t, v, layer_b].astype(BF16)


def pack_rows(ids_ref, f_ref, outer_ref, inner_ref):
    nt, nv, ni = f_ref.shape[:3]
    for t in range(nt):
        for v in range(nv):
            for i in range(ni):
                row = (t * nv + v) * ni + i
                here = slice(row, row + 1)
                outer_ref[here, :] = edge_row(ids_ref, f_ref, t, v, i, True)
                inner_ref[here, :] = edge_row(ids_ref, f_ref, t, v, i, False)


def prepare_kernel(ids_ref, f_ref, a_ref, b_ref, outer_ref, inner_ref):
    pack_rows(ids_ref, f_ref, outer_ref, inner_ref)
    by_parity(ids_ref, functools.partial(pack_layers, f_ref, a_ref, b_ref))


def rhs_kernel(ids_ref, f_ref, src_ref, pa_ref, pb_ref, out_ref):
    nt, nv, ni, nj, nk = f_ref.shape

    def run(layer_a, layer_b):
        for layer, other in ((layer_a, pa_ref), (layer_b, pb_ref)):

            def one(v, carry):
                for j in range(0, nj, 16):
                    rows = slice(j, j + 16)
                    own = [
                        f_ref[t, v, layer, rows, :].astype(BF16).astype(F32)
                        for t in range(nt)
                    ]
                    far = [other[t, v, rows, :].astype(F32) for t in range(nt)]
                    times = own + far
                    for b in range(nt):
                        total = src_ref[b, v, layer, rows, :]
                        for n in range(1, NT // 2):
                            diff = times[(b + n) % NT] - times[(b - n) % NT]
                            total = total - derivative(n) * diff
                        out_ref[b, v, layer, rows, :] = total
                return carry

            lax.fori_loop(0, nv, one, 0)

    by_parity(ids_ref, run)


def shifted(f_ref, t, u, i, j, lanes, rows_id):
    nj = f_ref.shape[3]
    here = f_ref[t, u, i, j : j + 8, lanes]
    after = before = jnp.zeros_like(here)
    if j + 8 < nj:
        after = pltpu.roll(f_ref[t, u, i, j + 8 : j + 16, lanes], 7, 0)
    if j > 0:
        before = pltpu.roll(f_ref[t, u, i, j - 8 : j, lanes], 1, 0)
    plus = jnp.where(rows_id == 7, after, pltpu.roll(here, 7, 0))
    minus = jnp.where(rows_id == 0, before, pltpu.roll(here, 1, 0))
    return here, plus, minus


def local_tile(refs, i, j, lanes):
    f_ref, rhs_ref, jac_ref, sig_ref, dmp_ref = refs
    nt, nv, ni = f_ref.shape[:3]
    pair = slice(j // 16 * 16, j // 16 * 16 + 16)
    half = slice(j % 16, j % 16 + 8)
    sigma = sig_ref[i, j : j + 8, lanes]
    damping = dmp_ref[i, j : j + 8, lanes]
    scaling = 1.0 / (sigma + 4.0 * damping)
    rows_id = lax.broadcasted_iota(jnp.int32, sigma.shape, 0)
    acc = [[None] * nv for _ in range(nt)]
    for u in range(nv):
        jac = [
            [jac_ref[d, u, v, i, pair, lanes].astype(F32)[half] for v in range(nv)]
            for d in range(2)
        ]
        for t in range(nt):
            here, plus_j, minus_j = shifted(f_ref, t, u, i, j, lanes, rows_id)
            inner = f_ref[t, u, 1 - i, j : j + 8, lanes]
            diff_i = here if i else here - inner
            diff_j = here - plus_j
            both = (here + (here - inner)) + (diff_j + (here - minus_j))
            own = sigma * here + damping * both
            for v in range(nv):
                term = jac[0][v] * diff_i + jac[1][v] * diff_j
                if v == u:
                    term = term + own
                acc[t][v] = term if acc[t][v] is None else acc[t][v] + term
    return [
        [
            f_ref[t, v, i, j : j + 8, lanes]
            + (rhs_ref[t, v, i, j : j + 8, lanes] - acc[t][v]) * scaling
            for v in range(nv)
        ]
        for t in range(nt)
    ]


def finish_tile(upper, refs, layer_ref, i, j, lanes):
    part_ref, jac_i_ref, jac_j_ref, sig_ref, dmp_ref, outer_ref, inner_ref = refs
    nt, nv, ni, nj, nk = part_ref.shape
    pair = slice(j // 16 * 16, j // 16 * 16 + 16)
    half = slice(j % 16, j % 16 + 8)
    sigma = sig_ref[i, j : j + 8, lanes]
    damping = dmp_ref[i, j : j + 8, lanes]
    scaling = 1.0 / (sigma + 4.0 * damping)
    damping = damping * scaling
    first, last = j == 0, j == nj - 8
    rows_id = lax.broadcasted_iota(jnp.int32, sigma.shape, 0)
    acc = [[0.0] * nv for _ in range(nt)]

    def edge(t, u, high):
        row = (t * nv + u) * ni + i
        outer = outer_ref[row : row + 1, lanes]
        inner = inner_ref[row : row + 1, lanes]
        value = jnp.where(upper == high, outer, inner)
        mask = rows_id == (7 if high else 0)
        return jnp.where(mask, jnp.broadcast_to(value, sigma.shape), 0.0)

    for u in range(nv):
        jac_i = jac_j = None
        if i > 0:
            jac_i = [
                jac_i_ref[u, v, pair, lanes].astype(F32)[half] * scaling
                for v in range(nv)
            ]
        if last:
            jac_j = [
                jac_j_ref[u, v, i, :, lanes].astype(F32)[8:] * scaling
                for v in range(nv)
            ]
        for t in range(nt):
            layer = layer_ref[t, u, pair, lanes].astype(F32)[half]
            near = layer
            if first:
                near = near + edge(t, u, False)
            if last:
                high = edge(t, u, True)
                near = near + high
            acc[t][u] = acc[t][u] + damping * near
            for v in range(nv):
                if jac_i is not None:
                    acc[t][v] = acc[t][v] + jac_i[v] * layer
                if jac_j is not None:
                    acc[t][v] = acc[t][v] + jac_j[v] * high
    return [
        [part_ref[t, v, i, j : j + 8, lanes] + acc[t][v] for v in range(nv)]
        for t in range(nt)
    ]


def lanes_at(k):
    return pl.ds(pl.multiple_of(k * 128, 128), 128)


def local_kernel(*refs):
    ins, out_ref, slices = refs[:5], refs[5], refs[6:]
    nt, nv, ni, nj, nk = out_ref.shape
    if slices:
        jac_ref, (jac_i_ref, jac_j_ref) = ins[2], slices
        for u in range(nv):
            for v in range(nv):
                jac_i_ref[u, v] = jac_ref[0, u, v, ni - 1]
                for i in range(ni):
                    jac_j_ref[u, v, i] = jac_ref[1, u, v, i, nj - 16 :, :]

    def one(k, carry):
        lanes = lanes_at(k)
        for i in range(ni):
            for j in range(0, nj, 8):
                new = local_tile(ins, i, j, lanes)
                for t in range(nt):
                    for v in range(nv):
                        out_ref[t, v, i, j : j + 8, lanes] = new[t][v]
        return carry

    lax.fori_loop(0, nk // 128, one, 0)


def finish_all(ids_ref, ins, out_ref, layers):
    nt, nv, ni, nj, nk = out_ref.shape
    upper = ids_ref[1] == 1

    def one(k, carry):
        lanes = lanes_at(k)
        for i in range(ni):
            for j in range(0, nj, 8):
                new = finish_tile(upper, ins, layers[i], i, j, lanes)
                for t in range(nt):
                    for v in range(nv):
                        out_ref[t, v, i, j : j + 8, lanes] = new[t][v]
        return carry

    lax.fori_loop(0, nk // 128, one, 0)


def first_kernel(ids_ref, *refs):
    ins, ha_ref, hb_ref = refs[:7], refs[7], refs[8]
    out_ref, a_ref, b_ref, no_ref, ni_ref = refs[9:]

    def run(layer_a, layer_b):
        finish_all(ids_ref, ins, out_ref, {layer_a: ha_ref, layer_b: hb_ref})
        pack_layers(out_ref, a_ref, b_ref, layer_a, layer_b)

    by_parity(ids_ref, run)
    pack_rows(ids_ref, out_ref, no_ref, ni_ref)


def surface_kernel(ids_ref, *refs):
    ins, ha_ref, hb_ref, w_ref, sens_ref = refs[:7], *refs[7:11]
    nt, nv, ni, nj, nk = ins[0].shape

    def row_of(side, layers):
        j = side * (nj - 8)
        mask = lax.broadcasted_iota(jnp.int32, (8, 128), 0) == side * 7
        values = []
        for i in range(ni):
            for k in range(0, nk, 128):
                new = finish_tile(side == 1, ins, layers[i], i, j, slice(k, k + 128))
                total = jnp.zeros((8, 128), F32)
                for t in range(nt):
                    for v in range(nv):
                        at = t * nv + v
                        weight = w_ref[at : at + 1, i * nk + k : i * nk + k + 128]
                        total = total + new[t][v] * weight
                values.append(
                    jnp.sum(jnp.where(mask, total, 0.0), axis=0, keepdims=True)
                )
        sens_ref[...] = jnp.concatenate(values, axis=0)

    def run(layer_a, layer_b):
        layers = {layer_a: ha_ref, layer_b: hb_ref}
        for side in range(2):
            pl.when(ids_ref[1] == side)(functools.partial(row_of, side, layers))

    by_parity(ids_ref, run)


def share_kernel(own_ref, other_ref, out_ref, done_ref):
    done_ref[...] = jnp.zeros(done_ref.shape, F32)
    value = own_ref[...] + other_ref[...]
    for member in range(out_ref.shape[0]):
        out_ref[member] = value


def second_kernel(ids_ref, *refs):
    ins, ha_ref, hb_ref, out_ref, done_ref = refs[:7], *refs[7:9], *refs[10:12]
    done_ref[...] = jnp.zeros(done_ref.shape, F32)

    def run(layer_a, layer_b):
        finish_all(ids_ref, ins, out_ref, {layer_a: ha_ref, layer_b: hb_ref})

    by_parity(ids_ref, run)


def split3(x):
    one = x.astype(BF16)
    rest = x - one.astype(F32)
    two = rest.astype(BF16)
    three = (rest - two.astype(F32)).astype(BF16)
    return one, two, three


def one_hot(cells_ref, first, rows):
    cells = cells_ref.shape[1]
    index = lax.broadcasted_iota(jnp.int32, (rows, cells), 0) + first
    return jnp.where(cells_ref[0:1, :] == index, 1.0, 0.0).astype(BF16)


def order_kernel(ids_ref, cells_ref, w_ref, out_ref):
    rows, half = out_ref.shape
    nv, nt, _ = w_ref.shape
    own = one_hot(cells_ref, ids_ref[1] * half, half)
    parts = [part for v in range(nv) for part in split3(w_ref[v])]
    found = lax.dot_general(
        jnp.concatenate(parts, axis=0),
        own,
        (((1,), (1,)), ((), ())),
        preferred_element_type=F32,
    )
    for t in range(nt):
        for v in range(nv):
            one, two, three = (found[(v * 3 + p) * nt + t][None] for p in range(3))
            out_ref[t * nv + v : t * nv + v + 1, :] = one + (two + three)


def mode_table(side, modes, senders):
    row = lax.broadcasted_iota(jnp.int32, (2 * modes, senders), 0)
    sender = lax.broadcasted_iota(jnp.int32, (2 * modes, senders), 1)
    turns = ((row % modes) * (sender // 2)) % PASSAGES
    angle = turns.astype(F32) * (2.0 * math.pi / PASSAGES)
    value = jnp.where(row < modes, jnp.cos(angle), -jnp.sin(angle)) / PASSAGES**0.5
    return jnp.where(sender % 2 == side, value, 0.0)


def tables_kernel(cells_ref, done_ref, chosen_ref, table_ref):
    chosen_ref[...] = one_hot(cells_ref, 0, chosen_ref.shape[0])
    rows, senders = table_ref.shape
    for side in range(2):
        here = slice(side * rows // 2, (side + 1) * rows // 2)
        table_ref[here, :] = mode_table(side, rows // 4, senders)


def modes_kernel(chosen_ref, table_ref, sens_ref, out_ref):
    senders, pieces = sens_ref.shape[:2]
    half = pieces * 128
    rows = out_ref.shape[0]
    seen = jnp.concatenate([sens_ref[:, c, :] for c in range(pieces)], axis=1)
    both = jnp.dot(
        table_ref[...],
        seen,
        precision=lax.Precision.HIGHEST,
        preferred_element_type=F32,
    )
    modes = jnp.concatenate([both[:rows], both[rows:]], axis=1)
    found = jnp.dot(
        jnp.concatenate(split3(modes), axis=0),
        chosen_ref[...],
        preferred_element_type=F32,
    )
    out_ref[...] = found[:rows] + (found[rows : 2 * rows] + found[2 * rows :])


def body(start, source, jac, sigma, damping, cells, weights):
    nt, nv, ni, nj, nk = start.shape
    ring = lax.axis_size("passage")
    n_cell = lax.axis_size("cell")
    ids = jnp.stack([lax.axis_index("cell") & 1, lax.axis_index("passage") & 1])
    even = [(c, c ^ 1) for c in range(n_cell)]
    odd = [(c, c + 1) for c in range(1, n_cell - 1, 2)]
    odd += [(b, a) for a, b in odd]
    within = [(d, d ^ 1) for d in range(ring)]
    across = [(d, (d + 1) % ring) for d in range(1, ring, 2)]
    across += [(b, a) for a, b in across]
    swap = [(0, 1), (1, 0)]

    field_like = jax.ShapeDtypeStruct(start.shape, F32)
    layer_like = jax.ShapeDtypeStruct((nt, nv, nj, nk), BF16)
    rows_like = jax.ShapeDtypeStruct((nt * nv * ni, nk), F32)

    sends = [layer_like, layer_like, rows_like, rows_like]

    def exchange(a, b, outer, inner):
        with jax.named_scope("halos"):
            return (
                lax.ppermute(outer, "passage", across),
                lax.ppermute(inner, "passage", within),
                lax.ppermute(a, "cell", even),
                lax.ppermute(b, "cell", odd),
            )

    packed = call(
        prepare_kernel, sends, (ids, start), [SMEM, VMEM], 4, 10**6, "prepare"
    )
    with jax.named_scope("other_times"):
        pa = lax.ppermute(packed[0], "tm", swap)
        pb = lax.ppermute(packed[1], "tm", swap)
    halos = exchange(*packed)
    rhs = call(
        rhs_kernel,
        [field_like],
        (ids, start, source, pa, pb),
        [SMEM] + [VMEM] * 4,
        4,
        10**7,
        "rhs",
    )[0]
    ordered = call(
        order_kernel,
        [jax.ShapeDtypeStruct((nt * nv, ni * nk), F32)],
        (ids, cells, weights.transpose(1, 0, 2)),
        [SMEM, VMEM, VMEM],
        8,
        10**6,
        "order",
    )[0]
    def local(field, outs, name):
        args = (field, rhs, jac, sigma, damping)
        return call(local_kernel, outs, args, [VMEM] * 5, 4, 2 * 10**7, name)

    slices = [
        jax.ShapeDtypeStruct((nv, nv, nj, nk), BF16),
        jax.ShapeDtypeStruct((nv, nv, ni, 16, nk), BF16),
    ]
    part, jac_i, jac_j = local(start, [field_like] + slices, "first_local")

    def finish(kernel, outs, part, halos, more, name):
        outer, inner, ha, hb = halos
        args = (ids, part, jac_i, jac_j, sigma, damping, outer, inner, ha, hb, *more)
        specs = [SMEM] + [VMEM] * (len(args) - 1)
        return call(kernel, outs, args, specs, 4, 10**7, name)

    field, *packed = finish(
        first_kernel,
        [field_like] + sends,
        part,
        halos,
        (),
        "first_finish",
    )
    halos = exchange(*packed)
    part = local(field, [field_like], "second_local")[0]
    token_like = jax.ShapeDtypeStruct((8, 128), F32)
    pieces = ni * nk // 128
    sens_like = jax.ShapeDtypeStruct((pieces, 128), F32)
    sens = finish(surface_kernel, [sens_like], part, halos, (ordered,), "surface")[0]
    with jax.named_scope("share_sensitivities"):
        other = lax.ppermute(sens, "tm", swap)
        sens, done = call(
            share_kernel,
            [jax.ShapeDtypeStruct((ring, pieces, 128), F32), token_like],
            (sens, other),
            [VMEM] * 2,
            4,
            10**4,
            "share",
        )
        gathered = lax.all_to_all(sens, "passage", 0, 0, tiled=True)
    field, done = finish(
        second_kernel, [field_like, token_like], part, halos, (done,), "second_finish"
    )
    chosen, table = call(
        tables_kernel,
        [
            jax.ShapeDtypeStruct((cells.shape[1], cells.shape[1]), BF16),
            jax.ShapeDtypeStruct((4 * PASSAGES, ring), F32),
        ],
        (cells, done),
        [VMEM] * 2,
        8,
        10**6,
        "tables",
    )
    modes = call(
        modes_kernel,
        [jax.ShapeDtypeStruct((2 * PASSAGES, cells.shape[1]), F32)],
        (chosen, table, gathered),
        [VMEM] * 3,
        8,
        10**7,
        "modes",
    )[0]
    return field, modes.reshape(2, PASSAGES, -1)


def solution(mesh):
    in_specs = (
        P("tm", None, "cell", "passage", None),
        P("tm", None, "cell", "passage", None),
        P(None, None, None, "cell", "passage", None),
        P("cell", "passage", None),
        P("cell", "passage", None),
        P("cell", None),
        P("tm", None, "cell"),
    )
    out_specs = (P("tm", None, "cell", "passage", None), P(None, None, "cell"))
    return jax.shard_map(
        body, mesh=mesh, in_specs=in_specs, out_specs=out_specs, check_vma=False
    )
```

```python
import functools
import math

import jax
import jax.numpy as jnp
from jax import lax
from jax.experimental import pallas as pl
from jax.experimental.pallas import tpu as pltpu
from jax.sharding import PartitionSpec as P

PASSAGES = 16
NT = 8
F32 = jnp.float32
BF16 = jnp.bfloat16
VMEM = pl.BlockSpec(memory_space=pltpu.VMEM)
ANY = pl.BlockSpec(memory_space=pl.ANY)
SMEM = pl.BlockSpec(memory_space=pltpu.SMEM)


def derivative(offset):
    offset = offset % NT
    if offset in (0, NT // 2):
        return 0.0
    angle = math.pi * offset / NT
    return 0.5 * (-1) ** offset * math.cos(angle) / math.sin(angle)


def call(kernel, outs, args, specs, mib, flops, name, scratch=()):
    nbytes = sum(a.size * a.dtype.itemsize for a in args) + sum(
        math.prod(o.shape) * o.dtype.itemsize for o in outs
    )
    return pl.pallas_call(
        kernel,
        out_shape=outs,
        in_specs=specs,
        out_specs=[VMEM] * len(outs),
        scratch_shapes=scratch,
        compiler_params=pltpu.CompilerParams(vmem_limit_bytes=mib << 20),
        cost_estimate=pl.CostEstimate(
            flops=flops, bytes_accessed=nbytes, transcendentals=0
        ),
        name=name,
    )(*args)


def by_parity(ids_ref, run):
    @pl.when(ids_ref[0] == 0)
    def _():
        run(1, 0)

    @pl.when(ids_ref[0] != 0)
    def _():
        run(0, 1)


def edge_row(ids_ref, f_ref, t, v, i, outer):
    nj = f_ref.shape[3]
    low, high = f_ref[t, v, i, 0:1, :], f_ref[t, v, i, nj - 1 : nj, :]
    first = ids_ref[1] == (0 if outer else 1)
    return jnp.where(first, low, high)


def pack_layers(f_ref, a_ref, b_ref, layer_a, layer_b):
    nt, nv = f_ref.shape[:2]
    for t in range(nt):
        for v in range(nv):
            a_ref[t, v] = f_ref[t, v, layer_a].astype(BF16)
            b_ref[t, v] = f_ref[t, v, layer_b].astype(BF16)


def pack_rows(ids_ref, f_ref, outer_ref, inner_ref):
    nt, nv, ni = f_ref.shape[:3]
    for t in range(nt):
        for v in range(nv):
            for i in range(ni):
                row = (t * nv + v) * ni + i
                here = slice(row, row + 1)
                outer_ref[here, :] = edge_row(ids_ref, f_ref, t, v, i, True)
                inner_ref[here, :] = edge_row(ids_ref, f_ref, t, v, i, False)


def prepare_kernel(ids_ref, from_ref, a_ref, b_ref, outer_ref, inner_ref, f_ref, loads):
    nt, nv = f_ref.shape[:2]
    load = [
        pltpu.make_async_copy(from_ref.at[t], f_ref.at[t], loads.at[t])
        for t in range(nt)
    ]
    for copy in load:
        copy.start()
    for t in range(nt):
        load[t].wait()

        def run(layer_a, layer_b):
            for v in range(nv):
                a_ref[t, v] = f_ref[t, v, layer_a].astype(BF16)
                b_ref[t, v] = f_ref[t, v, layer_b].astype(BF16)

        by_parity(ids_ref, run)
    pack_rows(ids_ref, f_ref, outer_ref, inner_ref)


def rhs_kernel(f_ref, from_src_ref, from_far_ref, out_ref, src_ref, far_ref, loads):
    nt, nv, ni, nj, nk = f_ref.shape
    load = [
        [
            pltpu.make_async_copy(come.at[:, v], ref.at[:, v], loads.at[2 * v + at])
            for at, (come, ref) in enumerate(
                ((from_src_ref, src_ref), (from_far_ref, far_ref))
            )
        ]
        for v in range(nv)
    ]
    for pair in load:
        for copy in pair:
            copy.start()
    for v in range(nv):
        for copy in load[v]:
            copy.wait()

        def one(i, carry):
            for j in range(0, nj, 16):
                rows = slice(j, j + 16)
                times = [
                    ref[t, v, i, rows, :].astype(BF16).astype(F32)
                    for ref in (f_ref, far_ref)
                    for t in range(nt)
                ]
                for b in range(nt):
                    total = src_ref[b, v, i, rows, :]
                    for n in range(1, NT // 2):
                        diff = times[(b + n) % NT] - times[(b - n) % NT]
                        total = total - derivative(n) * diff
                    out_ref[b, v, i, rows, :] = total
            return carry

        lax.fori_loop(0, ni, one, 0)


def shifted(f_ref, t, u, i, j, lanes, rows_id):
    nj = f_ref.shape[3]
    here = f_ref[t, u, i, j : j + 8, lanes]
    after = before = jnp.zeros_like(here)
    if j + 8 < nj:
        after = pltpu.roll(f_ref[t, u, i, j + 8 : j + 16, lanes], 7, 0)
    if j > 0:
        before = pltpu.roll(f_ref[t, u, i, j - 8 : j, lanes], 1, 0)
    plus = jnp.where(rows_id == 7, after, pltpu.roll(here, 7, 0))
    minus = jnp.where(rows_id == 0, before, pltpu.roll(here, 1, 0))
    return here, plus, minus


def local_tile(refs, i, j, lanes):
    f_ref, rhs_ref, jac_ref, sig_ref, dmp_ref = refs
    nt, nv, ni = f_ref.shape[:3]
    pair = slice(j // 16 * 16, j // 16 * 16 + 16)
    half = slice(j % 16, j % 16 + 8)
    sigma = sig_ref[i, j : j + 8, lanes]
    damping = dmp_ref[i, j : j + 8, lanes]
    scaling = 1.0 / (sigma + 4.0 * damping)
    rows_id = lax.broadcasted_iota(jnp.int32, sigma.shape, 0)
    acc = [[None] * nv for _ in range(nt)]
    for u in range(nv):
        jac = [
            [jac_ref[d, u, v, i, pair, lanes].astype(F32)[half] for v in range(nv)]
            for d in range(2)
        ]
        for t in range(nt):
            here, plus_j, minus_j = shifted(f_ref, t, u, i, j, lanes, rows_id)
            inner = f_ref[t, u, 1 - i, j : j + 8, lanes]
            diff_i = here if i else here - inner
            diff_j = here - plus_j
            both = (here + (here - inner)) + (diff_j + (here - minus_j))
            own = sigma * here + damping * both
            for v in range(nv):
                term = jac[0][v] * diff_i + jac[1][v] * diff_j
                if v == u:
                    term = term + own
                acc[t][v] = term if acc[t][v] is None else acc[t][v] + term
    return [
        [
            f_ref[t, v, i, j : j + 8, lanes]
            + (rhs_ref[t, v, i, j : j + 8, lanes] - acc[t][v]) * scaling
            for v in range(nv)
        ]
        for t in range(nt)
    ]


def finish_tile(upper, refs, layer_ref, i, j, lanes):
    part_ref, jac_i_ref, jac_j_ref, sig_ref, dmp_ref, outer_ref, inner_ref = refs
    nt, nv, ni, nj, nk = part_ref.shape
    pair = slice(j // 16 * 16, j // 16 * 16 + 16)
    half = slice(j % 16, j % 16 + 8)
    sigma = sig_ref[i, j : j + 8, lanes]
    damping = dmp_ref[i, j : j + 8, lanes]
    scaling = 1.0 / (sigma + 4.0 * damping)
    damping = damping * scaling
    first, last = j == 0, j == nj - 8
    rows_id = lax.broadcasted_iota(jnp.int32, sigma.shape, 0)
    acc = [[0.0] * nv for _ in range(nt)]

    def edge(t, u, high):
        row = (t * nv + u) * ni + i
        outer = outer_ref[row : row + 1, lanes]
        inner = inner_ref[row : row + 1, lanes]
        value = jnp.where(upper == high, outer, inner)
        mask = rows_id == (7 if high else 0)
        return jnp.where(mask, jnp.broadcast_to(value, sigma.shape), 0.0)

    for u in range(nv):
        jac_i = jac_j = None
        if i > 0:
            jac_i = [
                jac_i_ref[u, v, pair, lanes].astype(F32)[half] * scaling
                for v in range(nv)
            ]
        if last:
            jac_j = [
                jac_j_ref[u, v, i, :, lanes].astype(F32)[8:] * scaling
                for v in range(nv)
            ]
        for t in range(nt):
            layer = layer_ref[t, u, pair, lanes].astype(F32)[half]
            near = layer
            if first:
                near = near + edge(t, u, False)
            if last:
                high = edge(t, u, True)
                near = near + high
            acc[t][u] = acc[t][u] + damping * near
            for v in range(nv):
                if jac_i is not None:
                    acc[t][v] = acc[t][v] + jac_i[v] * layer
                if jac_j is not None:
                    acc[t][v] = acc[t][v] + jac_j[v] * high
    return [
        [part_ref[t, v, i, j : j + 8, lanes] + acc[t][v] for v in range(nv)]
        for t in range(nt)
    ]


def lanes_at(k):
    return pl.ds(pl.multiple_of(k * 128, 128), 128)


def local_kernel(*refs):
    ins, out_ref, slices = refs[:5], refs[5], refs[6:]
    nt, nv, ni, nj, nk = out_ref.shape
    if slices:
        jac_ref, (jac_i_ref, jac_j_ref) = ins[2], slices
        for u in range(nv):
            for v in range(nv):
                jac_i_ref[u, v] = jac_ref[0, u, v, ni - 1]
                for i in range(ni):
                    jac_j_ref[u, v, i] = jac_ref[1, u, v, i, nj - 16 :, :]

    def one(k, carry):
        lanes = lanes_at(k)
        for i in range(ni):
            for j in range(0, nj, 8):
                new = local_tile(ins, i, j, lanes)
                for t in range(nt):
                    for v in range(nv):
                        out_ref[t, v, i, j : j + 8, lanes] = new[t][v]
        return carry

    lax.fori_loop(0, nk // 128, one, 0)


def finish_all(ids_ref, ins, out_ref, layers):
    nt, nv, ni, nj, nk = out_ref.shape
    upper = ids_ref[1] == 1

    def one(k, carry):
        lanes = lanes_at(k)
        for i in range(ni):
            for j in range(0, nj, 8):
                new = finish_tile(upper, ins, layers[i], i, j, lanes)
                for t in range(nt):
                    for v in range(nv):
                        out_ref[t, v, i, j : j + 8, lanes] = new[t][v]
        return carry

    lax.fori_loop(0, nk // 128, one, 0)


def first_kernel(ids_ref, *refs):
    ins, ha_ref, hb_ref = refs[:7], refs[7], refs[8]
    out_ref, a_ref, b_ref, no_ref, ni_ref = refs[9:]

    def run(layer_a, layer_b):
        finish_all(ids_ref, ins, out_ref, {layer_a: ha_ref, layer_b: hb_ref})
        pack_layers(out_ref, a_ref, b_ref, layer_a, layer_b)

    by_parity(ids_ref, run)
    pack_rows(ids_ref, out_ref, no_ref, ni_ref)


def surface_kernel(ids_ref, *refs):
    ins, ha_ref, hb_ref, w_ref, sens_ref = refs[:7], *refs[7:11]
    nt, nv, ni, nj, nk = ins[0].shape

    def row_of(side, layers):
        j = side * (nj - 8)
        mask = lax.broadcasted_iota(jnp.int32, (8, 128), 0) == side * 7
        values = []
        for i in range(ni):
            for k in range(0, nk, 128):
                new = finish_tile(side == 1, ins, layers[i], i, j, slice(k, k + 128))
                total = jnp.zeros((8, 128), F32)
                for t in range(nt):
                    for v in range(nv):
                        at = t * nv + v
                        weight = w_ref[at : at + 1, i * nk + k : i * nk + k + 128]
                        total = total + new[t][v] * weight
                values.append(
                    jnp.sum(jnp.where(mask, total, 0.0), axis=0, keepdims=True)
                )
        sens_ref[...] = jnp.concatenate(values, axis=0)

    def run(layer_a, layer_b):
        layers = {layer_a: ha_ref, layer_b: hb_ref}
        for side in range(2):
            pl.when(ids_ref[1] == side)(functools.partial(row_of, side, layers))

    by_parity(ids_ref, run)


def share_kernel(own_ref, other_ref, out_ref, done_ref):
    done_ref[...] = jnp.zeros(done_ref.shape, F32)
    value = own_ref[...] + other_ref[...]
    for member in range(out_ref.shape[0]):
        out_ref[member] = value


def second_kernel(ids_ref, *refs):
    ins, ha_ref, hb_ref, out_ref, done_ref = refs[:7], *refs[7:9], *refs[10:12]
    done_ref[...] = jnp.zeros(done_ref.shape, F32)

    def run(layer_a, layer_b):
        finish_all(ids_ref, ins, out_ref, {layer_a: ha_ref, layer_b: hb_ref})

    by_parity(ids_ref, run)


def split3(x):
    one = x.astype(BF16)
    rest = x - one.astype(F32)
    two = rest.astype(BF16)
    three = (rest - two.astype(F32)).astype(BF16)
    return one, two, three


def one_hot(cells_ref, first, rows):
    cells = cells_ref.shape[1]
    index = lax.broadcasted_iota(jnp.int32, (rows, cells), 0) + first
    return jnp.where(cells_ref[0:1, :] == index, 1.0, 0.0).astype(BF16)


def order_kernel(ids_ref, cells_ref, w_ref, out_ref):
    rows, half = out_ref.shape
    nv, nt, _ = w_ref.shape
    own = one_hot(cells_ref, ids_ref[1] * half, half)
    parts = [part for v in range(nv) for part in split3(w_ref[v])]
    found = lax.dot_general(
        jnp.concatenate(parts, axis=0),
        own,
        (((1,), (1,)), ((), ())),
        preferred_element_type=F32,
    )
    for t in range(nt):
        for v in range(nv):
            one, two, three = (found[(v * 3 + p) * nt + t][None] for p in range(3))
            out_ref[t * nv + v : t * nv + v + 1, :] = one + (two + three)


def mode_table(side, modes, senders):
    row = lax.broadcasted_iota(jnp.int32, (2 * modes, senders), 0)
    sender = lax.broadcasted_iota(jnp.int32, (2 * modes, senders), 1)
    turns = ((row % modes) * (sender // 2)) % PASSAGES
    angle = turns.astype(F32) * (2.0 * math.pi / PASSAGES)
    value = jnp.where(row < modes, jnp.cos(angle), -jnp.sin(angle)) / PASSAGES**0.5
    return jnp.where(sender % 2 == side, value, 0.0)


def tables_kernel(cells_ref, done_ref, chosen_ref, table_ref):
    chosen_ref[...] = one_hot(cells_ref, 0, chosen_ref.shape[0])
    rows, senders = table_ref.shape
    for side in range(2):
        here = slice(side * rows // 2, (side + 1) * rows // 2)
        table_ref[here, :] = mode_table(side, rows // 4, senders)


def modes_kernel(chosen_ref, table_ref, sens_ref, out_ref):
    senders, pieces = sens_ref.shape[:2]
    half = pieces * 128
    rows = out_ref.shape[0]
    seen = jnp.concatenate([sens_ref[:, c, :] for c in range(pieces)], axis=1)
    both = jnp.dot(
        table_ref[...],
        seen,
        precision=lax.Precision.HIGHEST,
        preferred_element_type=F32,
    )
    modes = jnp.concatenate([both[:rows], both[rows:]], axis=1)
    found = jnp.dot(
        jnp.concatenate(split3(modes), axis=0),
        chosen_ref[...],
        preferred_element_type=F32,
    )
    out_ref[...] = found[:rows] + (found[rows : 2 * rows] + found[2 * rows :])


def body(start, source, jac, sigma, damping, cells, weights):
    nt, nv, ni, nj, nk = start.shape
    ring = lax.axis_size("passage")
    n_cell = lax.axis_size("cell")
    ids = jnp.stack([lax.axis_index("cell") & 1, lax.axis_index("passage") & 1])
    even = [(c, c ^ 1) for c in range(n_cell)]
    odd = [(c, c + 1) for c in range(1, n_cell - 1, 2)]
    odd += [(b, a) for a, b in odd]
    within = [(d, d ^ 1) for d in range(ring)]
    across = [(d, (d + 1) % ring) for d in range(1, ring, 2)]
    across += [(b, a) for a, b in across]
    swap = [(0, 1), (1, 0)]

    field_like = jax.ShapeDtypeStruct(start.shape, F32)
    layer_like = jax.ShapeDtypeStruct((nt, nv, nj, nk), BF16)
    rows_like = jax.ShapeDtypeStruct((nt * nv * ni, nk), F32)

    sends = [layer_like, layer_like, rows_like, rows_like]

    def exchange(a, b, outer, inner):
        with jax.named_scope("halos"):
            return (
                lax.ppermute(outer, "passage", across),
                lax.ppermute(inner, "passage", within),
                lax.ppermute(a, "cell", even),
                lax.ppermute(b, "cell", odd),
            )

    in_hbm = functools.partial(
        pltpu.with_memory_space_constraint, memory_space=pltpu.HBM
    )
    with jax.named_scope("other_times"):
        far = lax.ppermute(start, "tm", swap)
    packed = call(
        prepare_kernel,
        sends,
        (ids, in_hbm(start)),
        [SMEM, ANY],
        8,
        10**6,
        "prepare",
        scratch=[pltpu.VMEM(start.shape, F32), pltpu.SemaphoreType.DMA((nt,))],
    )
    halos = exchange(*packed)
    rhs = call(
        rhs_kernel,
        [field_like],
        (start, in_hbm(source), in_hbm(far)),
        [VMEM, ANY, ANY],
        8,
        10**7,
        "rhs",
        scratch=[
            pltpu.VMEM(start.shape, F32),
            pltpu.VMEM(start.shape, F32),
            pltpu.SemaphoreType.DMA((2 * nv,)),
        ],
    )[0]
    ordered = call(
        order_kernel,
        [jax.ShapeDtypeStruct((nt * nv, ni * nk), F32)],
        (ids, cells, weights.transpose(1, 0, 2)),
        [SMEM, VMEM, VMEM],
        8,
        10**6,
        "order",
    )[0]
    def local(field, outs, name):
        args = (field, rhs, jac, sigma, damping)
        return call(local_kernel, outs, args, [VMEM] * 5, 4, 2 * 10**7, name)

    slices = [
        jax.ShapeDtypeStruct((nv, nv, nj, nk), BF16),
        jax.ShapeDtypeStruct((nv, nv, ni, 16, nk), BF16),
    ]
    part, jac_i, jac_j = local(start, [field_like] + slices, "first_local")

    def finish(kernel, outs, part, halos, more, name):
        outer, inner, ha, hb = halos
        args = (ids, part, jac_i, jac_j, sigma, damping, outer, inner, ha, hb, *more)
        specs = [SMEM] + [VMEM] * (len(args) - 1)
        return call(kernel, outs, args, specs, 4, 10**7, name)

    field, *packed = finish(
        first_kernel,
        [field_like] + sends,
        part,
        halos,
        (),
        "first_finish",
    )
    halos = exchange(*packed)
    part = local(field, [field_like], "second_local")[0]
    token_like = jax.ShapeDtypeStruct((8, 128), F32)
    pieces = ni * nk // 128
    sens_like = jax.ShapeDtypeStruct((pieces, 128), F32)
    sens = finish(surface_kernel, [sens_like], part, halos, (ordered,), "surface")[0]
    with jax.named_scope("share_sensitivities"):
        other = lax.ppermute(sens, "tm", swap)
        sens, done = call(
            share_kernel,
            [jax.ShapeDtypeStruct((ring, pieces, 128), F32), token_like],
            (sens, other),
            [VMEM] * 2,
            4,
            10**4,
            "share",
        )
        gathered = lax.all_to_all(sens, "passage", 0, 0, tiled=True)
    field, done = finish(
        second_kernel, [field_like, token_like], part, halos, (done,), "second_finish"
    )
    chosen, table = call(
        tables_kernel,
        [
            jax.ShapeDtypeStruct((cells.shape[1], cells.shape[1]), BF16),
            jax.ShapeDtypeStruct((4 * PASSAGES, ring), F32),
        ],
        (cells, done),
        [VMEM] * 2,
        8,
        10**6,
        "tables",
    )
    modes = call(
        modes_kernel,
        [jax.ShapeDtypeStruct((2 * PASSAGES, cells.shape[1]), F32)],
        (chosen, table, gathered),
        [VMEM] * 3,
        8,
        10**7,
        "modes",
    )[0]
    return field, modes.reshape(2, PASSAGES, -1)


def solution(mesh):
    in_specs = (
        P("tm", None, "cell", "passage", None),
        P("tm", None, "cell", "passage", None),
        P(None, None, None, "cell", "passage", None),
        P("cell", "passage", None),
        P("cell", "passage", None),
        P("cell", None),
        P("tm", None, "cell"),
    )
    out_specs = (P("tm", None, "cell", "passage", None), P(None, None, "cell"))
    return jax.shard_map(
        body, mesh=mesh, in_specs=in_specs, out_specs=out_specs, check_vma=False
    )
```

```python
import functools
import math

import jax
import jax.numpy as jnp
from jax import lax
from jax.experimental import pallas as pl
from jax.experimental.pallas import tpu as pltpu
from jax.sharding import PartitionSpec as P

PASSAGES = 16
NT = 8
F32 = jnp.float32
BF16 = jnp.bfloat16
VMEM = pl.BlockSpec(memory_space=pltpu.VMEM)
SMEM = pl.BlockSpec(memory_space=pltpu.SMEM)


def derivative(offset):
    offset = offset % NT
    if offset in (0, NT // 2):
        return 0.0
    angle = math.pi * offset / NT
    return 0.5 * (-1) ** offset * math.cos(angle) / math.sin(angle)


def call(kernel, outs, args, specs, mib, flops, name):
    nbytes = sum(a.size * a.dtype.itemsize for a in args) + sum(
        math.prod(o.shape) * o.dtype.itemsize for o in outs
    )
    return pl.pallas_call(
        kernel,
        out_shape=outs,
        in_specs=specs,
        out_specs=[VMEM] * len(outs),
        compiler_params=pltpu.CompilerParams(vmem_limit_bytes=mib << 20),
        cost_estimate=pl.CostEstimate(
            flops=flops, bytes_accessed=nbytes, transcendentals=0
        ),
        name=name,
    )(*args)


def by_parity(ids_ref, run):
    @pl.when(ids_ref[0] == 0)
    def _():
        run(1, 0)

    @pl.when(ids_ref[0] != 0)
    def _():
        run(0, 1)


def edge_row(ids_ref, f_ref, t, v, i, outer):
    nj = f_ref.shape[3]
    low, high = f_ref[t, v, i, 0:1, :], f_ref[t, v, i, nj - 1 : nj, :]
    first = ids_ref[1] == (0 if outer else 1)
    return jnp.where(first, low, high)


def pack_layers(f_ref, a_ref, b_ref, layer_a, layer_b):
    nt, nv = f_ref.shape[:2]
    for t in range(nt):
        for v in range(nv):
            a_ref[t, v] = f_ref[t, v, layer_a].astype(BF16)
            b_ref[t, v] = f_ref[t, v, layer_b].astype(BF16)


def pack_rows(ids_ref, f_ref, outer_ref, inner_ref):
    nt, nv, ni = f_ref.shape[:3]
    for t in range(nt):
        for v in range(nv):
            for i in range(ni):
                row = (t * nv + v) * ni + i
                here = slice(row, row + 1)
                outer_ref[here, :] = edge_row(ids_ref, f_ref, t, v, i, True)
                inner_ref[here, :] = edge_row(ids_ref, f_ref, t, v, i, False)


def prepare_kernel(ids_ref, f_ref, a_ref, b_ref, outer_ref, inner_ref):
    pack_rows(ids_ref, f_ref, outer_ref, inner_ref)
    by_parity(ids_ref, functools.partial(pack_layers, f_ref, a_ref, b_ref))


def rhs_kernel(ids_ref, f_ref, src_ref, pa_ref, pb_ref, out_ref):
    nt, nv, ni, nj, nk = f_ref.shape

    def run(layer_a, layer_b):
        for layer, other in ((layer_a, pa_ref), (layer_b, pb_ref)):

            def one(v, carry):
                for j in range(0, nj, 16):
                    rows = slice(j, j + 16)
                    own = [
                        f_ref[t, v, layer, rows, :].astype(BF16).astype(F32)
                        for t in range(nt)
                    ]
                    far = [other[t, v, rows, :].astype(F32) for t in range(nt)]
                    times = own + far
                    for b in range(nt):
                        total = src_ref[b, v, layer, rows, :]
                        for n in range(1, NT // 2):
                            diff = times[(b + n) % NT] - times[(b - n) % NT]
                            total = total - derivative(n) * diff
                        out_ref[b, v, layer, rows, :] = total
                return carry

            lax.fori_loop(0, nv, one, 0)

    by_parity(ids_ref, run)


def shifted(f_ref, t, u, i, j, lanes, rows_id):
    nj = f_ref.shape[3]
    here = f_ref[t, u, i, j : j + 8, lanes]
    after = before = jnp.zeros_like(here)
    if j + 8 < nj:
        after = pltpu.roll(f_ref[t, u, i, j + 8 : j + 16, lanes], 7, 0)
    if j > 0:
        before = pltpu.roll(f_ref[t, u, i, j - 8 : j, lanes], 1, 0)
    plus = jnp.where(rows_id == 7, after, pltpu.roll(here, 7, 0))
    minus = jnp.where(rows_id == 0, before, pltpu.roll(here, 1, 0))
    return here, plus, minus


def local_tile(refs, i, j, lanes):
    f_ref, rhs_ref, jac_ref, sig_ref, dmp_ref = refs
    nt, nv, ni = f_ref.shape[:3]
    pair = slice(j // 16 * 16, j // 16 * 16 + 16)
    half = slice(j % 16, j % 16 + 8)
    sigma = sig_ref[i, j : j + 8, lanes]
    damping = dmp_ref[i, j : j + 8, lanes]
    scaling = 1.0 / (sigma + 4.0 * damping)
    rows_id = lax.broadcasted_iota(jnp.int32, sigma.shape, 0)
    acc = [[None] * nv for _ in range(nt)]
    for u in range(nv):
        jac = [
            [jac_ref[d, u, v, i, pair, lanes].astype(F32)[half] for v in range(nv)]
            for d in range(2)
        ]
        for t in range(nt):
            here, plus_j, minus_j = shifted(f_ref, t, u, i, j, lanes, rows_id)
            inner = f_ref[t, u, 1 - i, j : j + 8, lanes]
            diff_i = here if i else here - inner
            diff_j = here - plus_j
            both = (here + (here - inner)) + (diff_j + (here - minus_j))
            own = sigma * here + damping * both
            for v in range(nv):
                term = jac[0][v] * diff_i + jac[1][v] * diff_j
                if v == u:
                    term = term + own
                acc[t][v] = term if acc[t][v] is None else acc[t][v] + term
    return [
        [
            f_ref[t, v, i, j : j + 8, lanes]
            + (rhs_ref[t, v, i, j : j + 8, lanes] - acc[t][v]) * scaling
            for v in range(nv)
        ]
        for t in range(nt)
    ]


def finish_tile(upper, refs, layer_ref, i, j, lanes):
    part_ref, jac_i_ref, jac_j_ref, sig_ref, dmp_ref, outer_ref, inner_ref = refs
    nt, nv, ni, nj, nk = part_ref.shape
    pair = slice(j // 16 * 16, j // 16 * 16 + 16)
    half = slice(j % 16, j % 16 + 8)
    sigma = sig_ref[i, j : j + 8, lanes]
    damping = dmp_ref[i, j : j + 8, lanes]
    scaling = 1.0 / (sigma + 4.0 * damping)
    damping = damping * scaling
    first, last = j == 0, j == nj - 8
    rows_id = lax.broadcasted_iota(jnp.int32, sigma.shape, 0)
    acc = [[0.0] * nv for _ in range(nt)]

    def edge(t, u, high):
        row = (t * nv + u) * ni + i
        outer = outer_ref[row : row + 1, lanes]
        inner = inner_ref[row : row + 1, lanes]
        value = jnp.where(upper == high, outer, inner)
        mask = rows_id == (7 if high else 0)
        return jnp.where(mask, jnp.broadcast_to(value, sigma.shape), 0.0)

    for u in range(nv):
        jac_i = jac_j = None
        if i > 0:
            jac_i = [
                jac_i_ref[u, v, pair, lanes].astype(F32)[half] * scaling
                for v in range(nv)
            ]
        if last:
            jac_j = [
                jac_j_ref[u, v, i, :, lanes].astype(F32)[8:] * scaling
                for v in range(nv)
            ]
        for t in range(nt):
            layer = layer_ref[t, u, pair, lanes].astype(F32)[half]
            near = layer
            if first:
                near = near + edge(t, u, False)
            if last:
                high = edge(t, u, True)
                near = near + high
            acc[t][u] = acc[t][u] + damping * near
            for v in range(nv):
                if jac_i is not None:
                    acc[t][v] = acc[t][v] + jac_i[v] * layer
                if jac_j is not None:
                    acc[t][v] = acc[t][v] + jac_j[v] * high
    return [
        [part_ref[t, v, i, j : j + 8, lanes] + acc[t][v] for v in range(nv)]
        for t in range(nt)
    ]


def lanes_at(k):
    return pl.ds(pl.multiple_of(k * 128, 128), 128)


def local_kernel(*refs):
    ins, out_ref, slices = refs[:5], refs[5], refs[6:]
    nt, nv, ni, nj, nk = out_ref.shape
    if slices:
        jac_ref, (jac_i_ref, jac_j_ref) = ins[2], slices
        for u in range(nv):
            for v in range(nv):
                jac_i_ref[u, v] = jac_ref[0, u, v, ni - 1]
                for i in range(ni):
                    jac_j_ref[u, v, i] = jac_ref[1, u, v, i, nj - 16 :, :]

    def one(k, carry):
        lanes = lanes_at(k)
        for i in range(ni):
            for j in range(0, nj, 8):
                new = local_tile(ins, i, j, lanes)
                for t in range(nt):
                    for v in range(nv):
                        out_ref[t, v, i, j : j + 8, lanes] = new[t][v]
        return carry

    lax.fori_loop(0, nk // 128, one, 0)


def finish_all(ids_ref, ins, out_ref, layers):
    nt, nv, ni, nj, nk = out_ref.shape
    upper = ids_ref[1] == 1

    def one(k, carry):
        lanes = lanes_at(k)
        for i in range(ni):
            for j in range(0, nj, 8):
                new = finish_tile(upper, ins, layers[i], i, j, lanes)
                for t in range(nt):
                    for v in range(nv):
                        out_ref[t, v, i, j : j + 8, lanes] = new[t][v]
        return carry

    lax.fori_loop(0, nk // 128, one, 0)


def first_kernel(ids_ref, *refs):
    ins, ha_ref, hb_ref = refs[:7], refs[7], refs[8]
    out_ref, a_ref, b_ref, no_ref, ni_ref = refs[9:]

    def run(layer_a, layer_b):
        finish_all(ids_ref, ins, out_ref, {layer_a: ha_ref, layer_b: hb_ref})
        pack_layers(out_ref, a_ref, b_ref, layer_a, layer_b)

    by_parity(ids_ref, run)
    pack_rows(ids_ref, out_ref, no_ref, ni_ref)


def surface_kernel(ids_ref, *refs):
    ins, ha_ref, hb_ref, w_ref, sens_ref = refs[:7], *refs[7:11]
    nt, nv, ni, nj, nk = ins[0].shape

    def row_of(side, layers):
        j = side * (nj - 8)
        mask = lax.broadcasted_iota(jnp.int32, (8, 128), 0) == side * 7
        values = []
        for i in range(ni):
            for k in range(0, nk, 128):
                new = finish_tile(side == 1, ins, layers[i], i, j, slice(k, k + 128))
                total = jnp.zeros((8, 128), F32)
                for t in range(nt):
                    for v in range(nv):
                        at = t * nv + v
                        weight = w_ref[at : at + 1, i * nk + k : i * nk + k + 128]
                        total = total + new[t][v] * weight
                values.append(
                    jnp.sum(jnp.where(mask, total, 0.0), axis=0, keepdims=True)
                )
        sens_ref[...] = jnp.concatenate(values, axis=0)

    def run(layer_a, layer_b):
        layers = {layer_a: ha_ref, layer_b: hb_ref}
        for side in range(2):
            pl.when(ids_ref[1] == side)(functools.partial(row_of, side, layers))

    by_parity(ids_ref, run)


def share_kernel(own_ref, other_ref, out_ref, done_ref):
    done_ref[...] = jnp.zeros(done_ref.shape, F32)
    value = own_ref[...] + other_ref[...]
    for member in range(out_ref.shape[0]):
        out_ref[member] = value


def second_kernel(ids_ref, *refs):
    ins, ha_ref, hb_ref, out_ref, done_ref = refs[:7], *refs[7:9], *refs[10:12]
    done_ref[...] = jnp.zeros(done_ref.shape, F32)

    def run(layer_a, layer_b):
        finish_all(ids_ref, ins, out_ref, {layer_a: ha_ref, layer_b: hb_ref})

    by_parity(ids_ref, run)


def split3(x):
    one = x.astype(BF16)
    rest = x - one.astype(F32)
    two = rest.astype(BF16)
    three = (rest - two.astype(F32)).astype(BF16)
    return one, two, three


def one_hot(cells_ref, first, rows):
    cells = cells_ref.shape[1]
    index = lax.broadcasted_iota(jnp.int32, (rows, cells), 0) + first
    return jnp.where(cells_ref[0:1, :] == index, 1.0, 0.0).astype(BF16)


def order_kernel(ids_ref, cells_ref, w_ref, out_ref):
    rows, half = out_ref.shape
    nv, nt, _ = w_ref.shape
    own = one_hot(cells_ref, ids_ref[1] * half, half)
    parts = [part for v in range(nv) for part in split3(w_ref[v])]
    found = lax.dot_general(
        jnp.concatenate(parts, axis=0),
        own,
        (((1,), (1,)), ((), ())),
        preferred_element_type=F32,
    )
    for t in range(nt):
        for v in range(nv):
            one, two, three = (found[(v * 3 + p) * nt + t][None] for p in range(3))
            out_ref[t * nv + v : t * nv + v + 1, :] = one + (two + three)


def mode_table(side, modes, senders):
    row = lax.broadcasted_iota(jnp.int32, (2 * modes, senders), 0)
    sender = lax.broadcasted_iota(jnp.int32, (2 * modes, senders), 1)
    turns = ((row % modes) * (sender // 2)) % PASSAGES
    angle = turns.astype(F32) * (2.0 * math.pi / PASSAGES)
    value = jnp.where(row < modes, jnp.cos(angle), -jnp.sin(angle)) / PASSAGES**0.5
    return jnp.where(sender % 2 == side, value, 0.0)


def tables_kernel(cells_ref, done_ref, chosen_ref, table_ref):
    chosen_ref[...] = one_hot(cells_ref, 0, chosen_ref.shape[0])
    rows, senders = table_ref.shape
    for side in range(2):
        here = slice(side * rows // 2, (side + 1) * rows // 2)
        table_ref[here, :] = mode_table(side, rows // 4, senders)


def modes_kernel(chosen_ref, table_ref, sens_ref, out_ref):
    senders, pieces = sens_ref.shape[:2]
    half = pieces * 128
    rows = out_ref.shape[0]
    seen = jnp.concatenate([sens_ref[:, c, :] for c in range(pieces)], axis=1)
    both = jnp.dot(
        table_ref[...],
        seen,
        precision=lax.Precision.HIGHEST,
        preferred_element_type=F32,
    )
    modes = jnp.concatenate([both[:rows], both[rows:]], axis=1)
    found = jnp.dot(
        jnp.concatenate(split3(modes), axis=0),
        chosen_ref[...],
        preferred_element_type=F32,
    )
    out_ref[...] = found[:rows] + (found[rows : 2 * rows] + found[2 * rows :])


def body(start, source, jac, sigma, damping, cells, weights):
    nt, nv, ni, nj, nk = start.shape
    ring = lax.axis_size("passage")
    n_cell = lax.axis_size("cell")
    parity = 1 - (lax.axis_index("cell") & 1)
    ids = jnp.stack([parity, lax.axis_index("passage") & 1])
    even = [(c, c ^ 1) for c in range(n_cell)]
    odd = [(c, c + 1) for c in range(1, n_cell - 1, 2)]
    odd += [(b, a) for a, b in odd]
    within = [(d, d ^ 1) for d in range(ring)]
    across = [(d, (d + 1) % ring) for d in range(1, ring, 2)]
    across += [(b, a) for a, b in across]
    swap = [(0, 1), (1, 0)]

    field_like = jax.ShapeDtypeStruct(start.shape, F32)
    layer_like = jax.ShapeDtypeStruct((nt, nv, nj, nk), BF16)
    rows_like = jax.ShapeDtypeStruct((nt * nv * ni, nk), F32)

    sends = [layer_like, layer_like, rows_like, rows_like]

    def exchange(a, b, outer, inner):
        with jax.named_scope("halos"):
            return (
                lax.ppermute(outer, "passage", across),
                lax.ppermute(inner, "passage", within),
                lax.ppermute(a, "cell", odd),
                lax.ppermute(b, "cell", even),
            )

    packed = call(
        prepare_kernel, sends, (ids, start), [SMEM, VMEM], 4, 10**6, "prepare"
    )
    with jax.named_scope("other_times"):
        pa = lax.ppermute(packed[0], "tm", swap)
        pb = lax.ppermute(packed[1], "tm", swap)
    halos = exchange(*packed)
    rhs = call(
        rhs_kernel,
        [field_like],
        (ids, start, source, pa, pb),
        [SMEM] + [VMEM] * 4,
        4,
        10**7,
        "rhs",
    )[0]
    ordered = call(
        order_kernel,
        [jax.ShapeDtypeStruct((nt * nv, ni * nk), F32)],
        (ids, cells, weights.transpose(1, 0, 2)),
        [SMEM, VMEM, VMEM],
        8,
        10**6,
        "order",
    )[0]
    def local(field, outs, name):
        args = (field, rhs, jac, sigma, damping)
        return call(local_kernel, outs, args, [VMEM] * 5, 4, 2 * 10**7, name)

    slices = [
        jax.ShapeDtypeStruct((nv, nv, nj, nk), BF16),
        jax.ShapeDtypeStruct((nv, nv, ni, 16, nk), BF16),
    ]
    part, jac_i, jac_j = local(start, [field_like] + slices, "first_local")

    def finish(kernel, outs, part, halos, more, name):
        outer, inner, ha, hb = halos
        args = (ids, part, jac_i, jac_j, sigma, damping, outer, inner, ha, hb, *more)
        specs = [SMEM] + [VMEM] * (len(args) - 1)
        return call(kernel, outs, args, specs, 4, 10**7, name)

    field, *packed = finish(
        first_kernel,
        [field_like] + sends,
        part,
        halos,
        (),
        "first_finish",
    )
    halos = exchange(*packed)
    part = local(field, [field_like], "second_local")[0]
    token_like = jax.ShapeDtypeStruct((8, 128), F32)
    pieces = ni * nk // 128
    sens_like = jax.ShapeDtypeStruct((pieces, 128), F32)
    sens = finish(surface_kernel, [sens_like], part, halos, (ordered,), "surface")[0]
    with jax.named_scope("share_sensitivities"):
        other = lax.ppermute(sens, "tm", swap)
        sens, done = call(
            share_kernel,
            [jax.ShapeDtypeStruct((ring, pieces, 128), F32), token_like],
            (sens, other),
            [VMEM] * 2,
            4,
            10**4,
            "share",
        )
        gathered = lax.all_to_all(sens, "passage", 0, 0, tiled=True)
    field, done = finish(
        second_kernel, [field_like, token_like], part, halos, (done,), "second_finish"
    )
    chosen, table = call(
        tables_kernel,
        [
            jax.ShapeDtypeStruct((cells.shape[1], cells.shape[1]), BF16),
            jax.ShapeDtypeStruct((4 * PASSAGES, ring), F32),
        ],
        (cells, done),
        [VMEM] * 2,
        8,
        10**6,
        "tables",
    )
    modes = call(
        modes_kernel,
        [jax.ShapeDtypeStruct((2 * PASSAGES, cells.shape[1]), F32)],
        (chosen, table, gathered),
        [VMEM] * 3,
        8,
        10**7,
        "modes",
    )[0]
    return field, modes.reshape(2, PASSAGES, -1)


def solution(mesh):
    in_specs = (
        P("tm", None, "cell", "passage", None),
        P("tm", None, "cell", "passage", None),
        P(None, None, None, "cell", "passage", None),
        P("cell", "passage", None),
        P("cell", "passage", None),
        P("cell", None),
        P("tm", None, "cell"),
    )
    out_specs = (P("tm", None, "cell", "passage", None), P(None, None, "cell"))
    return jax.shard_map(
        body, mesh=mesh, in_specs=in_specs, out_specs=out_specs, check_vma=False
    )
```

```python
import functools
import math

import jax
import jax.numpy as jnp
from jax import lax
from jax.experimental import pallas as pl
from jax.experimental.pallas import tpu as pltpu
from jax.sharding import PartitionSpec as P

PASSAGES = 16
NT = 8
F32 = jnp.float32
BF16 = jnp.bfloat16
VMEM = pl.BlockSpec(memory_space=pltpu.VMEM)
SMEM = pl.BlockSpec(memory_space=pltpu.SMEM)


def derivative(offset):
    offset = offset % NT
    if offset in (0, NT // 2):
        return 0.0
    angle = math.pi * offset / NT
    return 0.5 * (-1) ** offset * math.cos(angle) / math.sin(angle)


def call(kernel, outs, args, specs, mib, flops, name, scratch=()):
    nbytes = sum(a.size * a.dtype.itemsize for a in args) + sum(
        math.prod(o.shape) * o.dtype.itemsize for o in outs
    )
    return pl.pallas_call(
        kernel,
        out_shape=outs,
        in_specs=specs,
        out_specs=[VMEM] * len(outs),
        scratch_shapes=scratch,
        compiler_params=pltpu.CompilerParams(vmem_limit_bytes=mib << 20),
        cost_estimate=pl.CostEstimate(
            flops=flops, bytes_accessed=nbytes, transcendentals=0
        ),
        name=name,
    )(*args)


def by_parity(ids_ref, run):
    @pl.when(ids_ref[0] == 0)
    def _():
        run(1, 0)

    @pl.when(ids_ref[0] != 0)
    def _():
        run(0, 1)


def edge_row(ids_ref, f_ref, t, v, i, outer):
    nj = f_ref.shape[3]
    low, high = f_ref[t, v, i, 0:1, :], f_ref[t, v, i, nj - 1 : nj, :]
    first = ids_ref[1] == (0 if outer else 1)
    return jnp.where(first, low, high)


def pack_layers(f_ref, a_ref, b_ref, layer_a, layer_b):
    nt, nv = f_ref.shape[:2]
    for t in range(nt):
        for v in range(nv):
            a_ref[t, v] = f_ref[t, v, layer_a].astype(BF16)
            b_ref[t, v] = f_ref[t, v, layer_b].astype(BF16)


def pack_rows(ids_ref, f_ref, outer_ref, inner_ref):
    nt, nv, ni = f_ref.shape[:3]
    for t in range(nt):
        for v in range(nv):
            for i in range(ni):
                row = (t * nv + v) * ni + i
                here = slice(row, row + 1)
                outer_ref[here, :] = edge_row(ids_ref, f_ref, t, v, i, True)
                inner_ref[here, :] = edge_row(ids_ref, f_ref, t, v, i, False)


def prepare_kernel(ids_ref, from_ref, f_ref, a_ref, b_ref, outer_ref, inner_ref, loads):
    nt, nv = f_ref.shape[:2]
    pieces = [(t, slice(*v)) for t in range(nt) for v in ((0, 2), (2, nv))]
    load = [
        pltpu.make_async_copy(from_ref.at[t, vs], f_ref.at[t, vs], loads.at[n])
        for n, (t, vs) in enumerate(pieces)
    ]
    for copy in load:
        copy.start()
    for copy, (t, vs) in zip(load, pieces):
        copy.wait()

        def run(layer_a, layer_b):
            for v in range(vs.start, vs.stop):
                a_ref[t, v] = f_ref[t, v, layer_a].astype(BF16)
                b_ref[t, v] = f_ref[t, v, layer_b].astype(BF16)

        by_parity(ids_ref, run)
    pack_rows(ids_ref, f_ref, outer_ref, inner_ref)


def rhs_kernel(ids_ref, f_ref, src_ref, pa_ref, pb_ref, out_ref):
    nt, nv, ni, nj, nk = f_ref.shape

    def run(layer_a, layer_b):
        for layer, other in ((layer_a, pa_ref), (layer_b, pb_ref)):

            def one(v, carry):
                for j in range(0, nj, 16):
                    rows = slice(j, j + 16)
                    own = [
                        f_ref[t, v, layer, rows, :].astype(BF16).astype(F32)
                        for t in range(nt)
                    ]
                    far = [other[t, v, rows, :].astype(F32) for t in range(nt)]
                    times = own + far
                    for b in range(nt):
                        total = src_ref[b, v, layer, rows, :]
                        for n in range(1, NT // 2):
                            diff = times[(b + n) % NT] - times[(b - n) % NT]
                            total = total - derivative(n) * diff
                        out_ref[b, v, layer, rows, :] = total
                return carry

            lax.fori_loop(0, nv, one, 0)

    by_parity(ids_ref, run)


def shifted(f_ref, t, u, i, j, lanes, rows_id):
    nj = f_ref.shape[3]
    here = f_ref[t, u, i, j : j + 8, lanes]
    after = before = jnp.zeros_like(here)
    if j + 8 < nj:
        after = pltpu.roll(f_ref[t, u, i, j + 8 : j + 16, lanes], 7, 0)
    if j > 0:
        before = pltpu.roll(f_ref[t, u, i, j - 8 : j, lanes], 1, 0)
    plus = jnp.where(rows_id == 7, after, pltpu.roll(here, 7, 0))
    minus = jnp.where(rows_id == 0, before, pltpu.roll(here, 1, 0))
    return here, plus, minus


def local_tile(refs, i, j, lanes):
    f_ref, rhs_ref, jac_ref, sig_ref, dmp_ref = refs
    nt, nv, ni = f_ref.shape[:3]
    pair = slice(j // 16 * 16, j // 16 * 16 + 16)
    half = slice(j % 16, j % 16 + 8)
    sigma = sig_ref[i, j : j + 8, lanes]
    damping = dmp_ref[i, j : j + 8, lanes]
    scaling = 1.0 / (sigma + 4.0 * damping)
    rows_id = lax.broadcasted_iota(jnp.int32, sigma.shape, 0)
    acc = [[None] * nv for _ in range(nt)]
    for u in range(nv):
        jac = [
            [jac_ref[d, u, v, i, pair, lanes].astype(F32)[half] for v in range(nv)]
            for d in range(2)
        ]
        for t in range(nt):
            here, plus_j, minus_j = shifted(f_ref, t, u, i, j, lanes, rows_id)
            inner = f_ref[t, u, 1 - i, j : j + 8, lanes]
            diff_i = here if i else here - inner
            diff_j = here - plus_j
            both = (here + (here - inner)) + (diff_j + (here - minus_j))
            own = sigma * here + damping * both
            for v in range(nv):
                term = jac[0][v] * diff_i + jac[1][v] * diff_j
                if v == u:
                    term = term + own
                acc[t][v] = term if acc[t][v] is None else acc[t][v] + term
    return [
        [
            f_ref[t, v, i, j : j + 8, lanes]
            + (rhs_ref[t, v, i, j : j + 8, lanes] - acc[t][v]) * scaling
            for v in range(nv)
        ]
        for t in range(nt)
    ]


def finish_tile(upper, refs, layer_ref, i, j, lanes):
    part_ref, jac_i_ref, jac_j_ref, sig_ref, dmp_ref, outer_ref, inner_ref = refs
    nt, nv, ni, nj, nk = part_ref.shape
    pair = slice(j // 16 * 16, j // 16 * 16 + 16)
    half = slice(j % 16, j % 16 + 8)
    sigma = sig_ref[i, j : j + 8, lanes]
    damping = dmp_ref[i, j : j + 8, lanes]
    scaling = 1.0 / (sigma + 4.0 * damping)
    damping = damping * scaling
    first, last = j == 0, j == nj - 8
    rows_id = lax.broadcasted_iota(jnp.int32, sigma.shape, 0)
    acc = [[0.0] * nv for _ in range(nt)]

    def edge(t, u, high):
        row = (t * nv + u) * ni + i
        outer = outer_ref[row : row + 1, lanes]
        inner = inner_ref[row : row + 1, lanes]
        value = jnp.where(upper == high, outer, inner)
        mask = rows_id == (7 if high else 0)
        return jnp.where(mask, jnp.broadcast_to(value, sigma.shape), 0.0)

    for u in range(nv):
        jac_i = jac_j = None
        if i > 0:
            jac_i = [
                jac_i_ref[u, v, pair, lanes].astype(F32)[half] * scaling
                for v in range(nv)
            ]
        if last:
            jac_j = [
                jac_j_ref[u, v, i, :, lanes].astype(F32)[8:] * scaling
                for v in range(nv)
            ]
        for t in range(nt):
            layer = layer_ref[t, u, pair, lanes].astype(F32)[half]
            near = layer
            if first:
                near = near + edge(t, u, False)
            if last:
                high = edge(t, u, True)
                near = near + high
            acc[t][u] = acc[t][u] + damping * near
            for v in range(nv):
                if jac_i is not None:
                    acc[t][v] = acc[t][v] + jac_i[v] * layer
                if jac_j is not None:
                    acc[t][v] = acc[t][v] + jac_j[v] * high
    return [
        [part_ref[t, v, i, j : j + 8, lanes] + acc[t][v] for v in range(nv)]
        for t in range(nt)
    ]


def lanes_at(k):
    return pl.ds(pl.multiple_of(k * 128, 128), 128)


def local_kernel(*refs):
    ins, out_ref, slices = refs[:5], refs[5], refs[6:]
    nt, nv, ni, nj, nk = out_ref.shape
    if slices:
        jac_ref, (jac_i_ref, jac_j_ref) = ins[2], slices
        for u in range(nv):
            for v in range(nv):
                jac_i_ref[u, v] = jac_ref[0, u, v, ni - 1]
                for i in range(ni):
                    jac_j_ref[u, v, i] = jac_ref[1, u, v, i, nj - 16 :, :]

    def one(k, carry):
        lanes = lanes_at(k)
        for i in range(ni):
            for j in range(0, nj, 8):
                new = local_tile(ins, i, j, lanes)
                for t in range(nt):
                    for v in range(nv):
                        out_ref[t, v, i, j : j + 8, lanes] = new[t][v]
        return carry

    lax.fori_loop(0, nk // 128, one, 0)


def finish_all(ids_ref, ins, out_ref, layers):
    nt, nv, ni, nj, nk = out_ref.shape
    upper = ids_ref[1] == 1

    def one(k, carry):
        lanes = lanes_at(k)
        for i in range(ni):
            for j in range(0, nj, 8):
                new = finish_tile(upper, ins, layers[i], i, j, lanes)
                for t in range(nt):
                    for v in range(nv):
                        out_ref[t, v, i, j : j + 8, lanes] = new[t][v]
        return carry

    lax.fori_loop(0, nk // 128, one, 0)


def first_kernel(ids_ref, *refs):
    ins, ha_ref, hb_ref = refs[:7], refs[7], refs[8]
    out_ref, a_ref, b_ref, no_ref, ni_ref = refs[9:]

    def run(layer_a, layer_b):
        finish_all(ids_ref, ins, out_ref, {layer_a: ha_ref, layer_b: hb_ref})
        pack_layers(out_ref, a_ref, b_ref, layer_a, layer_b)

    by_parity(ids_ref, run)
    pack_rows(ids_ref, out_ref, no_ref, ni_ref)


def surface_kernel(ids_ref, *refs):
    ins, ha_ref, hb_ref, w_ref, sens_ref = refs[:7], *refs[7:11]
    nt, nv, ni, nj, nk = ins[0].shape

    def row_of(side, layers):
        j = side * (nj - 8)
        mask = lax.broadcasted_iota(jnp.int32, (8, 128), 0) == side * 7
        values = []
        for i in range(ni):
            for k in range(0, nk, 128):
                new = finish_tile(side == 1, ins, layers[i], i, j, slice(k, k + 128))
                total = jnp.zeros((8, 128), F32)
                for t in range(nt):
                    for v in range(nv):
                        at = t * nv + v
                        weight = w_ref[at : at + 1, i * nk + k : i * nk + k + 128]
                        total = total + new[t][v] * weight
                values.append(
                    jnp.sum(jnp.where(mask, total, 0.0), axis=0, keepdims=True)
                )
        sens_ref[...] = jnp.concatenate(values, axis=0)

    def run(layer_a, layer_b):
        layers = {layer_a: ha_ref, layer_b: hb_ref}
        for side in range(2):
            pl.when(ids_ref[1] == side)(functools.partial(row_of, side, layers))

    by_parity(ids_ref, run)


def share_kernel(own_ref, other_ref, out_ref, done_ref):
    done_ref[...] = jnp.zeros(done_ref.shape, F32)
    value = own_ref[...] + other_ref[...]
    for member in range(out_ref.shape[0]):
        out_ref[member] = value


def second_kernel(ids_ref, *refs):
    ins, ha_ref, hb_ref, out_ref, done_ref = refs[:7], *refs[7:9], *refs[10:12]
    done_ref[...] = jnp.zeros(done_ref.shape, F32)

    def run(layer_a, layer_b):
        finish_all(ids_ref, ins, out_ref, {layer_a: ha_ref, layer_b: hb_ref})

    by_parity(ids_ref, run)


def split3(x):
    one = x.astype(BF16)
    rest = x - one.astype(F32)
    two = rest.astype(BF16)
    three = (rest - two.astype(F32)).astype(BF16)
    return one, two, three


def one_hot(cells_ref, first, rows):
    cells = cells_ref.shape[1]
    index = lax.broadcasted_iota(jnp.int32, (rows, cells), 0) + first
    return jnp.where(cells_ref[0:1, :] == index, 1.0, 0.0).astype(BF16)


def order_kernel(ids_ref, cells_ref, w_ref, out_ref):
    rows, half = out_ref.shape
    nv, nt, _ = w_ref.shape
    own = one_hot(cells_ref, ids_ref[1] * half, half)
    parts = [part for v in range(nv) for part in split3(w_ref[v])]
    found = lax.dot_general(
        jnp.concatenate(parts, axis=0),
        own,
        (((1,), (1,)), ((), ())),
        preferred_element_type=F32,
    )
    for t in range(nt):
        for v in range(nv):
            one, two, three = (found[(v * 3 + p) * nt + t][None] for p in range(3))
            out_ref[t * nv + v : t * nv + v + 1, :] = one + (two + three)


def mode_table(side, modes, senders):
    row = lax.broadcasted_iota(jnp.int32, (2 * modes, senders), 0)
    sender = lax.broadcasted_iota(jnp.int32, (2 * modes, senders), 1)
    turns = ((row % modes) * (sender // 2)) % PASSAGES
    angle = turns.astype(F32) * (2.0 * math.pi / PASSAGES)
    value = jnp.where(row < modes, jnp.cos(angle), -jnp.sin(angle)) / PASSAGES**0.5
    return jnp.where(sender % 2 == side, value, 0.0)


def tables_kernel(cells_ref, done_ref, chosen_ref, table_ref):
    chosen_ref[...] = one_hot(cells_ref, 0, chosen_ref.shape[0])
    rows, senders = table_ref.shape
    for side in range(2):
        here = slice(side * rows // 2, (side + 1) * rows // 2)
        table_ref[here, :] = mode_table(side, rows // 4, senders)


def modes_kernel(chosen_ref, table_ref, sens_ref, out_ref):
    senders, pieces = sens_ref.shape[:2]
    half = pieces * 128
    rows = out_ref.shape[0]
    seen = jnp.concatenate([sens_ref[:, c, :] for c in range(pieces)], axis=1)
    both = jnp.dot(
        table_ref[...],
        seen,
        precision=lax.Precision.HIGHEST,
        preferred_element_type=F32,
    )
    modes = jnp.concatenate([both[:rows], both[rows:]], axis=1)
    found = jnp.dot(
        jnp.concatenate(split3(modes), axis=0),
        chosen_ref[...],
        preferred_element_type=F32,
    )
    out_ref[...] = found[:rows] + (found[rows : 2 * rows] + found[2 * rows :])


def body(start, source, jac, sigma, damping, cells, weights):
    nt, nv, ni, nj, nk = start.shape
    ring = lax.axis_size("passage")
    n_cell = lax.axis_size("cell")
    ids = jnp.stack([lax.axis_index("cell") & 1, lax.axis_index("passage") & 1])
    even = [(c, c ^ 1) for c in range(n_cell)]
    odd = [(c, c + 1) for c in range(1, n_cell - 1, 2)]
    odd += [(b, a) for a, b in odd]
    within = [(d, d ^ 1) for d in range(ring)]
    across = [(d, (d + 1) % ring) for d in range(1, ring, 2)]
    across += [(b, a) for a, b in across]
    swap = [(0, 1), (1, 0)]

    field_like = jax.ShapeDtypeStruct(start.shape, F32)
    layer_like = jax.ShapeDtypeStruct((nt, nv, nj, nk), BF16)
    rows_like = jax.ShapeDtypeStruct((nt * nv * ni, nk), F32)

    sends = [layer_like, layer_like, rows_like, rows_like]

    def exchange(a, b, outer, inner):
        with jax.named_scope("halos"):
            return (
                lax.ppermute(outer, "passage", across),
                lax.ppermute(inner, "passage", within),
                lax.ppermute(a, "cell", even),
                lax.ppermute(b, "cell", odd),
            )

    start, *packed = call(
        prepare_kernel,
        [field_like] + sends,
        (ids, pltpu.with_memory_space_constraint(start, pltpu.HBM)),
        [SMEM, pl.BlockSpec(memory_space=pl.ANY)],
        8,
        10**6,
        "prepare",
        scratch=[pltpu.SemaphoreType.DMA((2 * nt,))],
    )
    with jax.named_scope("other_times"):
        pa = lax.ppermute(packed[0], "tm", swap)
        pb = lax.ppermute(packed[1], "tm", swap)
    halos = exchange(*packed)
    rhs = call(
        rhs_kernel,
        [field_like],
        (ids, start, source, pa, pb),
        [SMEM] + [VMEM] * 4,
        4,
        10**7,
        "rhs",
    )[0]
    ordered = call(
        order_kernel,
        [jax.ShapeDtypeStruct((nt * nv, ni * nk), F32)],
        (ids, cells, weights.transpose(1, 0, 2)),
        [SMEM, VMEM, VMEM],
        8,
        10**6,
        "order",
    )[0]
    def local(field, outs, name):
        args = (field, rhs, jac, sigma, damping)
        return call(local_kernel, outs, args, [VMEM] * 5, 4, 2 * 10**7, name)

    slices = [
        jax.ShapeDtypeStruct((nv, nv, nj, nk), BF16),
        jax.ShapeDtypeStruct((nv, nv, ni, 16, nk), BF16),
    ]
    part, jac_i, jac_j = local(start, [field_like] + slices, "first_local")

    def finish(kernel, outs, part, halos, more, name):
        outer, inner, ha, hb = halos
        args = (ids, part, jac_i, jac_j, sigma, damping, outer, inner, ha, hb, *more)
        specs = [SMEM] + [VMEM] * (len(args) - 1)
        return call(kernel, outs, args, specs, 4, 10**7, name)

    field, *packed = finish(
        first_kernel,
        [field_like] + sends,
        part,
        halos,
        (),
        "first_finish",
    )
    halos = exchange(*packed)
    part = local(field, [field_like], "second_local")[0]
    token_like = jax.ShapeDtypeStruct((8, 128), F32)
    pieces = ni * nk // 128
    sens_like = jax.ShapeDtypeStruct((pieces, 128), F32)
    sens = finish(surface_kernel, [sens_like], part, halos, (ordered,), "surface")[0]
    with jax.named_scope("share_sensitivities"):
        other = lax.ppermute(sens, "tm", swap)
        sens, done = call(
            share_kernel,
            [jax.ShapeDtypeStruct((ring, pieces, 128), F32), token_like],
            (sens, other),
            [VMEM] * 2,
            4,
            10**4,
            "share",
        )
        gathered = lax.all_to_all(sens, "passage", 0, 0, tiled=True)
    field, done = finish(
        second_kernel, [field_like, token_like], part, halos, (done,), "second_finish"
    )
    chosen, table = call(
        tables_kernel,
        [
            jax.ShapeDtypeStruct((cells.shape[1], cells.shape[1]), BF16),
            jax.ShapeDtypeStruct((4 * PASSAGES, ring), F32),
        ],
        (cells, done),
        [VMEM] * 2,
        8,
        10**6,
        "tables",
    )
    modes = call(
        modes_kernel,
        [jax.ShapeDtypeStruct((2 * PASSAGES, cells.shape[1]), F32)],
        (chosen, table, gathered),
        [VMEM] * 3,
        8,
        10**7,
        "modes",
    )[0]
    return field, modes.reshape(2, PASSAGES, -1)


def solution(mesh):
    in_specs = (
        P("tm", None, "cell", "passage", None),
        P("tm", None, "cell", "passage", None),
        P(None, None, None, "cell", "passage", None),
        P("cell", "passage", None),
        P("cell", "passage", None),
        P("cell", None),
        P("tm", None, "cell"),
    )
    out_specs = (P("tm", None, "cell", "passage", None), P(None, None, "cell"))
    return jax.shard_map(
        body, mesh=mesh, in_specs=in_specs, out_specs=out_specs, check_vma=False
    )
```

```python
import functools
import math

import jax
import jax.numpy as jnp
from jax import lax
from jax.experimental import pallas as pl
from jax.experimental.pallas import tpu as pltpu
from jax.sharding import PartitionSpec as P

PASSAGES = 16
NT = 8
F32 = jnp.float32
BF16 = jnp.bfloat16
VMEM = pl.BlockSpec(memory_space=pltpu.VMEM)
ANY = pl.BlockSpec(memory_space=pl.ANY)
SMEM = pl.BlockSpec(memory_space=pltpu.SMEM)


def derivative(offset):
    offset = offset % NT
    if offset in (0, NT // 2):
        return 0.0
    angle = math.pi * offset / NT
    return 0.5 * (-1) ** offset * math.cos(angle) / math.sin(angle)


def call(kernel, outs, args, specs, mib, flops, name, scratch=()):
    nbytes = sum(a.size * a.dtype.itemsize for a in args) + sum(
        math.prod(o.shape) * o.dtype.itemsize for o in outs
    )
    return pl.pallas_call(
        kernel,
        out_shape=outs,
        in_specs=specs,
        out_specs=[VMEM] * len(outs),
        scratch_shapes=scratch,
        compiler_params=pltpu.CompilerParams(vmem_limit_bytes=mib << 20),
        cost_estimate=pl.CostEstimate(
            flops=flops, bytes_accessed=nbytes, transcendentals=0
        ),
        name=name,
    )(*args)


def by_parity(ids_ref, run):
    @pl.when(ids_ref[0] == 0)
    def _():
        run(1, 0)

    @pl.when(ids_ref[0] != 0)
    def _():
        run(0, 1)


def edge_row(ids_ref, f_ref, t, v, i, outer):
    nj = f_ref.shape[3]
    low, high = f_ref[t, v, i, 0:1, :], f_ref[t, v, i, nj - 1 : nj, :]
    first = ids_ref[1] == (0 if outer else 1)
    return jnp.where(first, low, high)


def pack_layers(f_ref, a_ref, b_ref, layer_a, layer_b):
    nt, nv = f_ref.shape[:2]
    for t in range(nt):
        for v in range(nv):
            a_ref[t, v] = f_ref[t, v, layer_a].astype(BF16)
            b_ref[t, v] = f_ref[t, v, layer_b].astype(BF16)


def pack_rows(ids_ref, f_ref, outer_ref, inner_ref):
    nt, nv, ni = f_ref.shape[:3]
    for t in range(nt):
        for v in range(nv):
            for i in range(ni):
                row = (t * nv + v) * ni + i
                here = slice(row, row + 1)
                outer_ref[here, :] = edge_row(ids_ref, f_ref, t, v, i, True)
                inner_ref[here, :] = edge_row(ids_ref, f_ref, t, v, i, False)


def prepare_kernel(ids_ref, from_ref, f_ref, a_ref, b_ref, outer_ref, inner_ref, loads):
    nt, nv = f_ref.shape[:2]
    pieces = [(t, slice(*v)) for t in range(nt) for v in ((0, 2), (2, nv))]
    load = [
        pltpu.make_async_copy(from_ref.at[t, vs], f_ref.at[t, vs], loads.at[n])
        for n, (t, vs) in enumerate(pieces)
    ]
    for copy in load:
        copy.start()
    for copy, (t, vs) in zip(load, pieces):
        copy.wait()

        def run(layer_a, layer_b):
            for v in range(vs.start, vs.stop):
                a_ref[t, v] = f_ref[t, v, layer_a].astype(BF16)
                b_ref[t, v] = f_ref[t, v, layer_b].astype(BF16)

        by_parity(ids_ref, run)
    pack_rows(ids_ref, f_ref, outer_ref, inner_ref)


def rhs_kernel(ids_ref, f_ref, from_ref, pa_ref, pb_ref, out_ref, src_ref, loads):
    nt, nv, ni, nj, nk = f_ref.shape
    load = [
        pltpu.make_async_copy(from_ref.at[:, v], src_ref.at[:, v], loads.at[v])
        for v in range(nv)
    ]
    for copy in load:
        copy.start()

    def run(v, layer_a, layer_b):
        for layer, other in ((layer_a, pa_ref), (layer_b, pb_ref)):
            for j in range(0, nj, 16):
                rows = slice(j, j + 16)
                own = [
                    f_ref[t, v, layer, rows, :].astype(BF16).astype(F32)
                    for t in range(nt)
                ]
                far = [other[t, v, rows, :].astype(F32) for t in range(nt)]
                times = own + far
                for b in range(nt):
                    total = src_ref[b, v, layer, rows, :]
                    for n in range(1, NT // 2):
                        diff = times[(b + n) % NT] - times[(b - n) % NT]
                        total = total - derivative(n) * diff
                    out_ref[b, v, layer, rows, :] = total

    for v in range(nv):
        load[v].wait()
        by_parity(ids_ref, functools.partial(run, v))


def shifted(f_ref, t, u, i, j, lanes, rows_id):
    nj = f_ref.shape[3]
    here = f_ref[t, u, i, j : j + 8, lanes]
    after = before = jnp.zeros_like(here)
    if j + 8 < nj:
        after = pltpu.roll(f_ref[t, u, i, j + 8 : j + 16, lanes], 7, 0)
    if j > 0:
        before = pltpu.roll(f_ref[t, u, i, j - 8 : j, lanes], 1, 0)
    plus = jnp.where(rows_id == 7, after, pltpu.roll(here, 7, 0))
    minus = jnp.where(rows_id == 0, before, pltpu.roll(here, 1, 0))
    return here, plus, minus


def local_tile(refs, i, j, lanes):
    f_ref, rhs_ref, jac_ref, sig_ref, dmp_ref = refs
    nt, nv, ni = f_ref.shape[:3]
    pair = slice(j // 16 * 16, j // 16 * 16 + 16)
    half = slice(j % 16, j % 16 + 8)
    sigma = sig_ref[i, j : j + 8, lanes]
    damping = dmp_ref[i, j : j + 8, lanes]
    scaling = 1.0 / (sigma + 4.0 * damping)
    rows_id = lax.broadcasted_iota(jnp.int32, sigma.shape, 0)
    acc = [[None] * nv for _ in range(nt)]
    for u in range(nv):
        jac = [
            [jac_ref[d, u, v, i, pair, lanes].astype(F32)[half] for v in range(nv)]
            for d in range(2)
        ]
        for t in range(nt):
            here, plus_j, minus_j = shifted(f_ref, t, u, i, j, lanes, rows_id)
            inner = f_ref[t, u, 1 - i, j : j + 8, lanes]
            diff_i = here if i else here - inner
            diff_j = here - plus_j
            both = (here + (here - inner)) + (diff_j + (here - minus_j))
            own = sigma * here + damping * both
            for v in range(nv):
                term = jac[0][v] * diff_i + jac[1][v] * diff_j
                if v == u:
                    term = term + own
                acc[t][v] = term if acc[t][v] is None else acc[t][v] + term
    return [
        [
            f_ref[t, v, i, j : j + 8, lanes]
            + (rhs_ref[t, v, i, j : j + 8, lanes] - acc[t][v]) * scaling
            for v in range(nv)
        ]
        for t in range(nt)
    ]


def finish_tile(upper, refs, layer_ref, i, j, lanes):
    part_ref, jac_i_ref, jac_j_ref, sig_ref, dmp_ref, outer_ref, inner_ref = refs
    nt, nv, ni, nj, nk = part_ref.shape
    pair = slice(j // 16 * 16, j // 16 * 16 + 16)
    half = slice(j % 16, j % 16 + 8)
    sigma = sig_ref[i, j : j + 8, lanes]
    damping = dmp_ref[i, j : j + 8, lanes]
    scaling = 1.0 / (sigma + 4.0 * damping)
    damping = damping * scaling
    first, last = j == 0, j == nj - 8
    rows_id = lax.broadcasted_iota(jnp.int32, sigma.shape, 0)
    acc = [[0.0] * nv for _ in range(nt)]

    def edge(t, u, high):
        row = (t * nv + u) * ni + i
        outer = outer_ref[row : row + 1, lanes]
        inner = inner_ref[row : row + 1, lanes]
        value = jnp.where(upper == high, outer, inner)
        mask = rows_id == (7 if high else 0)
        return jnp.where(mask, jnp.broadcast_to(value, sigma.shape), 0.0)

    for u in range(nv):
        jac_i = jac_j = None
        if i > 0:
            jac_i = [
                jac_i_ref[u, v, pair, lanes].astype(F32)[half] * scaling
                for v in range(nv)
            ]
        if last:
            jac_j = [
                jac_j_ref[u, v, i, :, lanes].astype(F32)[8:] * scaling
                for v in range(nv)
            ]
        for t in range(nt):
            layer = layer_ref[t, u, pair, lanes].astype(F32)[half]
            near = layer
            if first:
                near = near + edge(t, u, False)
            if last:
                high = edge(t, u, True)
                near = near + high
            acc[t][u] = acc[t][u] + damping * near
            for v in range(nv):
                if jac_i is not None:
                    acc[t][v] = acc[t][v] + jac_i[v] * layer
                if jac_j is not None:
                    acc[t][v] = acc[t][v] + jac_j[v] * high
    return [
        [part_ref[t, v, i, j : j + 8, lanes] + acc[t][v] for v in range(nv)]
        for t in range(nt)
    ]


def lanes_at(k):
    return pl.ds(pl.multiple_of(k * 128, 128), 128)


def local_kernel(*refs):
    ins, out_ref, slices = refs[:5], refs[5], refs[6:]
    nt, nv, ni, nj, nk = out_ref.shape
    if slices:
        jac_ref, (jac_i_ref, jac_j_ref) = ins[2], slices
        for u in range(nv):
            for v in range(nv):
                jac_i_ref[u, v] = jac_ref[0, u, v, ni - 1]
                for i in range(ni):
                    jac_j_ref[u, v, i] = jac_ref[1, u, v, i, nj - 16 :, :]

    def one(k, carry):
        lanes = lanes_at(k)
        for i in range(ni):
            for j in range(0, nj, 8):
                new = local_tile(ins, i, j, lanes)
                for t in range(nt):
                    for v in range(nv):
                        out_ref[t, v, i, j : j + 8, lanes] = new[t][v]
        return carry

    lax.fori_loop(0, nk // 128, one, 0)


def finish_all(ids_ref, ins, out_ref, layers):
    nt, nv, ni, nj, nk = out_ref.shape
    upper = ids_ref[1] == 1

    def one(k, carry):
        lanes = lanes_at(k)
        for i in range(ni):
            for j in range(0, nj, 8):
                new = finish_tile(upper, ins, layers[i], i, j, lanes)
                for t in range(nt):
                    for v in range(nv):
                        out_ref[t, v, i, j : j + 8, lanes] = new[t][v]
        return carry

    lax.fori_loop(0, nk // 128, one, 0)


def first_kernel(ids_ref, *refs):
    ins, ha_ref, hb_ref = refs[:7], refs[7], refs[8]
    out_ref, a_ref, b_ref, no_ref, ni_ref = refs[9:]

    def run(layer_a, layer_b):
        finish_all(ids_ref, ins, out_ref, {layer_a: ha_ref, layer_b: hb_ref})
        pack_layers(out_ref, a_ref, b_ref, layer_a, layer_b)

    by_parity(ids_ref, run)
    pack_rows(ids_ref, out_ref, no_ref, ni_ref)


def surface_kernel(ids_ref, *refs):
    ins, ha_ref, hb_ref, w_ref, sens_ref = refs[:7], *refs[7:11]
    nt, nv, ni, nj, nk = ins[0].shape

    def row_of(side, layers):
        j = side * (nj - 8)
        mask = lax.broadcasted_iota(jnp.int32, (8, 128), 0) == side * 7
        values = []
        for i in range(ni):
            for k in range(0, nk, 128):
                new = finish_tile(side == 1, ins, layers[i], i, j, slice(k, k + 128))
                total = jnp.zeros((8, 128), F32)
                for t in range(nt):
                    for v in range(nv):
                        at = t * nv + v
                        weight = w_ref[at : at + 1, i * nk + k : i * nk + k + 128]
                        total = total + new[t][v] * weight
                values.append(
                    jnp.sum(jnp.where(mask, total, 0.0), axis=0, keepdims=True)
                )
        sens_ref[...] = jnp.concatenate(values, axis=0)

    def run(layer_a, layer_b):
        layers = {layer_a: ha_ref, layer_b: hb_ref}
        for side in range(2):
            pl.when(ids_ref[1] == side)(functools.partial(row_of, side, layers))

    by_parity(ids_ref, run)


def share_kernel(own_ref, other_ref, out_ref, done_ref):
    done_ref[...] = jnp.zeros(done_ref.shape, F32)
    value = own_ref[...] + other_ref[...]
    for member in range(out_ref.shape[0]):
        out_ref[member] = value


def second_kernel(ids_ref, *refs):
    ins, ha_ref, hb_ref, out_ref, done_ref = refs[:7], *refs[7:9], *refs[10:12]
    done_ref[...] = jnp.zeros(done_ref.shape, F32)

    def run(layer_a, layer_b):
        finish_all(ids_ref, ins, out_ref, {layer_a: ha_ref, layer_b: hb_ref})

    by_parity(ids_ref, run)


def split3(x):
    one = x.astype(BF16)
    rest = x - one.astype(F32)
    two = rest.astype(BF16)
    three = (rest - two.astype(F32)).astype(BF16)
    return one, two, three


def one_hot(cells_ref, first, rows):
    cells = cells_ref.shape[1]
    index = lax.broadcasted_iota(jnp.int32, (rows, cells), 0) + first
    return jnp.where(cells_ref[0:1, :] == index, 1.0, 0.0).astype(BF16)


def order_kernel(ids_ref, cells_ref, w_ref, out_ref):
    rows, half = out_ref.shape
    nv, nt, _ = w_ref.shape
    own = one_hot(cells_ref, ids_ref[1] * half, half)
    parts = [part for v in range(nv) for part in split3(w_ref[v])]
    found = lax.dot_general(
        jnp.concatenate(parts, axis=0),
        own,
        (((1,), (1,)), ((), ())),
        preferred_element_type=F32,
    )
    for t in range(nt):
        for v in range(nv):
            one, two, three = (found[(v * 3 + p) * nt + t][None] for p in range(3))
            out_ref[t * nv + v : t * nv + v + 1, :] = one + (two + three)


def mode_table(side, modes, senders):
    row = lax.broadcasted_iota(jnp.int32, (2 * modes, senders), 0)
    sender = lax.broadcasted_iota(jnp.int32, (2 * modes, senders), 1)
    turns = ((row % modes) * (sender // 2)) % PASSAGES
    angle = turns.astype(F32) * (2.0 * math.pi / PASSAGES)
    value = jnp.where(row < modes, jnp.cos(angle), -jnp.sin(angle)) / PASSAGES**0.5
    return jnp.where(sender % 2 == side, value, 0.0)


def tables_kernel(cells_ref, done_ref, chosen_ref, table_ref):
    chosen_ref[...] = one_hot(cells_ref, 0, chosen_ref.shape[0])
    rows, senders = table_ref.shape
    for side in range(2):
        here = slice(side * rows // 2, (side + 1) * rows // 2)
        table_ref[here, :] = mode_table(side, rows // 4, senders)


def modes_kernel(chosen_ref, table_ref, sens_ref, out_ref):
    senders, pieces = sens_ref.shape[:2]
    half = pieces * 128
    rows = out_ref.shape[0]
    seen = jnp.concatenate([sens_ref[:, c, :] for c in range(pieces)], axis=1)
    both = jnp.dot(
        table_ref[...],
        seen,
        precision=lax.Precision.HIGHEST,
        preferred_element_type=F32,
    )
    modes = jnp.concatenate([both[:rows], both[rows:]], axis=1)
    found = jnp.dot(
        jnp.concatenate(split3(modes), axis=0),
        chosen_ref[...],
        preferred_element_type=F32,
    )
    out_ref[...] = found[:rows] + (found[rows : 2 * rows] + found[2 * rows :])


def body(start, source, jac, sigma, damping, cells, weights):
    nt, nv, ni, nj, nk = start.shape
    ring = lax.axis_size("passage")
    n_cell = lax.axis_size("cell")
    ids = jnp.stack([lax.axis_index("cell") & 1, lax.axis_index("passage") & 1])
    even = [(c, c ^ 1) for c in range(n_cell)]
    odd = [(c, c + 1) for c in range(1, n_cell - 1, 2)]
    odd += [(b, a) for a, b in odd]
    within = [(d, d ^ 1) for d in range(ring)]
    across = [(d, (d + 1) % ring) for d in range(1, ring, 2)]
    across += [(b, a) for a, b in across]
    swap = [(0, 1), (1, 0)]

    field_like = jax.ShapeDtypeStruct(start.shape, F32)
    layer_like = jax.ShapeDtypeStruct((nt, nv, nj, nk), BF16)
    rows_like = jax.ShapeDtypeStruct((nt * nv * ni, nk), F32)

    sends = [layer_like, layer_like, rows_like, rows_like]

    def exchange(a, b, outer, inner):
        with jax.named_scope("halos"):
            return (
                lax.ppermute(outer, "passage", across),
                lax.ppermute(inner, "passage", within),
                lax.ppermute(a, "cell", even),
                lax.ppermute(b, "cell", odd),
            )

    in_hbm = functools.partial(
        pltpu.with_memory_space_constraint, memory_space=pltpu.HBM
    )
    start, *packed = call(
        prepare_kernel,
        [field_like] + sends,
        (ids, in_hbm(start)),
        [SMEM, ANY],
        8,
        10**6,
        "prepare",
        scratch=[pltpu.SemaphoreType.DMA((2 * nt,))],
    )
    with jax.named_scope("other_times"):
        pa = lax.ppermute(packed[0], "tm", swap)
        pb = lax.ppermute(packed[1], "tm", swap)
    halos = exchange(*packed)
    rhs = call(
        rhs_kernel,
        [field_like],
        (ids, start, in_hbm(source), pa, pb),
        [SMEM, VMEM, ANY, VMEM, VMEM],
        8,
        10**7,
        "rhs",
        scratch=[pltpu.VMEM(source.shape, F32), pltpu.SemaphoreType.DMA((nv,))],
    )[0]
    ordered = call(
        order_kernel,
        [jax.ShapeDtypeStruct((nt * nv, ni * nk), F32)],
        (ids, cells, weights.transpose(1, 0, 2)),
        [SMEM, VMEM, VMEM],
        8,
        10**6,
        "order",
    )[0]
    def local(field, outs, name):
        args = (field, rhs, jac, sigma, damping)
        return call(local_kernel, outs, args, [VMEM] * 5, 4, 2 * 10**7, name)

    slices = [
        jax.ShapeDtypeStruct((nv, nv, nj, nk), BF16),
        jax.ShapeDtypeStruct((nv, nv, ni, 16, nk), BF16),
    ]
    part, jac_i, jac_j = local(start, [field_like] + slices, "first_local")

    def finish(kernel, outs, part, halos, more, name):
        outer, inner, ha, hb = halos
        args = (ids, part, jac_i, jac_j, sigma, damping, outer, inner, ha, hb, *more)
        specs = [SMEM] + [VMEM] * (len(args) - 1)
        return call(kernel, outs, args, specs, 4, 10**7, name)

    field, *packed = finish(
        first_kernel,
        [field_like] + sends,
        part,
        halos,
        (),
        "first_finish",
    )
    halos = exchange(*packed)
    part = local(field, [field_like], "second_local")[0]
    token_like = jax.ShapeDtypeStruct((8, 128), F32)
    pieces = ni * nk // 128
    sens_like = jax.ShapeDtypeStruct((pieces, 128), F32)
    sens = finish(surface_kernel, [sens_like], part, halos, (ordered,), "surface")[0]
    with jax.named_scope("share_sensitivities"):
        other = lax.ppermute(sens, "tm", swap)
        sens, done = call(
            share_kernel,
            [jax.ShapeDtypeStruct((ring, pieces, 128), F32), token_like],
            (sens, other),
            [VMEM] * 2,
            4,
            10**4,
            "share",
        )
        gathered = lax.all_to_all(sens, "passage", 0, 0, tiled=True)
    field, done = finish(
        second_kernel, [field_like, token_like], part, halos, (done,), "second_finish"
    )
    chosen, table = call(
        tables_kernel,
        [
            jax.ShapeDtypeStruct((cells.shape[1], cells.shape[1]), BF16),
            jax.ShapeDtypeStruct((4 * PASSAGES, ring), F32),
        ],
        (cells, done),
        [VMEM] * 2,
        8,
        10**6,
        "tables",
    )
    modes = call(
        modes_kernel,
        [jax.ShapeDtypeStruct((2 * PASSAGES, cells.shape[1]), F32)],
        (chosen, table, gathered),
        [VMEM] * 3,
        8,
        10**7,
        "modes",
    )[0]
    return field, modes.reshape(2, PASSAGES, -1)


def solution(mesh):
    in_specs = (
        P("tm", None, "cell", "passage", None),
        P("tm", None, "cell", "passage", None),
        P(None, None, None, "cell", "passage", None),
        P("cell", "passage", None),
        P("cell", "passage", None),
        P("cell", None),
        P("tm", None, "cell"),
    )
    out_specs = (P("tm", None, "cell", "passage", None), P(None, None, "cell"))
    return jax.shard_map(
        body, mesh=mesh, in_specs=in_specs, out_specs=out_specs, check_vma=False
    )
```

```python
import functools
import math

import jax
import jax.numpy as jnp
from jax import lax
from jax.experimental import pallas as pl
from jax.experimental.pallas import tpu as pltpu
from jax.sharding import PartitionSpec as P

PASSAGES = 16
NT = 8
F32 = jnp.float32
BF16 = jnp.bfloat16
VMEM = pl.BlockSpec(memory_space=pltpu.VMEM)
SMEM = pl.BlockSpec(memory_space=pltpu.SMEM)


def derivative(offset):
    offset = offset % NT
    if offset in (0, NT // 2):
        return 0.0
    angle = math.pi * offset / NT
    return 0.5 * (-1) ** offset * math.cos(angle) / math.sin(angle)


def call(kernel, outs, args, specs, mib, flops, name):
    nbytes = sum(a.size * a.dtype.itemsize for a in args) + sum(
        math.prod(o.shape) * o.dtype.itemsize for o in outs
    )
    return pl.pallas_call(
        kernel,
        out_shape=outs,
        in_specs=specs,
        out_specs=[VMEM] * len(outs),
        compiler_params=pltpu.CompilerParams(vmem_limit_bytes=mib << 20),
        cost_estimate=pl.CostEstimate(
            flops=flops, bytes_accessed=nbytes, transcendentals=0
        ),
        name=name,
    )(*args)


def by_parity(ids_ref, run):
    @pl.when(ids_ref[0] == 0)
    def _():
        run(1, 0)

    @pl.when(ids_ref[0] != 0)
    def _():
        run(0, 1)


def edge_row(ids_ref, f_ref, t, v, i, outer):
    nj = f_ref.shape[3]
    low, high = f_ref[t, v, i, 0:1, :], f_ref[t, v, i, nj - 1 : nj, :]
    first = ids_ref[1] == (0 if outer else 1)
    return jnp.where(first, low, high)


def pack_layers(f_ref, a_ref, b_ref, layer_a, layer_b):
    nt, nv = f_ref.shape[:2]
    for t in range(nt):
        for v in range(nv):
            a_ref[t, v] = f_ref[t, v, layer_a].astype(BF16)
            b_ref[t, v] = f_ref[t, v, layer_b].astype(BF16)


def pack_rows(ids_ref, f_ref, outer_ref, inner_ref):
    nt, nv, ni = f_ref.shape[:3]
    for t in range(nt):
        for v in range(nv):
            for i in range(ni):
                row = (t * nv + v) * ni + i
                here = slice(row, row + 1)
                outer_ref[here, :] = edge_row(ids_ref, f_ref, t, v, i, True)
                inner_ref[here, :] = edge_row(ids_ref, f_ref, t, v, i, False)


def prepare_kernel(ids_ref, f_ref, a_ref, b_ref):
    by_parity(ids_ref, functools.partial(pack_layers, f_ref, a_ref, b_ref))


def rhs_kernel(ids_ref, f_ref, src_ref, pa_ref, pb_ref, out_ref):
    nt, nv, ni, nj, nk = f_ref.shape

    def run(layer_a, layer_b):
        for layer, other in ((layer_a, pa_ref), (layer_b, pb_ref)):

            def one(v, carry):
                for j in range(0, nj, 16):
                    rows = slice(j, j + 16)
                    own = [
                        f_ref[t, v, layer, rows, :].astype(BF16).astype(F32)
                        for t in range(nt)
                    ]
                    far = [other[t, v, rows, :].astype(F32) for t in range(nt)]
                    times = own + far
                    for b in range(nt):
                        total = src_ref[b, v, layer, rows, :]
                        for n in range(1, NT // 2):
                            diff = times[(b + n) % NT] - times[(b - n) % NT]
                            total = total - derivative(n) * diff
                        out_ref[b, v, layer, rows, :] = total
                return carry

            lax.fori_loop(0, nv, one, 0)

    by_parity(ids_ref, run)


def shifted(f_ref, t, u, i, j, lanes, rows_id):
    nj = f_ref.shape[3]
    here = f_ref[t, u, i, j : j + 8, lanes]
    after = before = jnp.zeros_like(here)
    if j + 8 < nj:
        after = pltpu.roll(f_ref[t, u, i, j + 8 : j + 16, lanes], 7, 0)
    if j > 0:
        before = pltpu.roll(f_ref[t, u, i, j - 8 : j, lanes], 1, 0)
    plus = jnp.where(rows_id == 7, after, pltpu.roll(here, 7, 0))
    minus = jnp.where(rows_id == 0, before, pltpu.roll(here, 1, 0))
    return here, plus, minus


def local_tile(refs, i, j, lanes):
    f_ref, rhs_ref, jac_ref, sig_ref, dmp_ref = refs
    nt, nv, ni = f_ref.shape[:3]
    pair = slice(j // 16 * 16, j // 16 * 16 + 16)
    half = slice(j % 16, j % 16 + 8)
    sigma = sig_ref[i, j : j + 8, lanes]
    damping = dmp_ref[i, j : j + 8, lanes]
    scaling = 1.0 / (sigma + 4.0 * damping)
    rows_id = lax.broadcasted_iota(jnp.int32, sigma.shape, 0)
    acc = [[None] * nv for _ in range(nt)]
    for u in range(nv):
        jac = [
            [jac_ref[d, u, v, i, pair, lanes].astype(F32)[half] for v in range(nv)]
            for d in range(2)
        ]
        for t in range(nt):
            here, plus_j, minus_j = shifted(f_ref, t, u, i, j, lanes, rows_id)
            inner = f_ref[t, u, 1 - i, j : j + 8, lanes]
            diff_i = here if i else here - inner
            diff_j = here - plus_j
            both = (here + (here - inner)) + (diff_j + (here - minus_j))
            own = sigma * here + damping * both
            for v in range(nv):
                term = jac[0][v] * diff_i + jac[1][v] * diff_j
                if v == u:
                    term = term + own
                acc[t][v] = term if acc[t][v] is None else acc[t][v] + term
    return [
        [
            f_ref[t, v, i, j : j + 8, lanes]
            + (rhs_ref[t, v, i, j : j + 8, lanes] - acc[t][v]) * scaling
            for v in range(nv)
        ]
        for t in range(nt)
    ]


def finish_tile(upper, refs, layer_ref, i, j, lanes):
    part_ref, jac_i_ref, jac_j_ref, sig_ref, dmp_ref, outer_ref, inner_ref = refs
    nt, nv, ni, nj, nk = part_ref.shape
    pair = slice(j // 16 * 16, j // 16 * 16 + 16)
    half = slice(j % 16, j % 16 + 8)
    sigma = sig_ref[i, j : j + 8, lanes]
    damping = dmp_ref[i, j : j + 8, lanes]
    scaling = 1.0 / (sigma + 4.0 * damping)
    damping = damping * scaling
    first, last = j == 0, j == nj - 8
    rows_id = lax.broadcasted_iota(jnp.int32, sigma.shape, 0)
    acc = [[0.0] * nv for _ in range(nt)]

    def edge(t, u, high):
        row = (t * nv + u) * ni + i
        outer = outer_ref[row : row + 1, lanes]
        inner = inner_ref[row : row + 1, lanes]
        value = jnp.where(upper == high, outer, inner)
        mask = rows_id == (7 if high else 0)
        return jnp.where(mask, jnp.broadcast_to(value, sigma.shape), 0.0)

    for u in range(nv):
        jac_i = jac_j = None
        if i > 0:
            jac_i = [
                jac_i_ref[u, v, pair, lanes].astype(F32)[half] * scaling
                for v in range(nv)
            ]
        if last:
            jac_j = [
                jac_j_ref[u, v, i, :, lanes].astype(F32)[8:] * scaling
                for v in range(nv)
            ]
        for t in range(nt):
            layer = layer_ref[t, u, pair, lanes].astype(F32)[half]
            near = layer
            if first:
                near = near + edge(t, u, False)
            if last:
                high = edge(t, u, True)
                near = near + high
            acc[t][u] = acc[t][u] + damping * near
            for v in range(nv):
                if jac_i is not None:
                    acc[t][v] = acc[t][v] + jac_i[v] * layer
                if jac_j is not None:
                    acc[t][v] = acc[t][v] + jac_j[v] * high
    return [
        [part_ref[t, v, i, j : j + 8, lanes] + acc[t][v] for v in range(nv)]
        for t in range(nt)
    ]


def lanes_at(k):
    return pl.ds(pl.multiple_of(k * 128, 128), 128)


def local_kernel(*refs):
    ins, out_ref, slices = refs[:5], refs[5], refs[6:]
    nt, nv, ni, nj, nk = out_ref.shape
    if slices:
        jac_ref, (jac_i_ref, jac_j_ref) = ins[2], slices
        for u in range(nv):
            for v in range(nv):
                jac_i_ref[u, v] = jac_ref[0, u, v, ni - 1]
                for i in range(ni):
                    jac_j_ref[u, v, i] = jac_ref[1, u, v, i, nj - 16 :, :]

    def one(k, carry):
        lanes = lanes_at(k)
        for i in range(ni):
            for j in range(0, nj, 8):
                new = local_tile(ins, i, j, lanes)
                for t in range(nt):
                    for v in range(nv):
                        out_ref[t, v, i, j : j + 8, lanes] = new[t][v]
        return carry

    lax.fori_loop(0, nk // 128, one, 0)


def finish_all(ids_ref, ins, out_ref, layers):
    nt, nv, ni, nj, nk = out_ref.shape
    upper = ids_ref[1] == 1

    def one(k, carry):
        lanes = lanes_at(k)
        for i in range(ni):
            for j in range(0, nj, 8):
                new = finish_tile(upper, ins, layers[i], i, j, lanes)
                for t in range(nt):
                    for v in range(nv):
                        out_ref[t, v, i, j : j + 8, lanes] = new[t][v]
        return carry

    lax.fori_loop(0, nk // 128, one, 0)


def first_kernel(ids_ref, *refs):
    ins, ha_ref, hb_ref = refs[:7], refs[7], refs[8]
    out_ref, a_ref, b_ref = refs[9:]

    def run(layer_a, layer_b):
        finish_all(ids_ref, ins, out_ref, {layer_a: ha_ref, layer_b: hb_ref})
        pack_layers(out_ref, a_ref, b_ref, layer_a, layer_b)

    by_parity(ids_ref, run)


def surface_kernel(ids_ref, *refs):
    ins, ha_ref, hb_ref, w_ref, sens_ref = refs[:7], *refs[7:11]
    nt, nv, ni, nj, nk = ins[0].shape

    def row_of(side, layers):
        j = side * (nj - 8)
        mask = lax.broadcasted_iota(jnp.int32, (8, 128), 0) == side * 7
        values = []
        for i in range(ni):
            for k in range(0, nk, 128):
                new = finish_tile(side == 1, ins, layers[i], i, j, slice(k, k + 128))
                total = jnp.zeros((8, 128), F32)
                for t in range(nt):
                    for v in range(nv):
                        at = t * nv + v
                        weight = w_ref[at : at + 1, i * nk + k : i * nk + k + 128]
                        total = total + new[t][v] * weight
                values.append(
                    jnp.sum(jnp.where(mask, total, 0.0), axis=0, keepdims=True)
                )
        sens_ref[...] = jnp.concatenate(values, axis=0)

    def run(layer_a, layer_b):
        layers = {layer_a: ha_ref, layer_b: hb_ref}
        for side in range(2):
            pl.when(ids_ref[1] == side)(functools.partial(row_of, side, layers))

    by_parity(ids_ref, run)


def share_kernel(own_ref, other_ref, out_ref, done_ref):
    done_ref[...] = jnp.zeros(done_ref.shape, F32)
    value = own_ref[...] + other_ref[...]
    for member in range(out_ref.shape[0]):
        out_ref[member] = value


def second_kernel(ids_ref, *refs):
    ins, ha_ref, hb_ref, out_ref, done_ref = refs[:7], *refs[7:9], *refs[10:12]
    done_ref[...] = jnp.zeros(done_ref.shape, F32)

    def run(layer_a, layer_b):
        finish_all(ids_ref, ins, out_ref, {layer_a: ha_ref, layer_b: hb_ref})

    by_parity(ids_ref, run)


def split3(x):
    one = x.astype(BF16)
    rest = x - one.astype(F32)
    two = rest.astype(BF16)
    three = (rest - two.astype(F32)).astype(BF16)
    return one, two, three


def one_hot(cells_ref, first, rows):
    cells = cells_ref.shape[1]
    index = lax.broadcasted_iota(jnp.int32, (rows, cells), 0) + first
    return jnp.where(cells_ref[0:1, :] == index, 1.0, 0.0).astype(BF16)


def order_kernel(ids_ref, cells_ref, w_ref, out_ref):
    rows, half = out_ref.shape
    nv, nt, _ = w_ref.shape
    own = one_hot(cells_ref, ids_ref[1] * half, half)
    parts = [part for v in range(nv) for part in split3(w_ref[v])]
    found = lax.dot_general(
        jnp.concatenate(parts, axis=0),
        own,
        (((1,), (1,)), ((), ())),
        preferred_element_type=F32,
    )
    for t in range(nt):
        for v in range(nv):
            one, two, three = (found[(v * 3 + p) * nt + t][None] for p in range(3))
            out_ref[t * nv + v : t * nv + v + 1, :] = one + (two + three)


def mode_table(side, modes, senders):
    row = lax.broadcasted_iota(jnp.int32, (2 * modes, senders), 0)
    sender = lax.broadcasted_iota(jnp.int32, (2 * modes, senders), 1)
    turns = ((row % modes) * (sender // 2)) % PASSAGES
    angle = turns.astype(F32) * (2.0 * math.pi / PASSAGES)
    value = jnp.where(row < modes, jnp.cos(angle), -jnp.sin(angle)) / PASSAGES**0.5
    return jnp.where(sender % 2 == side, value, 0.0)


def tables_kernel(cells_ref, done_ref, chosen_ref, table_ref):
    chosen_ref[...] = one_hot(cells_ref, 0, chosen_ref.shape[0])
    rows, senders = table_ref.shape
    for side in range(2):
        here = slice(side * rows // 2, (side + 1) * rows // 2)
        table_ref[here, :] = mode_table(side, rows // 4, senders)


def modes_kernel(chosen_ref, table_ref, sens_ref, out_ref):
    senders, pieces = sens_ref.shape[:2]
    half = pieces * 128
    rows = out_ref.shape[0]
    seen = jnp.concatenate([sens_ref[:, c, :] for c in range(pieces)], axis=1)
    both = jnp.dot(
        table_ref[...],
        seen,
        precision=lax.Precision.HIGHEST,
        preferred_element_type=F32,
    )
    modes = jnp.concatenate([both[:rows], both[rows:]], axis=1)
    found = jnp.dot(
        jnp.concatenate(split3(modes), axis=0),
        chosen_ref[...],
        preferred_element_type=F32,
    )
    out_ref[...] = found[:rows] + (found[rows : 2 * rows] + found[2 * rows :])


def body(start, source, jac, sigma, damping, cells, weights):
    nt, nv, ni, nj, nk = start.shape
    ring = lax.axis_size("passage")
    n_cell = lax.axis_size("cell")
    ids = jnp.stack([lax.axis_index("cell") & 1, lax.axis_index("passage") & 1])
    even = [(c, c ^ 1) for c in range(n_cell)]
    odd = [(c, c + 1) for c in range(1, n_cell - 1, 2)]
    odd += [(b, a) for a, b in odd]
    within = [(d, d ^ 1) for d in range(ring)]
    across = [(d, (d + 1) % ring) for d in range(1, ring, 2)]
    across += [(b, a) for a, b in across]
    swap = [(0, 1), (1, 0)]

    field_like = jax.ShapeDtypeStruct(start.shape, F32)
    layer_like = jax.ShapeDtypeStruct((nt, nv, nj, nk), BF16)
    rows_like = jax.ShapeDtypeStruct((nt * nv * ni, nk), F32)

    sends = [layer_like, layer_like]

    def exchange(field, a, b):
        rows = [rows_like, rows_like]
        outer, inner = call(
            pack_rows, rows, (ids, field), [SMEM, VMEM], 4, 10**6, "rows"
        )
        with jax.named_scope("halos"):
            return (
                lax.ppermute(outer, "passage", across),
                lax.ppermute(inner, "passage", within),
                lax.ppermute(a, "cell", even),
                lax.ppermute(b, "cell", odd),
            )

    packed = call(
        prepare_kernel, sends, (ids, start), [SMEM, VMEM], 4, 10**6, "prepare"
    )
    with jax.named_scope("other_times"):
        pa = lax.ppermute(packed[0], "tm", swap)
        pb = lax.ppermute(packed[1], "tm", swap)
    halos = exchange(start, *packed)
    rhs = call(
        rhs_kernel,
        [field_like],
        (ids, start, source, pa, pb),
        [SMEM] + [VMEM] * 4,
        4,
        10**7,
        "rhs",
    )[0]
    ordered = call(
        order_kernel,
        [jax.ShapeDtypeStruct((nt * nv, ni * nk), F32)],
        (ids, cells, weights.transpose(1, 0, 2)),
        [SMEM, VMEM, VMEM],
        8,
        10**6,
        "order",
    )[0]
    def local(field, outs, name):
        args = (field, rhs, jac, sigma, damping)
        return call(local_kernel, outs, args, [VMEM] * 5, 4, 2 * 10**7, name)

    slices = [
        jax.ShapeDtypeStruct((nv, nv, nj, nk), BF16),
        jax.ShapeDtypeStruct((nv, nv, ni, 16, nk), BF16),
    ]
    part, jac_i, jac_j = local(start, [field_like] + slices, "first_local")

    def finish(kernel, outs, part, halos, more, name):
        outer, inner, ha, hb = halos
        args = (ids, part, jac_i, jac_j, sigma, damping, outer, inner, ha, hb, *more)
        specs = [SMEM] + [VMEM] * (len(args) - 1)
        return call(kernel, outs, args, specs, 4, 10**7, name)

    field, *packed = finish(
        first_kernel,
        [field_like] + sends,
        part,
        halos,
        (),
        "first_finish",
    )
    halos = exchange(field, *packed)
    part = local(field, [field_like], "second_local")[0]
    token_like = jax.ShapeDtypeStruct((8, 128), F32)
    pieces = ni * nk // 128
    sens_like = jax.ShapeDtypeStruct((pieces, 128), F32)
    sens = finish(surface_kernel, [sens_like], part, halos, (ordered,), "surface")[0]
    with jax.named_scope("share_sensitivities"):
        other = lax.ppermute(sens, "tm", swap)
        sens, done = call(
            share_kernel,
            [jax.ShapeDtypeStruct((ring, pieces, 128), F32), token_like],
            (sens, other),
            [VMEM] * 2,
            4,
            10**4,
            "share",
        )
        gathered = lax.all_to_all(sens, "passage", 0, 0, tiled=True)
    field, done = finish(
        second_kernel, [field_like, token_like], part, halos, (done,), "second_finish"
    )
    chosen, table = call(
        tables_kernel,
        [
            jax.ShapeDtypeStruct((cells.shape[1], cells.shape[1]), BF16),
            jax.ShapeDtypeStruct((4 * PASSAGES, ring), F32),
        ],
        (cells, done),
        [VMEM] * 2,
        8,
        10**6,
        "tables",
    )
    modes = call(
        modes_kernel,
        [jax.ShapeDtypeStruct((2 * PASSAGES, cells.shape[1]), F32)],
        (chosen, table, gathered),
        [VMEM] * 3,
        8,
        10**7,
        "modes",
    )[0]
    return field, modes.reshape(2, PASSAGES, -1)


def solution(mesh):
    in_specs = (
        P("tm", None, "cell", "passage", None),
        P("tm", None, "cell", "passage", None),
        P(None, None, None, "cell", "passage", None),
        P("cell", "passage", None),
        P("cell", "passage", None),
        P("cell", None),
        P("tm", None, "cell"),
    )
    out_specs = (P("tm", None, "cell", "passage", None), P(None, None, "cell"))
    return jax.shard_map(
        body, mesh=mesh, in_specs=in_specs, out_specs=out_specs, check_vma=False
    )
```

```python
import functools
import math

import jax
import jax.numpy as jnp
from jax import lax
from jax.experimental import pallas as pl
from jax.experimental.pallas import tpu as pltpu
from jax.sharding import PartitionSpec as P

PASSAGES = 16
NT = 8
F32 = jnp.float32
BF16 = jnp.bfloat16
VMEM = pl.BlockSpec(memory_space=pltpu.VMEM)
SMEM = pl.BlockSpec(memory_space=pltpu.SMEM)


def derivative(offset):
    offset = offset % NT
    if offset in (0, NT // 2):
        return 0.0
    angle = math.pi * offset / NT
    return 0.5 * (-1) ** offset * math.cos(angle) / math.sin(angle)


def call(kernel, outs, args, specs, mib, flops, name):
    nbytes = sum(a.size * a.dtype.itemsize for a in args) + sum(
        math.prod(o.shape) * o.dtype.itemsize for o in outs
    )
    return pl.pallas_call(
        kernel,
        out_shape=outs,
        in_specs=specs,
        out_specs=[VMEM] * len(outs),
        compiler_params=pltpu.CompilerParams(vmem_limit_bytes=mib << 20),
        cost_estimate=pl.CostEstimate(
            flops=flops, bytes_accessed=nbytes, transcendentals=0
        ),
        name=name,
    )(*args)


def by_parity(ids_ref, run):
    @pl.when(ids_ref[0] == 0)
    def _():
        run(1, 0)

    @pl.when(ids_ref[0] != 0)
    def _():
        run(0, 1)


def edge_row(ids_ref, f_ref, t, v, i, outer):
    nj = f_ref.shape[3]
    low, high = f_ref[t, v, i, 0:1, :], f_ref[t, v, i, nj - 1 : nj, :]
    first = ids_ref[1] == (0 if outer else 1)
    return jnp.where(first, low, high)


def pack_layers(f_ref, a_ref, b_ref, layer_a, layer_b):
    nt, nv = f_ref.shape[:2]
    for t in range(nt):
        for v in range(nv):
            a_ref[t, v] = f_ref[t, v, layer_a].astype(BF16)
            b_ref[t, v] = f_ref[t, v, layer_b].astype(BF16)


def pack_rows(ids_ref, f_ref, outer_ref, inner_ref):
    nt, nv, ni = f_ref.shape[:3]
    for t in range(nt):
        for v in range(nv):
            for i in range(ni):
                row = (t * nv + v) * ni + i
                here = slice(row, row + 1)
                outer_ref[here, :] = edge_row(ids_ref, f_ref, t, v, i, True)
                inner_ref[here, :] = edge_row(ids_ref, f_ref, t, v, i, False)


def prepare_kernel(ids_ref, f_ref, a_ref, b_ref, both_ref):
    def run(layer_a, layer_b):
        pack_layers(f_ref, a_ref, b_ref, layer_a, layer_b)
        pack_layers(f_ref, both_ref.at[0], both_ref.at[1], layer_a, layer_b)

    by_parity(ids_ref, run)


def rhs_kernel(ids_ref, f_ref, src_ref, far_ref, out_ref):
    pa_ref, pb_ref = far_ref.at[0], far_ref.at[1]
    nt, nv, ni, nj, nk = f_ref.shape

    def run(layer_a, layer_b):
        for layer, other in ((layer_a, pa_ref), (layer_b, pb_ref)):

            def one(v, carry):
                for j in range(0, nj, 16):
                    rows = slice(j, j + 16)
                    own = [
                        f_ref[t, v, layer, rows, :].astype(BF16).astype(F32)
                        for t in range(nt)
                    ]
                    far = [other[t, v, rows, :].astype(F32) for t in range(nt)]
                    times = own + far
                    for b in range(nt):
                        total = src_ref[b, v, layer, rows, :]
                        for n in range(1, NT // 2):
                            diff = times[(b + n) % NT] - times[(b - n) % NT]
                            total = total - derivative(n) * diff
                        out_ref[b, v, layer, rows, :] = total
                return carry

            lax.fori_loop(0, nv, one, 0)

    by_parity(ids_ref, run)


def shifted(f_ref, t, u, i, j, lanes, rows_id):
    nj = f_ref.shape[3]
    here = f_ref[t, u, i, j : j + 8, lanes]
    after = before = jnp.zeros_like(here)
    if j + 8 < nj:
        after = pltpu.roll(f_ref[t, u, i, j + 8 : j + 16, lanes], 7, 0)
    if j > 0:
        before = pltpu.roll(f_ref[t, u, i, j - 8 : j, lanes], 1, 0)
    plus = jnp.where(rows_id == 7, after, pltpu.roll(here, 7, 0))
    minus = jnp.where(rows_id == 0, before, pltpu.roll(here, 1, 0))
    return here, plus, minus


def local_tile(refs, i, j, lanes):
    f_ref, rhs_ref, jac_ref, sig_ref, dmp_ref = refs
    nt, nv, ni = f_ref.shape[:3]
    pair = slice(j // 16 * 16, j // 16 * 16 + 16)
    half = slice(j % 16, j % 16 + 8)
    sigma = sig_ref[i, j : j + 8, lanes]
    damping = dmp_ref[i, j : j + 8, lanes]
    scaling = 1.0 / (sigma + 4.0 * damping)
    rows_id = lax.broadcasted_iota(jnp.int32, sigma.shape, 0)
    acc = [[None] * nv for _ in range(nt)]
    for u in range(nv):
        jac = [
            [jac_ref[d, u, v, i, pair, lanes].astype(F32)[half] for v in range(nv)]
            for d in range(2)
        ]
        for t in range(nt):
            here, plus_j, minus_j = shifted(f_ref, t, u, i, j, lanes, rows_id)
            inner = f_ref[t, u, 1 - i, j : j + 8, lanes]
            diff_i = here if i else here - inner
            diff_j = here - plus_j
            both = (here + (here - inner)) + (diff_j + (here - minus_j))
            own = sigma * here + damping * both
            for v in range(nv):
                term = jac[0][v] * diff_i + jac[1][v] * diff_j
                if v == u:
                    term = term + own
                acc[t][v] = term if acc[t][v] is None else acc[t][v] + term
    return [
        [
            f_ref[t, v, i, j : j + 8, lanes]
            + (rhs_ref[t, v, i, j : j + 8, lanes] - acc[t][v]) * scaling
            for v in range(nv)
        ]
        for t in range(nt)
    ]


def finish_tile(upper, refs, layer_ref, i, j, lanes):
    part_ref, jac_i_ref, jac_j_ref, sig_ref, dmp_ref, outer_ref, inner_ref = refs
    nt, nv, ni, nj, nk = part_ref.shape
    pair = slice(j // 16 * 16, j // 16 * 16 + 16)
    half = slice(j % 16, j % 16 + 8)
    sigma = sig_ref[i, j : j + 8, lanes]
    damping = dmp_ref[i, j : j + 8, lanes]
    scaling = 1.0 / (sigma + 4.0 * damping)
    damping = damping * scaling
    first, last = j == 0, j == nj - 8
    rows_id = lax.broadcasted_iota(jnp.int32, sigma.shape, 0)
    acc = [[0.0] * nv for _ in range(nt)]

    def edge(t, u, high):
        row = (t * nv + u) * ni + i
        outer = outer_ref[row : row + 1, lanes]
        inner = inner_ref[row : row + 1, lanes]
        value = jnp.where(upper == high, outer, inner)
        mask = rows_id == (7 if high else 0)
        return jnp.where(mask, jnp.broadcast_to(value, sigma.shape), 0.0)

    for u in range(nv):
        jac_i = jac_j = None
        if i > 0:
            jac_i = [
                jac_i_ref[u, v, pair, lanes].astype(F32)[half] * scaling
                for v in range(nv)
            ]
        if last:
            jac_j = [
                jac_j_ref[u, v, i, :, lanes].astype(F32)[8:] * scaling
                for v in range(nv)
            ]
        for t in range(nt):
            layer = layer_ref[t, u, pair, lanes].astype(F32)[half]
            near = layer
            if first:
                near = near + edge(t, u, False)
            if last:
                high = edge(t, u, True)
                near = near + high
            acc[t][u] = acc[t][u] + damping * near
            for v in range(nv):
                if jac_i is not None:
                    acc[t][v] = acc[t][v] + jac_i[v] * layer
                if jac_j is not None:
                    acc[t][v] = acc[t][v] + jac_j[v] * high
    return [
        [part_ref[t, v, i, j : j + 8, lanes] + acc[t][v] for v in range(nv)]
        for t in range(nt)
    ]


def lanes_at(k):
    return pl.ds(pl.multiple_of(k * 128, 128), 128)


def local_kernel(*refs):
    ins, out_ref, slices = refs[:5], refs[5], refs[6:]
    nt, nv, ni, nj, nk = out_ref.shape
    if slices:
        jac_ref, (jac_i_ref, jac_j_ref) = ins[2], slices
        for u in range(nv):
            for v in range(nv):
                jac_i_ref[u, v] = jac_ref[0, u, v, ni - 1]
                for i in range(ni):
                    jac_j_ref[u, v, i] = jac_ref[1, u, v, i, nj - 16 :, :]

    def one(k, carry):
        lanes = lanes_at(k)
        for i in range(ni):
            for j in range(0, nj, 8):
                new = local_tile(ins, i, j, lanes)
                for t in range(nt):
                    for v in range(nv):
                        out_ref[t, v, i, j : j + 8, lanes] = new[t][v]
        return carry

    lax.fori_loop(0, nk // 128, one, 0)


def finish_all(ids_ref, ins, out_ref, layers):
    nt, nv, ni, nj, nk = out_ref.shape
    upper = ids_ref[1] == 1

    def one(k, carry):
        lanes = lanes_at(k)
        for i in range(ni):
            for j in range(0, nj, 8):
                new = finish_tile(upper, ins, layers[i], i, j, lanes)
                for t in range(nt):
                    for v in range(nv):
                        out_ref[t, v, i, j : j + 8, lanes] = new[t][v]
        return carry

    lax.fori_loop(0, nk // 128, one, 0)


def first_kernel(ids_ref, *refs):
    ins, ha_ref, hb_ref = refs[:7], refs[7], refs[8]
    out_ref, a_ref, b_ref = refs[9:]

    def run(layer_a, layer_b):
        finish_all(ids_ref, ins, out_ref, {layer_a: ha_ref, layer_b: hb_ref})
        pack_layers(out_ref, a_ref, b_ref, layer_a, layer_b)

    by_parity(ids_ref, run)


def surface_kernel(ids_ref, *refs):
    ins, ha_ref, hb_ref, w_ref, sens_ref = refs[:7], *refs[7:11]
    nt, nv, ni, nj, nk = ins[0].shape

    def row_of(side, layers):
        j = side * (nj - 8)
        mask = lax.broadcasted_iota(jnp.int32, (8, 128), 0) == side * 7
        values = []
        for i in range(ni):
            for k in range(0, nk, 128):
                new = finish_tile(side == 1, ins, layers[i], i, j, slice(k, k + 128))
                total = jnp.zeros((8, 128), F32)
                for t in range(nt):
                    for v in range(nv):
                        at = t * nv + v
                        weight = w_ref[at : at + 1, i * nk + k : i * nk + k + 128]
                        total = total + new[t][v] * weight
                values.append(
                    jnp.sum(jnp.where(mask, total, 0.0), axis=0, keepdims=True)
                )
        sens_ref[...] = jnp.concatenate(values, axis=0)

    def run(layer_a, layer_b):
        layers = {layer_a: ha_ref, layer_b: hb_ref}
        for side in range(2):
            pl.when(ids_ref[1] == side)(functools.partial(row_of, side, layers))

    by_parity(ids_ref, run)


def share_kernel(own_ref, other_ref, out_ref, done_ref):
    done_ref[...] = jnp.zeros(done_ref.shape, F32)
    value = own_ref[...] + other_ref[...]
    for member in range(out_ref.shape[0]):
        out_ref[member] = value


def second_kernel(ids_ref, *refs):
    ins, ha_ref, hb_ref, out_ref, done_ref = refs[:7], *refs[7:9], *refs[10:12]
    done_ref[...] = jnp.zeros(done_ref.shape, F32)

    def run(layer_a, layer_b):
        finish_all(ids_ref, ins, out_ref, {layer_a: ha_ref, layer_b: hb_ref})

    by_parity(ids_ref, run)


def split3(x):
    one = x.astype(BF16)
    rest = x - one.astype(F32)
    two = rest.astype(BF16)
    three = (rest - two.astype(F32)).astype(BF16)
    return one, two, three


def one_hot(cells_ref, first, rows):
    cells = cells_ref.shape[1]
    index = lax.broadcasted_iota(jnp.int32, (rows, cells), 0) + first
    return jnp.where(cells_ref[0:1, :] == index, 1.0, 0.0).astype(BF16)


def order_kernel(ids_ref, cells_ref, w_ref, out_ref):
    rows, half = out_ref.shape
    nv, nt, _ = w_ref.shape
    own = one_hot(cells_ref, ids_ref[1] * half, half)
    parts = [part for v in range(nv) for part in split3(w_ref[v])]
    found = lax.dot_general(
        jnp.concatenate(parts, axis=0),
        own,
        (((1,), (1,)), ((), ())),
        preferred_element_type=F32,
    )
    for t in range(nt):
        for v in range(nv):
            one, two, three = (found[(v * 3 + p) * nt + t][None] for p in range(3))
            out_ref[t * nv + v : t * nv + v + 1, :] = one + (two + three)


def mode_table(side, modes, senders):
    row = lax.broadcasted_iota(jnp.int32, (2 * modes, senders), 0)
    sender = lax.broadcasted_iota(jnp.int32, (2 * modes, senders), 1)
    turns = ((row % modes) * (sender // 2)) % PASSAGES
    angle = turns.astype(F32) * (2.0 * math.pi / PASSAGES)
    value = jnp.where(row < modes, jnp.cos(angle), -jnp.sin(angle)) / PASSAGES**0.5
    return jnp.where(sender % 2 == side, value, 0.0)


def tables_kernel(cells_ref, done_ref, chosen_ref, table_ref):
    chosen_ref[...] = one_hot(cells_ref, 0, chosen_ref.shape[0])
    rows, senders = table_ref.shape
    for side in range(2):
        here = slice(side * rows // 2, (side + 1) * rows // 2)
        table_ref[here, :] = mode_table(side, rows // 4, senders)


def modes_kernel(chosen_ref, table_ref, sens_ref, out_ref):
    senders, pieces = sens_ref.shape[:2]
    half = pieces * 128
    rows = out_ref.shape[0]
    seen = jnp.concatenate([sens_ref[:, c, :] for c in range(pieces)], axis=1)
    both = jnp.dot(
        table_ref[...],
        seen,
        precision=lax.Precision.HIGHEST,
        preferred_element_type=F32,
    )
    modes = jnp.concatenate([both[:rows], both[rows:]], axis=1)
    found = jnp.dot(
        jnp.concatenate(split3(modes), axis=0),
        chosen_ref[...],
        preferred_element_type=F32,
    )
    out_ref[...] = found[:rows] + (found[rows : 2 * rows] + found[2 * rows :])


def body(start, source, jac, sigma, damping, cells, weights):
    nt, nv, ni, nj, nk = start.shape
    ring = lax.axis_size("passage")
    n_cell = lax.axis_size("cell")
    ids = jnp.stack([lax.axis_index("cell") & 1, lax.axis_index("passage") & 1])
    even = [(c, c ^ 1) for c in range(n_cell)]
    odd = [(c, c + 1) for c in range(1, n_cell - 1, 2)]
    odd += [(b, a) for a, b in odd]
    within = [(d, d ^ 1) for d in range(ring)]
    across = [(d, (d + 1) % ring) for d in range(1, ring, 2)]
    across += [(b, a) for a, b in across]
    swap = [(0, 1), (1, 0)]

    field_like = jax.ShapeDtypeStruct(start.shape, F32)
    layer_like = jax.ShapeDtypeStruct((nt, nv, nj, nk), BF16)
    rows_like = jax.ShapeDtypeStruct((nt * nv * ni, nk), F32)

    sends = [layer_like, layer_like]

    def exchange(field, a, b):
        rows = [rows_like, rows_like]
        outer, inner = call(
            pack_rows, rows, (ids, field), [SMEM, VMEM], 4, 10**6, "rows"
        )
        with jax.named_scope("halos"):
            return (
                lax.ppermute(outer, "passage", across),
                lax.ppermute(inner, "passage", within),
                lax.ppermute(a, "cell", even),
                lax.ppermute(b, "cell", odd),
            )

    both_like = jax.ShapeDtypeStruct((2, *layer_like.shape), BF16)
    *packed, both = call(
        prepare_kernel, sends + [both_like], (ids, start), [SMEM, VMEM], 4, 10**6, "prepare"
    )
    with jax.named_scope("other_times"):
        far = lax.ppermute(both, "tm", swap)
    halos = exchange(start, *packed)
    rhs = call(
        rhs_kernel,
        [field_like],
        (ids, start, source, far),
        [SMEM] + [VMEM] * 3,
        4,
        10**7,
        "rhs",
    )[0]
    ordered = call(
        order_kernel,
        [jax.ShapeDtypeStruct((nt * nv, ni * nk), F32)],
        (ids, cells, weights.transpose(1, 0, 2)),
        [SMEM, VMEM, VMEM],
        8,
        10**6,
        "order",
    )[0]
    def local(field, outs, name):
        args = (field, rhs, jac, sigma, damping)
        return call(local_kernel, outs, args, [VMEM] * 5, 4, 2 * 10**7, name)

    slices = [
        jax.ShapeDtypeStruct((nv, nv, nj, nk), BF16),
        jax.ShapeDtypeStruct((nv, nv, ni, 16, nk), BF16),
    ]
    part, jac_i, jac_j = local(start, [field_like] + slices, "first_local")

    def finish(kernel, outs, part, halos, more, name):
        outer, inner, ha, hb = halos
        args = (ids, part, jac_i, jac_j, sigma, damping, outer, inner, ha, hb, *more)
        specs = [SMEM] + [VMEM] * (len(args) - 1)
        return call(kernel, outs, args, specs, 4, 10**7, name)

    field, *packed = finish(
        first_kernel,
        [field_like] + sends,
        part,
        halos,
        (),
        "first_finish",
    )
    halos = exchange(field, *packed)
    part = local(field, [field_like], "second_local")[0]
    token_like = jax.ShapeDtypeStruct((8, 128), F32)
    pieces = ni * nk // 128
    sens_like = jax.ShapeDtypeStruct((pieces, 128), F32)
    sens = finish(surface_kernel, [sens_like], part, halos, (ordered,), "surface")[0]
    with jax.named_scope("share_sensitivities"):
        other = lax.ppermute(sens, "tm", swap)
        sens, done = call(
            share_kernel,
            [jax.ShapeDtypeStruct((ring, pieces, 128), F32), token_like],
            (sens, other),
            [VMEM] * 2,
            4,
            10**4,
            "share",
        )
        gathered = lax.all_to_all(sens, "passage", 0, 0, tiled=True)
    field, done = finish(
        second_kernel, [field_like, token_like], part, halos, (done,), "second_finish"
    )
    chosen, table = call(
        tables_kernel,
        [
            jax.ShapeDtypeStruct((cells.shape[1], cells.shape[1]), BF16),
            jax.ShapeDtypeStruct((4 * PASSAGES, ring), F32),
        ],
        (cells, done),
        [VMEM] * 2,
        8,
        10**6,
        "tables",
    )
    modes = call(
        modes_kernel,
        [jax.ShapeDtypeStruct((2 * PASSAGES, cells.shape[1]), F32)],
        (chosen, table, gathered),
        [VMEM] * 3,
        8,
        10**7,
        "modes",
    )[0]
    return field, modes.reshape(2, PASSAGES, -1)


def solution(mesh):
    in_specs = (
        P("tm", None, "cell", "passage", None),
        P("tm", None, "cell", "passage", None),
        P(None, None, None, "cell", "passage", None),
        P("cell", "passage", None),
        P("cell", "passage", None),
        P("cell", None),
        P("tm", None, "cell"),
    )
    out_specs = (P("tm", None, "cell", "passage", None), P(None, None, "cell"))
    return jax.shard_map(
        body, mesh=mesh, in_specs=in_specs, out_specs=out_specs, check_vma=False
    )
```
